32 devices in a mesh: dp: 8 (over z, y), tensor: 4 (over x, core).
Axes of the slice: x: 2, y: 2, z: 4, core: 2. Of those that a mesh axis runs over, the one named last changes fastest.
Arguments:
- inputs: bfloat16 [32, 512, 512], P('dp', 'tensor'), may hold values from -6 to 6
- segment_ids: int32 [32, 512], P('dp'), may hold values from 0 to 22, as said below
- cotangent: bfloat16 [32, 512, 512], P('dp', 'tensor'), may hold values from -6 to 6
- attn_proj: float32 [3, 512, 512], P(None, 'dp', 'tensor'), may hold values from -0.25 to 0.25
- out_proj: float32 [512, 512], P(('tensor', 'dp')), may hold values from -2 to 2
- up_proj: float32 [512, 2048], P('dp', 'tensor'), may hold values from -0.25 to 0.25
- down_proj: float32 [2048, 512], P(('tensor', 'dp')), may hold values from -0.125 to 0.125
- pos_table: float32 [512, 512], P(('tensor', 'dp')), may hold values from -4 to 4
- norm_params: float32 [4, 512], P(None, 'dp'), may hold values from -1 to 1.6, as said below
- first_attn: float32 [3, 512, 512], P(None, 'dp', 'tensor'), may hold values from -32 to 32
- second_attn: float32 [3, 512, 512], P(None, 'dp', 'tensor'), may hold values from 137.6256 to 557.056
- first_out: float32 [512, 512], P(('tensor', 'dp')), may hold values from -5 to 5
- second_out: float32 [512, 512], P(('tensor', 'dp')), may hold values from 3.11296 to 12.45184
- first_up: float32 [512, 2048], P('dp', 'tensor'), may hold values from -16 to 16
- second_up: float32 [512, 2048], P('dp', 'tensor'), may hold values from 27.8528 to 111.4112
- first_down: float32 [2048, 512], P(('tensor', 'dp')), may hold values from -32 to 32
- second_down: float32 [2048, 512], P(('tensor', 'dp')), may hold values from 137.6256 to 557.056
- first_pos: float32 [512, 512], P(('tensor', 'dp')), may hold values from -4 to 4
- second_pos: float32 [512, 512], P(('tensor', 'dp')), may hold values from 1.696 to 6.72
- first_norm: float32 [4, 512], P(None, 'dp'), may hold values from -80 to 80
- second_norm: float32 [4, 512], P(None, 'dp'), may hold values from 868.352 to 3440.64
Outputs:
- outputs: bfloat16 [32, 512, 512], P('dp', 'tensor')
- grad_input: float32 [32, 512, 512], P('dp', 'tensor')
- new_attn_proj: float32 [3, 512, 512], P(None, 'dp', 'tensor')
- new_first_attn: float32 [3, 512, 512], P(None, 'dp', 'tensor')
- new_second_attn: float32 [3, 512, 512], P(None, 'dp', 'tensor')
- new_out_proj: float32 [512, 512], P(('tensor', 'dp'))
- new_first_out: float32 [512, 512], P(('tensor', 'dp'))
- new_second_out: float32 [512, 512], P(('tensor', 'dp'))
- new_up_proj: float32 [512, 2048], P('dp', 'tensor')
- new_first_up: float32 [512, 2048], P('dp', 'tensor')
- new_second_up: float32 [512, 2048], P('dp', 'tensor')
- new_down_proj: float32 [2048, 512], P(('tensor', 'dp'))
- new_first_down: float32 [2048, 512], P(('tensor', 'dp'))
- new_second_down: float32 [2048, 512], P(('tensor', 'dp'))
- new_pos_table: float32 [512, 512], P(('tensor', 'dp'))
- new_first_pos: float32 [512, 512], P(('tensor', 'dp'))
- new_second_pos: float32 [512, 512], P(('tensor', 'dp'))
- new_norm_params: float32 [4, 512], P(None, 'dp')
- new_first_norm: float32 [4, 512], P(None, 'dp')
- new_second_norm: float32 [4, 512], P(None, 'dp')
The draws below stay inside these ranges and needn't reach their ends.
Inputs may be any that keep to these rules, and one draw needn't show every extreme that they name: `segment_ids`: within each window ids start at 0 and never fall; characters with the same id in a window are one document; every window's last id is the largest allowed. `norm_params`: rows 0 and 2 are gains, rows 1 and 3 shifts.
All inputs are finite; a program needn't handle non-finite values.
Results may differ from the reference program's by a relative error of at most 0.018.
The reference program's roundings to bfloat16 on the way count: a program that leaves them out, or rounds other values in their place, can miss the bound.
Values may be sent and summed in bfloat16 or wider, within the bound.
No kernel may reach another device: no remote copies, remote signals or barrier semaphores. Data moves between devices by JAX's collectives and lax.ppermute only.
A program may use at most 64 MiB of HBM per device.

```python
import math
import jax
import jax.numpy as jnp
from jax import lax

D = 512
H = 8
HD = 64
FF = 2048
WIN = 512
SEQS = 4
STEP = 10
NWIN = 32
TOKENS = 16384
N_DP = 8
N_TENSOR = 4


def draw_segment_ids(key, part):
    key = jax.random.fold_in(key, 11)
    start_key, break_key = jax.random.split(key)
    long_span = WIN * 7 // 8
    free_count = WIN // 8 - 2
    chosen_count = free_count // 3
    starts = jax.random.randint(start_key, (NWIN, 1), 1, WIN - long_span)
    places = jnp.arange(WIN)[None, :]
    outside = (places > 0) & (places < starts) | (places > starts + long_span)
    ranks = jnp.cumsum(outside.astype(jnp.int32), axis=1) - 1
    break_keys = jax.random.split(break_key, NWIN)
    orders = jax.vmap(lambda row_key: jax.random.permutation(row_key, free_count))(break_keys)
    picked = jnp.take_along_axis(orders, jnp.clip(ranks, 0, free_count - 1), axis=1) < chosen_count
    bounds = (places == starts) | (places == starts + long_span) | picked & outside
    return jnp.cumsum(bounds.astype(jnp.int32), axis=1).astype(jnp.int32)


def draw_norm_params(key, part):
    key = jax.random.fold_in(key, 12)
    gain_key, shift_key = jax.random.split(key)
    gains = jax.random.uniform(gain_key, (2, D), minval=0.5, maxval=1.5)
    shifts = jnp.clip(jax.random.normal(shift_key, (2, D)) * 0.3, -1.0, 1.0)
    stacked = jnp.stack([gains[0], shifts[0], gains[1], shifts[1]])
    return stacked.astype(jnp.float32)


def block_scale(key, dims, cuts, smallest, top_value):
    loudness = 1.0
    for position, parts in cuts:
        steps = jax.random.uniform(jax.random.fold_in(jax.random.fold_in(key, 6), position), (parts,), jnp.float32, smallest / len(cuts), top_value / len(cuts))
        loudness = loudness * jnp.repeat(jnp.exp(steps), dims[position] // parts).reshape((-1,) + (1,) * (len(dims) - 1 - position))
    return loudness


def normal_values(key, shape, deviation, most, cuts=(), dtype=jnp.bfloat16):
    result = deviation * jax.random.normal(key, shape, jnp.float32)
    if cuts:
        result = result * block_scale(key, shape, cuts, -0.22, 0.18)
    return jnp.clip(result, -most, most).astype(dtype)


def setup_inputs(seed: int = 0) -> dict:
    key_of = jax.random.split(jax.random.key(seed), 22)
    inputs = normal_values(key_of[0], (NWIN, WIN, D), 1.0, 6.0, ((0, 8), (1, 4)))
    segment_ids = draw_segment_ids(jax.random.fold_in(key_of[21], 71), 0)
    cotangent = normal_values(key_of[2], (NWIN, WIN, D), 1.0, 6.0, ((0, 8), (1, 4)))
    attn_proj = normal_values(key_of[3], (3, D, D), D ** -0.5, 0.25, ((1, 8), (2, 4)), jnp.float32)
    out_proj = normal_values(key_of[4], (D, D), (D // 64) ** -0.5, 2.0, ((0, 32),), jnp.float32)
    up_proj = normal_values(key_of[5], (D, FF), D ** -0.5, 0.25, ((0, 8), (1, 4)), jnp.float32)
    down_proj = normal_values(key_of[6], (FF, D), FF ** -0.5, 0.125, ((0, 32),), jnp.float32)
    pos_table = normal_values(key_of[7], (WIN, D), 0.5, 4.0, ((0, 32),), jnp.float32)
    norm_params = draw_norm_params(jax.random.fold_in(key_of[21], 71), 0)
    first_attn = normal_values(key_of[9], (3, D, D), (0.044 * TOKENS ** 0.5), 32.0, ((1, 8), (2, 4)), jnp.float32)
    second_attn = jnp.clip(jnp.exp(math.log(557.056) - 1.3981289 * jax.random.uniform(key_of[10], (3, D, D), jnp.float32) ** block_scale(key_of[10], (3, D, D), ((1, 8), (2, 4)), -0.2, 0.2)), 137.6256, 557.056)
    first_out = normal_values(key_of[11], (D, D), (0.0067 * TOKENS ** 0.5), 5.0, ((0, 32),), jnp.float32)
    second_out = jnp.clip(jnp.exp(math.log(12.45184) - 1.3862944 * jax.random.uniform(key_of[12], (D, D), jnp.float32) ** block_scale(key_of[12], (D, D), ((0, 32),), -0.2, 0.2)), 3.11296, 12.45184)
    first_up = normal_values(key_of[13], (D, FF), (0.02 * TOKENS ** 0.5), 16.0, ((0, 8), (1, 4)), jnp.float32)
    second_up = jnp.clip(jnp.exp(math.log(111.4112) - 1.3862944 * jax.random.uniform(key_of[14], (D, FF), jnp.float32) ** block_scale(key_of[14], (D, FF), ((0, 8), (1, 4)), -0.2, 0.2)), 27.8528, 111.4112)
    first_down = normal_values(key_of[15], (FF, D), (0.044 * TOKENS ** 0.5), 32.0, ((0, 32),), jnp.float32)
    second_down = jnp.clip(jnp.exp(math.log(557.056) - 1.3981289 * jax.random.uniform(key_of[16], (FF, D), jnp.float32) ** block_scale(key_of[16], (FF, D), ((0, 32),), -0.2, 0.2)), 137.6256, 557.056)
    first_pos = normal_values(key_of[17], (WIN, D), (0.11 * NWIN ** 0.5), 4.0, ((0, 32),), jnp.float32)
    second_pos = jnp.clip(jnp.exp(math.log(6.72) - 1.3768156 * jax.random.uniform(key_of[18], (WIN, D), jnp.float32) ** block_scale(key_of[18], (WIN, D), ((0, 32),), -0.2, 0.2)), 1.696, 6.72)
    first_norm = normal_values(key_of[19], (4, D), (0.11 * TOKENS ** 0.5), 80.0, ((1, 8),), jnp.float32)
    second_norm = jnp.clip(jnp.exp(math.log(3440.64) - 1.3768156 * jax.random.uniform(key_of[20], (4, D), jnp.float32) ** block_scale(key_of[20], (4, D), ((1, 8),), -0.2, 0.2)), 868.352, 3440.64)
    return {"inputs": inputs, "segment_ids": segment_ids, "cotangent": cotangent, "attn_proj": attn_proj, "out_proj": out_proj, "up_proj": up_proj, "down_proj": down_proj, "pos_table": pos_table, "norm_params": norm_params, "first_attn": first_attn, "second_attn": second_attn, "first_out": first_out, "second_out": second_out, "first_up": first_up, "second_up": second_up, "first_down": first_down, "second_down": second_down, "first_pos": first_pos, "second_pos": second_pos, "first_norm": first_norm, "second_norm": second_norm}


@jax.custom_vjp
def low(v):
    return lax.optimization_barrier(v.astype(jnp.bfloat16)).astype(jnp.float32)

@jax.custom_vjp
def low_back(v):
    return v

def low_keep(v):
    return (low(v), None)

def low_pass(kept, grad):
    return (grad,)

def back_keep(v):
    return (v, None)

def back_low(kept, grad):
    return (low(grad),)
low.defvjp(low_keep, low_pass)
low_back.defvjp(back_keep, back_low)
PRECISE = lax.Precision.HIGHEST
NORM_EPS = 1e-05
NEG_FILL = -1e+30
BETA_ONE = 0.9
BETA_TWO = 0.95
ADAM_EPS = 1e-08
RATES = (0.03, 0.2, 0.03, 0.02, 0.3, 0.3)
DECAYS = (0.1, 0.1, 0.1, 0.1, 0.1, 0.0)

def normalize(values, norm_gain, norm_shift):
    center = values - lax.optimization_barrier(jnp.mean(values, axis=-1, keepdims=True))
    spread = lax.optimization_barrier(jnp.mean(center * center, axis=-1, keepdims=True))
    return center * lax.rsqrt(spread + NORM_EPS) * norm_gain + norm_shift

def attend(window_item):
    query_rows, key_rows, value_rows, segments = window_item
    scores = jnp.einsum('qhd,khd->hqk', query_rows, key_rows, precision=PRECISE) * query_rows.shape[-1] ** (-0.5)
    scores = low_back(scores)
    places = jnp.arange(segments.shape[0])
    allowed = (segments[:, None] == segments[None, :]) & (places[:, None] >= places[None, :])
    scores = jnp.where(allowed[None], scores, NEG_FILL)
    shifted = scores - lax.optimization_barrier(jnp.max(scores, axis=-1, keepdims=True))
    exponents = jnp.exp(shifted)
    weights = low(exponents / lax.optimization_barrier(jnp.sum(exponents, axis=-1, keepdims=True)))
    return jnp.einsum('hqk,khd->qhd', weights, value_rows, precision=PRECISE)

def block_layer(params, inputs, segments):
    attn_w, out_w, up_w, down_w, pos_w, norm_w = params
    attn_w = low(attn_w)
    out_w = low(out_w)
    up_w = low(up_w)
    down_w = low(down_w)
    block_count = inputs.shape[0]
    group_width = D // N_TENSOR
    group_inner = FF // N_TENSOR
    group_heads = H // N_TENSOR
    hidden = inputs + pos_w[None]
    sent_hidden = low(hidden)
    attn_total = jnp.zeros_like(hidden)
    for member in range(N_TENSOR):
        local_copy = low_back(sent_hidden)
        columns = slice(member * group_width, (member + 1) * group_width)
        projected = jnp.einsum('bld,tdc->tblc', local_copy, attn_w[:, :, columns], precision=PRECISE)
        projected = low_back(low(projected)).reshape(3, block_count, WIN, group_heads, HD)
        mixed_rows = lax.map(jax.checkpoint(attend), (projected[0], projected[1], projected[2], segments))
        mixed_rows = low_back(low(mixed_rows.reshape(block_count, WIN, group_width)))
        attn_total = attn_total + low(jnp.einsum('blc,cd->bld', mixed_rows, out_w[columns, :], precision=PRECISE))
    attn_total = low_back(attn_total)
    normed_one = normalize(hidden + attn_total, norm_w[0], norm_w[1])
    sent_normed = low(normed_one)
    ffn_total = jnp.zeros_like(hidden)
    for member in range(N_TENSOR):
        local_copy = low_back(sent_normed)
        columns = slice(member * group_inner, (member + 1) * group_inner)
        pre_active = low_back(jnp.einsum('bld,df->blf', local_copy, up_w[:, columns], precision=PRECISE))
        active = low(jax.nn.gelu(pre_active))
        ffn_total = ffn_total + low(jnp.einsum('blf,fd->bld', active, down_w[columns, :], precision=PRECISE))
    ffn_total = low_back(ffn_total)
    return normalize(normed_one + ffn_total, norm_w[2], norm_w[3])

def adam_step(weight, gradient, moment_one, second, step_rate, decay_rate):
    first_new = BETA_ONE * moment_one + (1.0 - BETA_ONE) * gradient
    second_new = BETA_TWO * second + (1.0 - BETA_TWO) * gradient * gradient
    fixed_first = first_new / (1.0 - BETA_ONE ** STEP)
    fixed_second = second_new / (1.0 - BETA_TWO ** STEP)
    weight_new = weight - step_rate * (fixed_first / (jnp.sqrt(fixed_second) + ADAM_EPS) + decay_rate * weight)
    return (weight_new, first_new, second_new)

def reference(inputs, segment_ids, cotangent, attn_proj, out_proj, up_proj, down_proj, pos_table, norm_params, first_attn, second_attn, first_out, second_out, first_up, second_up, first_down, second_down, first_pos, second_pos, first_norm, second_norm):
    masters = (attn_proj, out_proj, up_proj, down_proj, pos_table, norm_params)
    segment_blocks = segment_ids.reshape(N_DP, SEQS, WIN)

    def forward(params, flat_inputs):
        blocks = flat_inputs.reshape(N_DP, SEQS, WIN, D)
        runner = jax.checkpoint(lambda block_item: block_layer(params, block_item[0], block_item[1]))
        return lax.map(runner, (blocks, segment_blocks)).reshape(flat_inputs.shape)
    outputs, pullback = jax.vjp(forward, masters, inputs.astype(jnp.float32))
    gradients, input_grad = pullback(cotangent.astype(jnp.float32))
    firsts = (first_attn, first_out, first_up, first_down, first_pos, first_norm)
    seconds = (second_attn, second_out, second_up, second_down, second_pos, second_norm)
    updated = [adam_step(masters[index], gradients[index], firsts[index], seconds[index], RATES[index], DECAYS[index]) for index in range(6)]
    return (outputs.astype(jnp.bfloat16), input_grad, updated[0][0], updated[0][1], updated[0][2], updated[1][0], updated[1][1], updated[1][2], updated[2][0], updated[2][1], updated[2][2], updated[3][0], updated[3][1], updated[3][2], updated[4][0], updated[4][1], updated[4][2], updated[5][0], updated[5][1], updated[5][2])
```

```python
import functools

import jax
import jax.numpy as jnp
from jax import lax
from jax.experimental import pallas as pl
from jax.experimental.pallas import tpu as pltpu
from jax.sharding import PartitionSpec as P

HD = 64
STEP = 10
LANES = 128

NORM_EPS = 1e-05
NEG_FILL = -1e30
BETA_ONE = 0.9
BETA_TWO = 0.95
ADAM_EPS = 1e-08
RATES = (0.03, 0.2, 0.03, 0.02, 0.3, 0.3)
DECAYS = (0.1, 0.1, 0.1, 0.1, 0.1, 0.0)
GELU_A = 0.7978845608028654
GELU_B = 0.044715

F32 = jnp.float32
BF16 = jnp.bfloat16
AXES = ("dp", "tensor")

NN = (((1,), (0,)), ((), ()))
NT = (((1,), (1,)), ((), ()))


def mm(a, b, dims=NN):
    return lax.dot_general(a, b, dims, preferred_element_type=F32)


def swap(value, rd, rt):
    n_t = lax.axis_size("tensor")
    mask = rd * n_t + rt
    return lax.ppermute(value, AXES, [(i, i ^ mask) for i in range(lax.axis_size("dp") * n_t)])


def rows_at(start, size, step):
    return pl.ds(pl.multiple_of(start, step), size)


def fill_window(me_t, parts, out_ref):
    own, rx, c1, c3 = parts
    n = own.shape[1]
    out_ref[rows_at(me_t * n, n, n), :] = own[me_t]
    out_ref[rows_at((me_t ^ 1) * n, n, n), :] = c1[0]
    out_ref[rows_at((me_t ^ 2) * n, n, n), :] = rx[me_t & 1]
    out_ref[rows_at((me_t ^ 3) * n, n, n), :] = c3[0]


def attention_kernel(places, n_pieces, scal, *refs):
    own, rx, c1, c3, seg_row = refs[:5]
    pieces = refs[5 : 5 + n_pieces]
    hid_o, qkv_o, pt_o, mixt_o, w_o, nrm_o, x_s, pos_s, bias_s, nrm_s = refs[5 + n_pieces :]
    me_dp, me_t = scal[0], scal[1]
    win, width = x_s.shape
    groups = w_o.shape[0]
    fill_window(me_t, (own, rx, c1, c3), x_s)
    if places is None:
        w_o[...] = pieces[0][...]
        pos_s[...] = pieces[1][...]
        nrm_o[...] = pieces[2][...]
    else:
        n_dp = nrm_s.shape[0]
        per = width // n_dp
        pos_per = win // (n_dp * groups)
        for ref, (xr, yr, z0, c) in zip(pieces, places, strict=True):
            tr = xr * 2 + c
            for i in range(ref.shape[0]):
                src = me_dp ^ ((z0 + i) * 2 + yr)
                for t in range(3):
                    w_o[tr, rows_at(src * per, per, per), t * LANES : (t + 1) * LANES] = ref[i, t * per : (t + 1) * per]
                where = (me_t ^ tr) * (win // groups) + src * pos_per
                for k in range(width // LANES):
                    at = 3 * per + k * pos_per
                    pos_s[rows_at(where, pos_per, pos_per), k * LANES : (k + 1) * LANES] = ref[i, at : at + pos_per]
                if tr == 0:
                    at = 3 * per + width // LANES * pos_per
                    nrm_s[src] = ref[i, at : at + 16].astype(F32)
        low_lane = lax.broadcasted_iota(jnp.int32, (8, LANES), 1) < per
        for j in range(n_dp // 2):
            left = nrm_s[2 * j]
            right = nrm_s[2 * j + 1]
            both = jnp.where(low_lane, left[0:8] + left[8:16], right[0:8] + right[8:16])
            nrm_o[:, j * LANES : (j + 1) * LANES] = both

    seg = seg_row[...].astype(F32)
    seg_col = jnp.transpose(jnp.broadcast_to(seg, (LANES, win)))
    for i in range(win // LANES):
        key_seg = seg_col[i * LANES : (i + 1) * LANES, 0:1]
        key_at = lax.broadcasted_iota(jnp.int32, (LANES, win), 0) + i * LANES
        query_at = lax.broadcasted_iota(jnp.int32, (LANES, win), 1)
        counts = (key_seg == seg) & (query_at >= key_at)
        bias_s[i * LANES : (i + 1) * LANES, :] = jnp.where(counts, 0.0, NEG_FILL)

    hidden = x_s[...].astype(F32) + pos_s[...].astype(F32)
    hid_o[...] = hidden
    x_s[...] = hidden.astype(BF16)
    lane = lax.broadcasted_iota(jnp.int32, (win, LANES), 1)

    @pl.loop(0, groups)
    def _(g):
        qkv = mm(x_s[...], w_o[g]).astype(BF16)
        q = qkv[:, :LANES] * jnp.asarray(HD**-0.5, BF16)
        k = qkv[:, LANES : 2 * LANES]
        v = qkv[:, 2 * LANES :]
        qkv_o[g] = jnp.concatenate([q, k, v], axis=1)
        v_t = jnp.transpose(v)
        for h in range(LANES // HD):
            here = (lane >= h * HD) & (lane < (h + 1) * HD)
            k_h = jnp.where(here, k, jnp.zeros_like(k))
            for j in range(win // LANES):
                ext = (j + 1) * LANES
                cols = slice(j * LANES, ext)
                s = mm(k_h[:ext], q[cols], NT) + bias_s[:ext, cols]
                e = jnp.exp(s - jnp.max(s, axis=0, keepdims=True))
                p = (e * (1.0 / jnp.sum(e, axis=0, keepdims=True))).astype(BF16)
                pt_o[2 * g + h, :ext, cols] = p
                mixed = mm(v_t[h * HD : (h + 1) * HD, :ext], p)
                mixt_o[rows_at(g * LANES + h * HD, HD, HD), cols] = mixed.astype(BF16)


def norm_forward(v):
    center = v - jnp.mean(v, axis=-1, keepdims=True)
    rs = lax.rsqrt(jnp.mean(center * center, axis=-1, keepdims=True) + NORM_EPS)
    return center * rs, rs


def norm_backward(g, xhat, rs, gain):
    e = g * gain
    return rs * (e - jnp.mean(e, axis=-1, keepdims=True) - xhat * jnp.mean(e * xhat, axis=-1, keepdims=True))


def put_blocks(me_t, value, keep, s1, sx):
    n = keep.shape[0]
    for r, ref in ((0, keep), (1, s1.at[0]), (2, sx.at[0]), (3, sx.at[1])):
        ref[...] = value[rows_at((me_t ^ r) * n, n, n), :].astype(ref.dtype)


CHUNK = 64


def ffn_kernel(places, n_pieces, scal, *refs):
    own, rx, c1, c3, hid, mixt, nrm = refs[:7]
    pieces = refs[7 : 7 + n_pieces]
    rest = refs[7 + n_pieces :]
    res_k, res_1, res_x, gone_o, gm_o, gnorm_o = rest[:6]
    if places is None:
        gup_o, gdown_o, gout_o = rest[6:9]
        rest = rest[9:]
    else:
        keep_o, send_o = rest[6:8]
        rest = rest[8:]
    cot_s, out_s, up_s, down_s, a_s, b_s, xh1_s, r1_s, n1_s, sent_s, act_s, dg_s, low_s, xt_s = rest
    me_dp, me_t = scal[0], scal[1]
    win, width = hid.shape
    groups = up_s.shape[0]
    fill_window(me_t, (own, rx, c1, c3), cot_s)
    if places is None:
        up_s[...] = pieces[0][...]
        down_s[...] = pieces[1][...]
        out_s[...] = pieces[2][...]
        n_dp = 1
    else:
        n_dp = 2 * max(z0 + ref.shape[0] for ref, (_, _, z0, _) in zip(pieces, places, strict=True))
        per = width // n_dp
        out_per = LANES // n_dp
        for ref, (xr, yr, z0, c) in zip(pieces, places, strict=True):
            tr = xr * 2 + c
            for i in range(ref.shape[0]):
                src = me_dp ^ ((z0 + i) * 2 + yr)
                up_s[tr, rows_at(src * per, per, per), :] = ref[i, 0:per]
                down_s[tr, rows_at(src * per, per, per), :] = ref[i, per : 2 * per]
                out_s[rows_at(tr * LANES + src * out_per, out_per, out_per), :] = ref[i, 2 * per : 2 * per + out_per]

    def chunks(fn):
        @pl.loop(0, win // CHUNK)
        def _(i):
            fn(rows_at(i * CHUNK, CHUNK, CHUNK))

    a_s[...] = mm(jnp.transpose(mixt[...]), out_s[...])

    def norm_one(at):
        xhat, rs = norm_forward(hid[at, :] + a_s[at, :])
        xh1_s[at, :] = xhat
        r1_s[at, :] = jnp.broadcast_to(rs, (CHUNK, LANES))
        normed = xhat * nrm[0:1, :] + nrm[1:2, :]
        n1_s[at, :] = normed
        sent_s[at, :] = normed.astype(BF16)

    chunks(norm_one)

    @pl.loop(0, groups)
    def _(g):
        a_s[...] = mm(sent_s[...], up_s[g])

        def gelu(at):
            v = a_s[at, :]
            t = jnp.tanh(GELU_A * (v + GELU_B * v * v * v))
            act_s[g, at, :] = (0.5 * v * (1.0 + t)).astype(BF16)
            dg_s[g, at, :] = 0.5 * (1.0 + t) + 0.5 * v * (1.0 - t * t) * (GELU_A * (1.0 + 3.0 * GELU_B * v * v))

        chunks(gelu)
        n1_s[...] += mm(act_s[g], down_s[g])

    def norm_two(i, sums):
        at = rows_at(i * CHUNK, CHUNK, CHUNK)
        xhat, rs = norm_forward(n1_s[at, :])
        n1_s[at, :] = xhat * nrm[2:3, :] + nrm[3:4, :]
        g = cot_s[at, :].astype(F32)
        grad = norm_backward(g, xhat, rs, nrm[2:3, :])
        b_s[at, :] = grad
        low_s[at, :] = grad.astype(BF16)
        return (sums[0] + jnp.sum((g * xhat).reshape(-1, 8, width), axis=0), sums[1] + jnp.sum(g.reshape(-1, 8, width), axis=0))

    zero = jnp.zeros((8, width), F32)
    gain_two, shift_two = lax.fori_loop(0, win // CHUNK, norm_two, (zero, zero))
    put_blocks(me_t, n1_s, res_k, res_1, res_x)

    def put(c, xr, first, height, value):
        ref = keep_o if c == 0 else send_o
        each = value.shape[0] // n_dp
        for d in range(n_dp):
            rel = d ^ me_dp
            ref[xr * 2 + (rel & 1), rel >> 1, first : first + height, :] = value[d * each : (d + 1) * each].astype(BF16)

    xt_s[...] = jnp.transpose(sent_s[...])
    for xr in range(groups // 2):
        for c in range(2):
            g = xr * 2 + c
            gdown = mm(jnp.transpose(act_s[g]), low_s[...])
            a_s[...] = mm(low_s[...], down_s[g], NT)
            act_s[g] = (a_s[...] * dg_s[g]).astype(BF16)
            gup = mm(xt_s[...], act_s[g])
            if places is None:
                gdown_o[g] = gdown.astype(BF16)
                gup_o[g] = gup.astype(BF16)
            else:
                put(c, xr, 0, per, gup)
                put(c, xr, per, per, gdown)
            b_s[...] += mm(act_s[g], up_s[g], NT)

    def norm_one_back(i, sums):
        at = rows_at(i * CHUNK, CHUNK, CHUNK)
        g = b_s[at, :]
        xhat = xh1_s[at, :]
        grad = norm_backward(g, xhat, r1_s[at, 0:1], nrm[0:1, :])
        gone_o[at, :] = grad
        low_s[at, :] = grad.astype(BF16)
        return (sums[0] + jnp.sum((g * xhat).reshape(-1, 8, width), axis=0), sums[1] + jnp.sum(g.reshape(-1, 8, width), axis=0))

    gain_one, shift_one = lax.fori_loop(0, win // CHUNK, norm_one_back, (zero, zero))
    for k, total in enumerate((gain_one, shift_one, gain_two, shift_two)):
        gnorm_o[k : k + 1, :] = jnp.sum(total, axis=0, keepdims=True)
    gnorm_o[4:8, :] = jnp.zeros((4, width), F32)

    gout = mm(mixt[...], low_s[...])
    if places is None:
        gout_o[...] = gout.astype(BF16)
    else:
        for xr in range(groups // 2):
            for c in range(2):
                g = xr * 2 + c
                put(c, xr, 2 * per, out_per, gout[g * LANES : (g + 1) * LANES])
    gm = mm(low_s[...], out_s[...], NT).astype(BF16)
    for g in range(groups):
        gm_o[g] = gm[:, g * LANES : (g + 1) * LANES]


def attention_back_kernel(fast, scal, hid, qkv, pt, gm, w, gone, gnorm, *rest):
    gi_k, gi_1, gi_x = rest[:3]
    if fast:
        keep_o, send_o = rest[3:5]
    else:
        gattn_o, gpos_o = rest[3:5]
    ht_s, ds_s, dqkv_s, acc_s, dqt_s = rest[5:]
    me_dp, me_t = scal[0], scal[1]
    win, width = hid.shape
    groups = w.shape[0]
    blocks = win // LANES
    heads = LANES // HD
    ht_s[...] = jnp.transpose(hid[...].astype(BF16))
    acc_s[...] = gone[...]
    lane = lax.broadcasted_iota(jnp.int32, (win, LANES), 1)

    @pl.loop(0, groups)
    def _(g):
        q = qkv[g, :, :LANES]
        k = qkv[g, :, LANES : 2 * LANES]
        v = qkv[g, :, 2 * LANES :]
        d_mixed = gm[g]
        k_t = jnp.transpose(k)
        d_m_h = []
        q_h = []
        for h in range(heads):
            here = (lane >= h * HD) & (lane < (h + 1) * HD)
            q_h.append(jnp.where(here, q, jnp.zeros_like(q)))
            d_m_h.append(jnp.where(here, d_mixed, jnp.zeros_like(q)))
            for j in range(blocks):
                ext = (j + 1) * LANES
                cols = slice(j * LANES, ext)
                p = pt[2 * g + h, :ext, cols].astype(F32)
                dp = mm(v[:ext], d_m_h[h][cols], NT)
                ds = (p * (dp - jnp.sum(p * dp, axis=0, keepdims=True))).astype(BF16)
                ds_s[h, :ext, cols] = ds
                dqt_s[h * HD : (h + 1) * HD, cols] = mm(k_t[h * HD : (h + 1) * HD, :ext], ds) * (HD**-0.5)
        dqkv_s[g, :, :LANES] = jnp.transpose(dqt_s[...]).astype(BF16)
        for i in range(blocks):
            at = slice(i * LANES, (i + 1) * LANES)
            dk = jnp.zeros((LANES, LANES), F32)
            dv = jnp.zeros((LANES, LANES), F32)
            for h in range(heads):
                dk += mm(ds_s[h, at, i * LANES :], q_h[h][i * LANES :])
                dv += mm(pt[2 * g + h, at, i * LANES :], d_m_h[h][i * LANES :])
            dqkv_s[g, at, LANES : 2 * LANES] = dk.astype(BF16)
            dqkv_s[g, at, 2 * LANES :] = dv.astype(BF16)
        acc_s[...] += mm(dqkv_s[g], w[g], NT)

    put_blocks(me_t, acc_s, gi_k, gi_1, gi_x)
    if not fast:
        for g in range(groups):
            gattn_o[g] = mm(ht_s[...], dqkv_s[g]).astype(BF16)
        gpos_o[...] = acc_s[...].astype(BF16)
        return
    n_dp = 2 * keep_o.shape[1]
    per = width // n_dp
    pos_per = win // (n_dp * groups)
    for xr in range(groups // 2):
        for c in range(2):
            g = xr * 2 + c
            ref = keep_o if c == 0 else send_o
            grad = mm(ht_s[...], dqkv_s[g])
            for d in range(n_dp):
                rel = d ^ me_dp
                a, b = xr * 2 + (rel & 1), rel >> 1
                for t in range(3):
                    ref[a, b, t * per : (t + 1) * per, :] = grad[d * per : (d + 1) * per, t * LANES : (t + 1) * LANES].astype(BF16)
                where = (me_t ^ g) * (win // groups) + d * pos_per
                for k in range(width // LANES):
                    at = 3 * per + k * pos_per
                    ref[a, b, at : at + pos_per, :] = acc_s[rows_at(where, pos_per, pos_per), k * LANES : (k + 1) * LANES].astype(BF16)
                at = 3 * per + width // LANES * pos_per
                pair = d // 2 * LANES
                tile = gnorm[0:8, pair : pair + LANES]
                ref[a, b, at : at + 16, :] = jnp.concatenate([tile, tile], axis=0).astype(BF16)


def to_windows(value, me_t):
    x, c = me_t >> 1, me_t & 1
    rx = swap(lax.dynamic_slice_in_dim(value, 2 * (1 - x), 2, 0), 0, 2)
    c1 = swap(lax.dynamic_slice_in_dim(value, me_t ^ 1, 1, 0), 0, 1)
    c3 = swap(lax.dynamic_slice_in_dim(rx, 1 - c, 1, 0), 0, 1)
    return value, rx, c1, c3


def from_windows(keep, s1, sx, me_t):
    rx = swap(sx, 0, 2)
    r1 = swap(s1, 0, 1)[0]
    r3 = swap(rx[1:2], 0, 1)[0]
    flip = (me_t & 1) == 1
    low = [jnp.where(flip, r1, keep), jnp.where(flip, keep, r1)]
    high = [jnp.where(flip, r3, rx[0]), jnp.where(flip, rx[0], r3)]
    cross = (me_t >> 1) == 1
    return jnp.stack([jnp.where(cross, high[0], low[0]), jnp.where(cross, high[1], low[1]), jnp.where(cross, low[0], high[0]), jnp.where(cross, low[1], high[1])])


def gather(value, direct):
    nz = lax.axis_size("dp") // 2
    q = jnp.stack([value] + [swap(value, 2 * k, 0) for k in range(1, nz)])
    qx, qy = swap(q, 0, 2), swap(q, 1, 0)
    found = [(q, (0, 0, 0)), (qx, (1, 0, 0)), (qy, (0, 1, 0))]
    if direct:
        found.append((swap(q, 1, 2), (1, 1, 0)))
    else:
        half = nz // 2
        found.append((swap(qx[:half], 1, 0), (1, 1, 0)))
        found.append((swap(qy[half:], 0, 2), (1, 1, half)))
    out = []
    for array, place in found:
        out.append((array, (*place, 0)))
        out.append((swap(array, 0, 1), (*place, 1)))
    return out


def add(a, b):
    return (a.astype(F32) + b.astype(F32)).astype(BF16)


def scatter_sum(keep, send, direct):
    total = add(keep, swap(send, 0, 1))
    nz = total.shape[1]
    if direct:
        parts = [total[0], swap(total[2], 0, 2), swap(total[1], 1, 0), swap(total[3], 1, 2)]
        total = sum(p.astype(F32) for p in parts).astype(BF16)
    else:
        half = nz // 2
        a, b = total[:, :half], total[:, half:]
        a = add(a[:2], swap(a[2:], 0, 2))
        b = add(b[0::2], swap(b[1::2], 1, 0))
        a = add(a[0], swap(a[1], 1, 0))
        b = add(b[0], swap(b[1], 0, 2))
        total = jnp.concatenate([a, b])
    arrived = [total[0]] + [swap(total[k], 2 * k, 0) for k in range(1, nz)]
    return sum(p.astype(F32) for p in arrived)


def adam_step(weight, gradient, moment_one, second, step_rate, decay_rate):
    first_new = BETA_ONE * moment_one + (1.0 - BETA_ONE) * gradient
    second_new = BETA_TWO * second + (1.0 - BETA_TWO) * gradient * gradient
    fixed_first = first_new / (1.0 - BETA_ONE**STEP)
    fixed_second = second_new / (1.0 - BETA_TWO**STEP)
    weight_new = weight - step_rate * (fixed_first / (jnp.sqrt(fixed_second) + ADAM_EPS) + decay_rate * weight)
    return (weight_new, first_new, second_new)


def call(kernel, outs, scratch, args, mib, flops):
    vmem = pl.BlockSpec(memory_space=pltpu.VMEM)
    return pl.pallas_call(
        kernel,
        out_shape=outs,
        in_specs=[pl.BlockSpec(memory_space=pltpu.SMEM)] + [vmem] * (len(args) - 1),
        out_specs=[vmem] * len(outs),
        scratch_shapes=[pltpu.VMEM(s, t) for s, t in scratch],
        compiler_params=pltpu.CompilerParams(vmem_limit_bytes=mib * 1024 * 1024),
        cost_estimate=pl.CostEstimate(flops=flops, bytes_accessed=0, transcendentals=0),
    )(*args)


def body(
    inputs,
    segment_ids,
    cotangent,
    attn_proj,
    out_proj,
    up_proj,
    down_proj,
    pos_table,
    norm_params,
    first_attn,
    second_attn,
    first_out,
    second_out,
    first_up,
    second_up,
    first_down,
    second_down,
    first_pos,
    second_pos,
    first_norm,
    second_norm,
):
    n_dp, n_t = lax.axis_size("dp"), lax.axis_size("tensor")
    me_dp, me_t = lax.axis_index("dp"), lax.axis_index("tensor")
    scal = jnp.stack([me_dp, me_t]).astype(jnp.int32)
    windows, block, width = inputs.shape
    win = block * n_t
    inner = up_proj.shape[1]
    group = attn_proj.shape[2]
    per, out_per, pos_per = attn_proj.shape[1], out_proj.shape[0], pos_table.shape[0]
    fast = out_per % 16 == 0 and pos_per % 16 == 0 and 2 * per == LANES
    sds = jax.ShapeDtypeStruct

    seg_row = lax.dynamic_slice_in_dim(segment_ids, me_t, 1, 0)
    if fast:
        norm_tile = jnp.concatenate([norm_params, norm_params], axis=1)
        norm_high = norm_tile.astype(BF16)
        norm_low = (norm_tile - norm_high.astype(F32)).astype(BF16)
        none = jnp.zeros_like(norm_high)
        ga = jnp.concatenate(
            [
                attn_proj.astype(BF16).reshape(3 * per, group),
                pos_table.astype(BF16).reshape(pos_per, width // LANES, LANES).transpose(1, 0, 2).reshape(-1, LANES),
                jnp.concatenate([norm_high, none, norm_low, none]),
            ]
        )
        gb = jnp.concatenate([up_proj.astype(BF16), down_proj.astype(BF16), out_proj.astype(BF16)])
        found_a = gather(ga, True)
        x_parts = to_windows(inputs, me_t)
        found_b = gather(gb, False)
        a_args, a_places = [f[0] for f in found_a], tuple(f[1] for f in found_a)
        b_args, b_places = [f[0] for f in found_b], tuple(f[1] for f in found_b)
    else:
        x_parts = to_windows(inputs, me_t)
        relative = me_t ^ jnp.arange(n_t)
        whole = [lax.all_gather(lax.all_gather(v.astype(BF16), "dp"), "tensor") for v in (attn_proj, out_proj, up_proj, down_proj)]
        attn_w, out_w, up_w, down_w = [jnp.take(v, relative, axis=0) for v in whole]
        attn_w = attn_w.transpose(0, 1, 3, 2, 4).reshape(n_t, width, 3 * group)
        pos_w = lax.all_gather(lax.all_gather(pos_table.astype(BF16), "dp", axis=0, tiled=True), "tensor", axis=0, tiled=True)
        norm_w = lax.all_gather(norm_params, "dp", axis=1, tiled=True)
        norm_w = jnp.concatenate([norm_w, jnp.zeros_like(norm_w)])
        a_args, a_places = [attn_w, pos_w, norm_w], None
        b_args, b_places = [up_w.reshape(n_t, width, inner), down_w.reshape(n_t, inner, width), out_w.reshape(n_t * group, width)], None

    hid, qkv, pt, mixt, attn_all, norm_all = call(
        functools.partial(attention_kernel, a_places, len(a_args)),
        [
            sds((win, width), F32),
            sds((n_t, win, 3 * group), BF16),
            sds((n_t * group // HD, win, win), BF16),
            sds((n_t * group, win), BF16),
            sds((n_t, width, 3 * group), BF16),
            sds((8, width), F32),
        ],
        [((win, width), BF16), ((win, width), BF16), ((win, win), F32), ((n_dp, 16, LANES), F32)],
        [scal, *x_parts, seg_row, *a_args],
        32,
        2 * win * width * 3 * width,
    )
    cot_parts = to_windows(cotangent, me_t)

    blocks = [sds((block, width), BF16), sds((1, block, width), BF16), sds((2, block, width), BF16)]
    if fast:
        rows_b = 2 * per + out_per
        grads_b = [sds((4, n_dp // 2, rows_b, width), BF16)] * 2
    else:
        grads_b = [sds((n_t, width, inner), BF16), sds((n_t, inner, width), BF16), sds((n_t * group, width), BF16)]
    res_k, res_1, res_x, gone, gm, gnorm, *got_b = call(
        functools.partial(ffn_kernel, b_places, len(b_args)),
        [*blocks, sds((win, width), F32), sds((n_t, win, group), BF16), sds((8, width), F32), *grads_b],
        [
            ((win, width), BF16),
            ((n_t * group, width), BF16),
            ((n_t, width, inner), BF16),
            ((n_t, inner, width), BF16),
            ((win, width), F32),
            ((win, width), F32),
            ((win, width), F32),
            ((win, LANES), F32),
            ((win, width), F32),
            ((win, width), BF16),
            ((n_t, win, inner), BF16),
            ((n_t, win, inner), F32),
            ((win, width), BF16),
            ((width, win), BF16),
        ],
        [scal, *cot_parts, hid, mixt, norm_all, *b_args],
        50,
        12 * win * width * n_t * inner,
    )
    if fast:
        sum_b = scatter_sum(*got_b, False)
    outputs = from_windows(res_k, res_1, res_x, me_t)

    blocks = [sds((block, width), F32), *blocks[1:]]
    if fast:
        rows_a = 3 * per + width // LANES * pos_per + 16
        grads_a = [sds((4, n_dp // 2, rows_a, LANES), BF16)] * 2
    else:
        grads_a = [sds((n_t, width, 3 * group), BF16), sds((win, width), BF16)]
    gi_k, gi_1, gi_x, *got_a = call(
        functools.partial(attention_back_kernel, fast),
        [*blocks, *grads_a],
        [
            ((width, win), BF16),
            ((LANES // HD, win, win), BF16),
            ((n_t, win, 3 * group), BF16),
            ((win, width), F32),
            ((LANES, win), F32),
        ],
        [scal, hid, qkv, pt, gm, attn_all, gone, gnorm],
        40,
        4 * win * width * 3 * width,
    )
    gi_1, gi_x = gi_1.astype(F32), gi_x
    grad_input = from_windows(gi_k.astype(F32), gi_1.astype(BF16), gi_x, me_t)

    if fast:
        sum_a = scatter_sum(*got_a, True)
        g_attn = sum_a[: 3 * per].reshape(3, per, group)
        at = 3 * per
        n_pos = width // LANES * pos_per
        g_pos = sum_a[at : at + n_pos].reshape(width // LANES, pos_per, LANES).transpose(1, 0, 2).reshape(pos_per, width)
        tile = sum_a[at + n_pos : at + n_pos + 4]
        g_norm = jnp.where((me_dp & 1) == 1, tile[:, LANES // 2 :], tile[:, : LANES // 2])
        g_up, g_down, g_out = sum_b[:per], sum_b[per : 2 * per], sum_b[2 * per :]
    else:

        def reduced(value, own_axis):
            arrived = lax.all_to_all(value, "dp", split_axis=0, concat_axis=0, tiled=True)
            part = arrived.astype(F32).sum(axis=0).astype(BF16)
            arrived = lax.all_to_all(part, "tensor", split_axis=0, concat_axis=0, tiled=True)
            return arrived.astype(F32).sum(axis=0)

        gup, gdown, gout = got_b
        gattn, gpos = got_a
        gup, gdown, gout, gattn = [jnp.take(v, relative, axis=0) for v in (gup, gdown, gout.reshape(n_t, group, width), gattn)]
        g_up = reduced(gup.reshape(n_t, n_dp, per, inner).swapaxes(0, 1), 0)
        g_down = reduced(gdown.reshape(n_t, n_dp, inner // n_dp, width).swapaxes(0, 1), 0)
        g_out = reduced(gout.reshape(n_t, n_dp, out_per, width).swapaxes(0, 1), 0)
        g_pos = reduced(gpos.reshape(n_t, n_dp, pos_per, width).swapaxes(0, 1), 0)
        g_attn = reduced(gattn.reshape(n_t, n_dp, per, 3, group).swapaxes(0, 1), 0).swapaxes(0, 1)
        cut = gnorm[:4].reshape(4, n_dp, width // n_dp).swapaxes(0, 1).astype(BF16)
        g_norm = reduced(jnp.broadcast_to(cut[:, None], (n_dp, n_t, *cut.shape[1:])), 0)

    masters = (attn_proj, out_proj, up_proj, down_proj, pos_table, norm_params)
    gradients = (g_attn, g_out, g_up, g_down, g_pos, g_norm)
    firsts = (first_attn, first_out, first_up, first_down, first_pos, first_norm)
    seconds = (second_attn, second_out, second_up, second_down, second_pos, second_norm)
    updated = []
    for index in range(6):
        updated += adam_step(masters[index], gradients[index], firsts[index], seconds[index], RATES[index], DECAYS[index])
    return (outputs, grad_input, *updated)


def solution(mesh):
    acts = P("dp", "tensor", None)
    attn = P(None, "dp", "tensor")
    both = P(("tensor", "dp"), None)
    up = P("dp", "tensor")
    norm = P(None, "dp")
    return jax.shard_map(
        body,
        mesh=mesh,
        in_specs=(acts, P("dp", None), acts, attn, both, up, both, both, norm, *(attn,) * 2, *(both,) * 2, *(up,) * 2, *(both,) * 4, *(norm,) * 2),
        out_specs=(acts, acts, *(attn,) * 3, *(both,) * 3, *(up,) * 3, *(both,) * 6, *(norm,) * 3),
        check_vma=False,
    )
```

```python
import functools

import jax
import jax.numpy as jnp
from jax import lax
from jax.experimental import pallas as pl
from jax.experimental.pallas import tpu as pltpu
from jax.sharding import PartitionSpec as P

HD = 64
STEP = 10
LANES = 128

NORM_EPS = 1e-05
NEG_FILL = -1e30
BETA_ONE = 0.9
BETA_TWO = 0.95
ADAM_EPS = 1e-08
RATES = (0.03, 0.2, 0.03, 0.02, 0.3, 0.3)
DECAYS = (0.1, 0.1, 0.1, 0.1, 0.1, 0.0)
GELU_A = 0.7978845608028654
GELU_B = 0.044715

F32 = jnp.float32
BF16 = jnp.bfloat16
AXES = ("dp", "tensor")

NN = (((1,), (0,)), ((), ()))
NT = (((1,), (1,)), ((), ()))


def mm(a, b, dims=NN):
    return lax.dot_general(a, b, dims, preferred_element_type=F32)


def swap(value, rd, rt):
    n_t = lax.axis_size("tensor")
    mask = rd * n_t + rt
    return lax.ppermute(value, AXES, [(i, i ^ mask) for i in range(lax.axis_size("dp") * n_t)])


def rows_at(start, size, step):
    return pl.ds(pl.multiple_of(start, step), size)


def fill_window(me_t, which, parts, out_ref, sems):
    own, rx, c1, c3 = parts
    n = own.shape[1]
    sources = (own.at[me_t], c1.at[which], rx.at[which], c3.at[which])
    copies = [pltpu.make_async_copy(src, out_ref.at[rows_at((me_t ^ r) * n, n, n), :], sems.at[r]) for r, src in enumerate(sources)]
    for copy in copies:
        copy.start()
    return copies


def prepare_kernel(scal, inputs, cot, attn, out, up, down, pos, norm, ga, gb, xs, c1, attn_s, out_s, up_s, down_s, pos_s, norm_s, sems):
    me_t = scal[1]
    moves = [(attn, attn_s), (pos, pos_s), (norm, norm_s), (up, up_s), (down, down_s), (out, out_s)]
    for r, (rel, ref, at) in enumerate(((2, xs, 0), (3, xs, 2), (1, c1, 0))):
        moves += [(inputs.at[me_t ^ rel], ref.at[at]), (cot.at[me_t ^ rel], ref.at[at + 1])]
    copies = [pltpu.make_async_copy(src, dst, sems.at[i]) for i, (src, dst) in enumerate(moves)]
    for copy in copies:
        copy.start()
    for copy in copies[:3]:
        copy.wait()
    per = attn.shape[1]
    pos_per = pos.shape[0]
    tiles = pos.shape[1] // LANES
    for t in range(3):
        ga[t * per : (t + 1) * per, :] = attn_s[t].astype(BF16)
    for k in range(tiles):
        at = 3 * per + k * pos_per
        ga[at : at + pos_per, :] = pos_s[:, k * LANES : (k + 1) * LANES].astype(BF16)
    at = 3 * per + tiles * pos_per
    both = norm_s[...]
    both = jnp.concatenate([both, both], axis=1)
    both = jnp.concatenate([both, jnp.zeros_like(both)], axis=0)
    high = both.astype(BF16)
    low = (both - high.astype(F32)).astype(BF16)
    ga[at : at + 16, :] = jnp.concatenate([high, low], axis=0)
    for copy in copies[3:6]:
        copy.wait()
    gb[0:per, :] = up_s[...].astype(BF16)
    gb[per : 2 * per, :] = down_s[...].astype(BF16)
    gb[2 * per :, :] = out_s[...].astype(BF16)
    for copy in copies[6:]:
        copy.wait()


def attention_kernel(places, n_pieces, scal, *refs):
    own, rx, c1, c3, segs = refs[:5]
    pieces = refs[5 : 5 + n_pieces]
    hid_o, qkv_o, pt_o, mixt_o, w_o, nrm_o, x_s, pos_s, bias_s, nrm_s, sems = refs[5 + n_pieces :]
    me_dp, me_t = scal[0], scal[1]
    win, width = x_s.shape
    groups = w_o.shape[0]
    filling = fill_window(me_t, 0, (own, rx, c1, c3), x_s, sems)
    if places is None:
        w_o[...] = pieces[0][...]
        pos_s[...] = pieces[1][...]
        nrm_o[...] = pieces[2][...]
    else:
        n_dp = nrm_s.shape[0]
        per = width // n_dp
        pos_per = win // (n_dp * groups)
        for ref, (xr, yr, zs, c) in zip(pieces, places, strict=True):
            tr = xr * 2 + c
            for i, zr in enumerate(zs):
                src = me_dp ^ (zr * 2 + yr)
                for t in range(3):
                    w_o[tr, rows_at(src * per, per, per), t * LANES : (t + 1) * LANES] = ref[i, t * per : (t + 1) * per]
                where = (me_t ^ tr) * (win // groups) + src * pos_per
                for k in range(width // LANES):
                    at = 3 * per + k * pos_per
                    pos_s[rows_at(where, pos_per, pos_per), k * LANES : (k + 1) * LANES] = ref[i, at : at + pos_per]
                if tr == 0:
                    at = 3 * per + width // LANES * pos_per
                    nrm_s[src] = ref[i, at : at + 16].astype(F32)
        low_lane = lax.broadcasted_iota(jnp.int32, (8, LANES), 1) < per
        for j in range(n_dp // 2):
            left = nrm_s[2 * j]
            right = nrm_s[2 * j + 1]
            both = jnp.where(low_lane, left[0:8] + left[8:16], right[0:8] + right[8:16])
            nrm_o[:, j * LANES : (j + 1) * LANES] = both

    seg = segs[pl.ds(me_t, 1), :].astype(F32)
    seg_col = jnp.transpose(jnp.broadcast_to(seg, (LANES, win)))
    for i in range(win // LANES):
        key_seg = seg_col[i * LANES : (i + 1) * LANES, 0:1]
        key_at = lax.broadcasted_iota(jnp.int32, (LANES, win), 0) + i * LANES
        query_at = lax.broadcasted_iota(jnp.int32, (LANES, win), 1)
        counts = (key_seg == seg) & (query_at >= key_at)
        bias_s[i * LANES : (i + 1) * LANES, :] = jnp.where(counts, 0.0, NEG_FILL)

    for copy in filling:
        copy.wait()
    hidden = x_s[...].astype(F32) + pos_s[...].astype(F32)
    hid_o[...] = hidden
    x_s[...] = hidden.astype(BF16)
    lane = lax.broadcasted_iota(jnp.int32, (win, LANES), 1)

    @pl.loop(0, groups)
    def _(g):
        qkv = mm(x_s[...], w_o[g]).astype(BF16)
        q = qkv[:, :LANES] * jnp.asarray(HD**-0.5, BF16)
        k = qkv[:, LANES : 2 * LANES]
        v = qkv[:, 2 * LANES :]
        qkv_o[g] = jnp.concatenate([q, k, v], axis=1)
        v_t = jnp.transpose(v)
        for h in range(LANES // HD):
            here = (lane >= h * HD) & (lane < (h + 1) * HD)
            k_h = jnp.where(here, k, jnp.zeros_like(k))
            for j in range(win // LANES):
                ext = (j + 1) * LANES
                cols = slice(j * LANES, ext)
                s = mm(k_h[:ext], q[cols], NT) + bias_s[:ext, cols]
                e = jnp.exp(s - jnp.max(s, axis=0, keepdims=True))
                p = (e * (1.0 / jnp.sum(e, axis=0, keepdims=True))).astype(BF16)
                pt_o[2 * g + h, :ext, cols] = p
                mixed = mm(v_t[h * HD : (h + 1) * HD, :ext], p)
                mixt_o[rows_at(g * LANES + h * HD, HD, HD), cols] = mixed.astype(BF16)


def norm_forward(v):
    center = v - jnp.mean(v, axis=-1, keepdims=True)
    rs = lax.rsqrt(jnp.mean(center * center, axis=-1, keepdims=True) + NORM_EPS)
    return center * rs, rs


def norm_backward(g, xhat, rs, gain):
    e = g * gain
    return rs * (e - jnp.mean(e, axis=-1, keepdims=True) - xhat * jnp.mean(e * xhat, axis=-1, keepdims=True))


def put_blocks(me_t, value, keep, s1, sx):
    n = keep.shape[0]
    for r, ref in ((0, keep), (1, s1.at[0]), (2, sx.at[0]), (3, sx.at[1])):
        ref[...] = value[rows_at((me_t ^ r) * n, n, n), :].astype(ref.dtype)


CHUNK = 64


def chunk_of(refs, tr, r):
    c, xr, yr, zr = tr & 1, tr >> 1, r & 1, r >> 1
    half = refs[0].shape[0] // 4
    if zr < half:
        first, slot = xr == 1, yr * half + zr
    else:
        first, slot = yr == 1, 2 * half + xr * half + zr - half
    return refs[2 * c + (0 if first else 1)], slot


def ffn_kernel(places, n_pieces, scal, *refs):
    own, rx, c1, c3, hid, mixt, nrm = refs[:7]
    pieces = refs[7 : 7 + n_pieces]
    rest = refs[7 + n_pieces :]
    res_k, res_1, res_x, gone_o, gm_o, gnorm_o = rest[:6]
    if places is None:
        gup_o, gdown_o, gout_o = rest[6:9]
        rest = rest[9:]
    else:
        chunks_o = rest[6:10]
        rest = rest[10:]
    cot_s, out_s, up_s, down_s, a_s, b_s, g_s, xh1_s, r1_s, n1_s, sent_s, act_s, dg_s, low_s, xt_s, sems = rest
    me_dp, me_t = scal[0], scal[1]
    win, width = hid.shape
    groups = up_s.shape[0]
    filling = fill_window(me_t, 1, (own, rx, c1, c3), cot_s, sems)
    if places is None:
        n_dp = 1
        for src, dst in zip(pieces, (out_s, up_s, down_s), strict=True):
            dst[...] = src[...]
    else:
        n_dp = 2 * sum(len(zs) for _, yr, zs, c in places if yr == 0 and c == 0) // 2
        per = width // n_dp
        out_per = LANES // n_dp
        for ref, (xr, yr, zs, c) in zip(pieces, places, strict=True):
            tr = xr * 2 + c
            for i, zr in enumerate(zs):
                src = me_dp ^ (zr * 2 + yr)
                up_s[tr, rows_at(src * per, per, per), :] = ref[i, 0:per]
                down_s[tr, rows_at(src * per, per, per), :] = ref[i, per : 2 * per]
                out_s[rows_at(tr * LANES + src * out_per, out_per, out_per), :] = ref[i, 2 * per : 2 * per + out_per]

    def chunks(fn):
        @pl.loop(0, win // CHUNK)
        def _(i):
            fn(rows_at(i * CHUNK, CHUNK, CHUNK))

    a_s[...] = mm(jnp.transpose(mixt[...]), out_s[...])

    def norm_one(at):
        xhat, rs = norm_forward(hid[at, :] + a_s[at, :])
        xh1_s[at, :] = xhat
        r1_s[at, :] = jnp.broadcast_to(rs, (CHUNK, LANES))
        normed = xhat * nrm[0:1, :] + nrm[1:2, :]
        n1_s[at, :] = normed
        sent_s[at, :] = normed.astype(BF16)

    chunks(norm_one)

    @pl.loop(0, groups)
    def _(g):
        a_s[...] = mm(sent_s[...], up_s[g])

        def gelu(at):
            v = a_s[at, :]
            t = jnp.tanh(GELU_A * (v + GELU_B * v * v * v))
            act_s[g, at, :] = (0.5 * v * (1.0 + t)).astype(BF16)
            dg_s[g, at, :] = 0.5 * (1.0 + t) + 0.5 * v * (1.0 - t * t) * (GELU_A * (1.0 + 3.0 * GELU_B * v * v))

        chunks(gelu)
        n1_s[...] += mm(act_s[g], down_s[g])

    for copy in filling:
        copy.wait()

    def norm_two(i, sums):
        at = rows_at(i * CHUNK, CHUNK, CHUNK)
        xhat, rs = norm_forward(n1_s[at, :])
        n1_s[at, :] = xhat * nrm[2:3, :] + nrm[3:4, :]
        g = cot_s[at, :].astype(F32)
        grad = norm_backward(g, xhat, rs, nrm[2:3, :])
        b_s[at, :] = grad
        low_s[at, :] = grad.astype(BF16)
        return (sums[0] + jnp.sum((g * xhat).reshape(-1, 8, width), axis=0), sums[1] + jnp.sum(g.reshape(-1, 8, width), axis=0))

    zero = jnp.zeros((8, width), F32)
    gain_two, shift_two = lax.fori_loop(0, win // CHUNK, norm_two, (zero, zero))
    put_blocks(me_t, n1_s, res_k, res_1, res_x)

    def put(g, first, height, source, base):
        for r in range(n_dp):
            ref, slot = chunk_of(chunks_o, g, r)
            ref[slot, first : first + height, :] = source[rows_at(base + (r ^ me_dp) * height, height, height), :].astype(BF16)

    xt_s[...] = jnp.transpose(sent_s[...])
    for g in range(groups):
        gdown = mm(jnp.transpose(act_s[g]), low_s[...])
        if places is None:
            gdown_o[g] = gdown.astype(BF16)
        else:
            g_s[...] = gdown
            put(g, per, per, g_s, 0)
        a_s[...] = mm(low_s[...], down_s[g], NT)
        act_s[g] = (a_s[...] * dg_s[g]).astype(BF16)
        gup = mm(xt_s[...], act_s[g])
        if places is None:
            gup_o[g] = gup.astype(BF16)
        else:
            g_s[...] = gup
            put(g, 0, per, g_s, 0)
        b_s[...] += mm(act_s[g], up_s[g], NT)

    def norm_one_back(i, sums):
        at = rows_at(i * CHUNK, CHUNK, CHUNK)
        g = b_s[at, :]
        xhat = xh1_s[at, :]
        grad = norm_backward(g, xhat, r1_s[at, 0:1], nrm[0:1, :])
        gone_o[at, :] = grad
        low_s[at, :] = grad.astype(BF16)
        return (sums[0] + jnp.sum((g * xhat).reshape(-1, 8, width), axis=0), sums[1] + jnp.sum(g.reshape(-1, 8, width), axis=0))

    gain_one, shift_one = lax.fori_loop(0, win // CHUNK, norm_one_back, (zero, zero))
    for k, total in enumerate((gain_one, shift_one, gain_two, shift_two)):
        gnorm_o[k : k + 1, :] = jnp.sum(total, axis=0, keepdims=True)
    gnorm_o[4:8, :] = jnp.zeros((4, width), F32)

    gout = mm(mixt[...], low_s[...])
    if places is None:
        gout_o[...] = gout.astype(BF16)
    else:
        g_s[...] = gout
        for g in range(groups):
            put(g, 2 * per, out_per, g_s, g * LANES)
    gm = mm(low_s[...], out_s[...], NT).astype(BF16)
    for g in range(groups):
        gm_o[g] = gm[:, g * LANES : (g + 1) * LANES]


def attention_back_kernel(fast, scal, hid, qkv, pt, gm, w, gone, gnorm, *rest):
    gi_k, gi_1, gi_x = rest[:3]
    if fast:
        keep_o, send_o = rest[3:5]
    else:
        gattn_o, gpos_o = rest[3:5]
    ht_s, ds_s, dqkv_s, acc_s, dqt_s, g_s = rest[5:]
    me_dp, me_t = scal[0], scal[1]
    win, width = hid.shape
    groups = w.shape[0]
    blocks = win // LANES
    heads = LANES // HD
    ht_s[...] = jnp.transpose(hid[...].astype(BF16))
    acc_s[...] = gone[...]
    lane = lax.broadcasted_iota(jnp.int32, (win, LANES), 1)

    @pl.loop(0, groups)
    def _(g):
        q = qkv[g, :, :LANES]
        k = qkv[g, :, LANES : 2 * LANES]
        v = qkv[g, :, 2 * LANES :]
        d_mixed = gm[g]
        k_t = jnp.transpose(k)
        d_m_h = []
        q_h = []
        for h in range(heads):
            here = (lane >= h * HD) & (lane < (h + 1) * HD)
            q_h.append(jnp.where(here, q, jnp.zeros_like(q)))
            d_m_h.append(jnp.where(here, d_mixed, jnp.zeros_like(q)))
            for j in range(blocks):
                ext = (j + 1) * LANES
                cols = slice(j * LANES, ext)
                p = pt[2 * g + h, :ext, cols].astype(F32)
                dp = mm(v[:ext], d_m_h[h][cols], NT)
                ds = (p * (dp - jnp.sum(p * dp, axis=0, keepdims=True))).astype(BF16)
                ds_s[h, :ext, cols] = ds
                dqt_s[h * HD : (h + 1) * HD, cols] = mm(k_t[h * HD : (h + 1) * HD, :ext], ds) * (HD**-0.5)
        dqkv_s[g, :, :LANES] = jnp.transpose(dqt_s[...]).astype(BF16)
        for i in range(blocks):
            at = slice(i * LANES, (i + 1) * LANES)
            dk = jnp.zeros((LANES, LANES), F32)
            dv = jnp.zeros((LANES, LANES), F32)
            for h in range(heads):
                dk += mm(ds_s[h, at, i * LANES :], q_h[h][i * LANES :])
                dv += mm(pt[2 * g + h, at, i * LANES :], d_m_h[h][i * LANES :])
            dqkv_s[g, at, LANES : 2 * LANES] = dk.astype(BF16)
            dqkv_s[g, at, 2 * LANES :] = dv.astype(BF16)
        acc_s[...] += mm(dqkv_s[g], w[g], NT)

    put_blocks(me_t, acc_s, gi_k, gi_1, gi_x)
    if not fast:
        for g in range(groups):
            gattn_o[g] = mm(ht_s[...], dqkv_s[g]).astype(BF16)
        gpos_o[...] = acc_s[...].astype(BF16)
        return
    n_dp = 2 * keep_o.shape[1]
    per = width // n_dp
    pos_per = win // (n_dp * groups)
    for g in range(groups):
        g_s[...] = mm(ht_s[...], dqkv_s[g])
        for r in range(n_dp):
            d = r ^ me_dp
            ref, slot = (send_o if g & 1 else keep_o), ((g >> 1) * 2 + (r & 1), r >> 1)
            for t in range(3):
                ref[*slot, t * per : (t + 1) * per, :] = g_s[rows_at(d * per, per, per), t * LANES : (t + 1) * LANES].astype(BF16)
            where = (me_t ^ g) * (win // groups) + d * pos_per
            for k in range(width // LANES):
                at = 3 * per + k * pos_per
                ref[*slot, at : at + pos_per, :] = acc_s[rows_at(where, pos_per, pos_per), k * LANES : (k + 1) * LANES].astype(BF16)
            at = 3 * per + width // LANES * pos_per
            tile = gnorm[0:8, rows_at((d >> 1) * LANES, LANES, LANES)]
            ref[*slot, at : at + 16, :] = jnp.concatenate([tile, tile], axis=0).astype(BF16)


def after(value, *others):
    return lax.optimization_barrier((value, *others))[0]


def in_order(keep, r1, r2, r3, me_t):
    flip = (me_t & 1) == 1
    low = [jnp.where(flip, r1, keep), jnp.where(flip, keep, r1)]
    high = [jnp.where(flip, r3, r2), jnp.where(flip, r2, r3)]
    cross = (me_t >> 1) == 1
    return jnp.stack([jnp.where(cross, high[0], low[0]), jnp.where(cross, high[1], low[1]), jnp.where(cross, low[0], high[0]), jnp.where(cross, low[1], high[1])])


def gather_z(value, *others):
    nz = lax.axis_size("dp") // 2
    q, order = value[None], [0]
    step = nz // 2
    while step:
        if step == 1:
            q = after(q, *others)
        q = jnp.concatenate([q, swap(q, step * 2, 0)])
        order = order + [z ^ step for z in order]
        step //= 2
    return q, tuple(order)


def both_cores(found):
    out = []
    for array, place in found:
        out.append((array, (*place, 0)))
        out.append((swap(array, 0, 1), (*place, 1)))
    return [f[0] for f in out], tuple(f[1] for f in out)


def total(*parts):
    return sum(p.astype(F32) for p in parts)


def low(*parts):
    return total(*parts).astype(BF16)


class Reduction:
    def __init__(self, keep_first, keep_rest, send_first, send_rest):
        self.half = keep_first.shape[0] // 4
        self.n = keep_first.shape[0] // 2
        self.sums = [(keep_rest,)]
        self.send_rest = send_rest
        got = swap(send_first, 0, 1)
        self.a = low(keep_first[: self.n], got[: self.n])
        self.b = low(keep_first[self.n :], got[self.n :])

    def terms(self, a, start, stop):
        at = 0 if a else self.n
        found = [k[at + start : at + stop] for k in self.rest]
        for pair in self.got:
            g = pair[0 if a else 1]
            if g.shape[0] >= stop:
                found.append(g[start:stop])
        return found

    def first(self):
        self.rest = [self.sums[0][0], swap(self.send_rest, 0, 1)]
        self.got = [(swap(self.a, 0, 2), swap(self.b, 1, 0))]
        return self.got[0]

    def second(self):
        h = self.half
        a, b = low(*self.terms(True, h, 2 * h)), low(*self.terms(False, h, 2 * h))
        self.got.append((swap(a, 1, 0), swap(b, 0, 2)))
        return self.got[1]

    def over_z(self, *others):
        h = self.half
        arrived = []
        for z in range(1, 2 * h):
            chunk = low(*self.terms(z < h, z % h, z % h + 1))
            arrived.append(swap(after(chunk, *others), 2 * z, 0))
        return arrived

    def result(self, arrived):
        return total(*self.terms(True, 0, 1), *arrived)[0]


class DirectReduction:
    def __init__(self, keep, send):
        got = swap(send, 0, 1)
        self.sums = [low(k, got[i]) for i, k in enumerate(keep)]

    def over_xy(self):
        s = self.sums
        self.parts = [s[0], swap(s[2], 0, 2), swap(s[1], 1, 0), swap(s[3], 1, 2)]
        return self.parts[1:]

    def over_z(self, *others):
        nz = self.parts[0].shape[0]
        return [swap(after(low(*[p[z] for p in self.parts]), *others), 2 * z, 0) for z in range(1, nz)]

    def result(self, arrived):
        return total(*[p[0] for p in self.parts], *arrived)


def adam_step(weight, gradient, moment_one, second, step_rate, decay_rate):
    first_new = BETA_ONE * moment_one + (1.0 - BETA_ONE) * gradient
    second_new = BETA_TWO * second + (1.0 - BETA_TWO) * gradient * gradient
    fixed_first = first_new / (1.0 - BETA_ONE**STEP)
    fixed_second = second_new / (1.0 - BETA_TWO**STEP)
    weight_new = weight - step_rate * (fixed_first / (jnp.sqrt(fixed_second) + ADAM_EPS) + decay_rate * weight)
    return (weight_new, first_new, second_new)


def call(kernel, outs, scratch, args, spaces, mib, flops):
    vmem = pl.BlockSpec(memory_space=pltpu.VMEM)
    kinds = {"s": pl.BlockSpec(memory_space=pltpu.SMEM), "v": vmem, "a": pl.BlockSpec(memory_space=pl.ANY), "h": pl.BlockSpec(memory_space=pltpu.HBM)}
    return pl.pallas_call(
        kernel,
        out_shape=outs,
        in_specs=[kinds[k] for k in spaces],
        out_specs=[vmem] * len(outs),
        scratch_shapes=[pltpu.VMEM(*s) if isinstance(s, tuple) else pltpu.SemaphoreType.DMA(tuple(s)) for s in scratch],
        compiler_params=pltpu.CompilerParams(vmem_limit_bytes=mib * 1024 * 1024),
        cost_estimate=pl.CostEstimate(flops=flops, bytes_accessed=0, transcendentals=0),
    )(*args)


def body(
    inputs,
    segment_ids,
    cotangent,
    attn_proj,
    out_proj,
    up_proj,
    down_proj,
    pos_table,
    norm_params,
    first_attn,
    second_attn,
    first_out,
    second_out,
    first_up,
    second_up,
    first_down,
    second_down,
    first_pos,
    second_pos,
    first_norm,
    second_norm,
):
    n_dp, n_t = lax.axis_size("dp"), lax.axis_size("tensor")
    me_dp, me_t = lax.axis_index("dp"), lax.axis_index("tensor")
    scal = jnp.stack([me_dp, me_t]).astype(jnp.int32)
    windows, block, width = inputs.shape
    win = block * n_t
    inner = up_proj.shape[1]
    group = attn_proj.shape[2]
    per, out_per, pos_per = attn_proj.shape[1], out_proj.shape[0], pos_table.shape[0]
    fast = out_per % 16 == 0 and pos_per % 16 == 0 and 2 * per == LANES
    sds = jax.ShapeDtypeStruct

    if fast:
        ga, gb, xs, c1 = call(
            prepare_kernel,
            [sds((3 * per + width // LANES * pos_per + 16, LANES), BF16), sds((2 * per + out_per, width), BF16), sds((4, block, width), BF16), sds((2, block, width), BF16)],
            [(v.shape, F32) for v in (attn_proj, out_proj, up_proj, down_proj, pos_table, norm_params)] + [[12]],
            [scal, inputs, cotangent, attn_proj, out_proj, up_proj, down_proj, pos_table, norm_params],
            "s" + "h" * 8,
            60,
            1_000_000,
        )
        qa, za = gather_z(ga)
        rx = swap(xs, 0, 2)
        qb, zb = gather_z(gb, qa, rx)
        c1 = swap(c1, 0, 1)
        c3 = swap(rx[2:], 0, 1)
        found_a = [(qa, (0, 0, za)), (swap(qa, 0, 2), (1, 0, za)), (swap(qa, 1, 0), (0, 1, za)), (after(swap(qa, 1, 2), qb), (1, 1, za))]
        a_args, a_places = both_cores(found_a)
        qbx, qby, qbxy = swap(qb, 0, 2), swap(qb, 1, 0), swap(qb, 1, 2)
    else:

        def pair(rel):
            return jnp.concatenate([lax.dynamic_slice_in_dim(v, me_t ^ rel, 1, 0) for v in (inputs, cotangent)])

        rx = swap(jnp.concatenate([pair(2), pair(3)]), 0, 2)
        c1 = swap(pair(1), 0, 1)
        c3 = swap(rx[2:], 0, 1)
        relative = me_t ^ jnp.arange(n_t)
        whole = [lax.all_gather(lax.all_gather(v.astype(BF16), "dp"), "tensor") for v in (attn_proj, out_proj, up_proj, down_proj)]
        attn_w, out_w, up_w, down_w = [jnp.take(v, relative, axis=0) for v in whole]
        attn_w = attn_w.transpose(0, 1, 3, 2, 4).reshape(n_t, width, 3 * group)
        pos_w = lax.all_gather(lax.all_gather(pos_table.astype(BF16), "dp", axis=0, tiled=True), "tensor", axis=0, tiled=True)
        norm_w = lax.all_gather(norm_params, "dp", axis=1, tiled=True)
        norm_w = jnp.concatenate([norm_w, jnp.zeros_like(norm_w)])
        a_args, a_places = [attn_w, pos_w, norm_w], None
        b_args, b_places = [out_w.reshape(n_t * group, width), up_w.reshape(n_t, width, inner), down_w.reshape(n_t, inner, width)], None

    hid, qkv, pt, mixt, attn_all, norm_all = call(
        functools.partial(attention_kernel, a_places, len(a_args)),
        [
            sds((win, width), F32),
            sds((n_t, win, 3 * group), BF16),
            sds((n_t * group // HD, win, win), BF16),
            sds((n_t * group, win), BF16),
            sds((n_t, width, 3 * group), BF16),
            sds((8, width), F32),
        ],
        [((win, width), BF16), ((win, width), BF16), ((win, win), F32), ((n_dp, 16, LANES), F32), [4]],
        [scal, inputs, rx, c1, c3, segment_ids, *a_args],
        "shaaav" + "v" * len(a_args),
        12,
        1_000_000,
    )
    if fast:
        qbxy = after(qbxy, hid)
        b_args, b_places = both_cores([(qb, (0, 0, zb)), (qbx, (1, 0, zb)), (qby, (0, 1, zb)), (qbxy, (1, 1, zb))])

    blocks = [sds((block, width), BF16), sds((1, block, width), BF16), sds((2, block, width), BF16)]
    if fast:
        rows_b = 2 * per + out_per
        grads_b = [sds((n_dp, rows_b, width), BF16)] * 4
    else:
        grads_b = [sds((n_t, width, inner), BF16), sds((n_t, inner, width), BF16), sds((n_t * group, width), BF16)]
    res_k, res_1, res_x, gone, gm, gnorm, *got_b = call(
        functools.partial(ffn_kernel, b_places, len(b_args)),
        [*blocks, sds((win, width), F32), sds((n_t, win, group), BF16), sds((8, width), F32), *grads_b],
        [
            ((win, width), BF16),
            ((n_t * group, width), BF16),
            ((n_t, width, inner), BF16),
            ((n_t, inner, width), BF16),
            ((win, width), F32),
            ((win, width), F32),
            ((win, width), F32),
            ((win, width), F32),
            ((win, LANES), F32),
            ((win, width), F32),
            ((win, width), BF16),
            ((n_t, win, inner), BF16),
            ((n_t, win, inner), F32),
            ((win, width), BF16),
            ((width, win), BF16),
            [4],
        ],
        [scal, cotangent, rx, c1, c3, hid, mixt, norm_all, *b_args],
        "shaaavvv" + "v" * len(b_args),
        24,
        1_000_000,
    )
    if fast:
        red_b = Reduction(*got_b)
        gone = after(gone, red_b.a, red_b.b)
        first_b = red_b.first()

    blocks = [sds((block, width), F32), *blocks[1:]]
    if fast:
        rows_a = 3 * per + width // LANES * pos_per + 16
        grads_a = [sds((4, n_dp // 2, rows_a, LANES), BF16)] * 2
    else:
        grads_a = [sds((n_t, width, 3 * group), BF16), sds((win, width), BF16)]
    gi_k, gi_1, gi_x, *got_a = call(
        functools.partial(attention_back_kernel, fast),
        [*blocks, *grads_a],
        [
            ((width, win), BF16),
            ((LANES // HD, win, win), BF16),
            ((n_t, win, 3 * group), BF16),
            ((win, width), F32),
            ((LANES, win), F32),
            ((width, 3 * group), F32),
        ],
        [scal, hid, qkv, pt, gm, attn_all, gone, gnorm],
        "s" + "v" * 7,
        14,
        1_000_000,
    )
    leaving = jnp.concatenate([res_x[:1], gi_x[:1], res_x[1:], gi_x[1:]])
    if fast:
        red_a = DirectReduction(got_a[0], after(got_a[1], *first_b))
        red_b.second()
        xy_a = red_a.over_xy()
        z_b = red_b.over_z()
        z_a = red_a.over_z(*z_b)
        leaving = after(leaving, *xy_a)
        r2 = swap(leaving, 0, 2)
        sum_b = red_b.result(z_b)
        sum_a = red_a.result(z_a)
    else:
        r2 = swap(leaving, 0, 2)
    r3 = swap(r2[2:], 0, 1)
    outputs = in_order(res_k, swap(res_1, 0, 1)[0], r2[0], r3[0], me_t)
    grad_input = in_order(gi_k, swap(gi_1, 0, 1)[0].astype(F32), r2[1].astype(F32), r3[1].astype(F32), me_t)

    if fast:
        g_attn = sum_a[: 3 * per].reshape(3, per, group)
        at = 3 * per
        n_pos = width // LANES * pos_per
        g_pos = sum_a[at : at + n_pos].reshape(width // LANES, pos_per, LANES).transpose(1, 0, 2).reshape(pos_per, width)
        tile = sum_a[at + n_pos : at + n_pos + 4]
        g_norm = jnp.where((me_dp & 1) == 1, tile[:, LANES // 2 :], tile[:, : LANES // 2])
        g_up, g_down, g_out = sum_b[:per], sum_b[per : 2 * per], sum_b[2 * per :]
    else:

        def reduced(value, own_axis):
            arrived = lax.all_to_all(value, "dp", split_axis=0, concat_axis=0, tiled=True)
            part = arrived.astype(F32).sum(axis=0).astype(BF16)
            arrived = lax.all_to_all(part, "tensor", split_axis=0, concat_axis=0, tiled=True)
            return arrived.astype(F32).sum(axis=0)

        gup, gdown, gout = got_b
        gattn, gpos = got_a
        gup, gdown, gout, gattn = [jnp.take(v, relative, axis=0) for v in (gup, gdown, gout.reshape(n_t, group, width), gattn)]
        g_up = reduced(gup.reshape(n_t, n_dp, per, inner).swapaxes(0, 1), 0)
        g_down = reduced(gdown.reshape(n_t, n_dp, inner // n_dp, width).swapaxes(0, 1), 0)
        g_out = reduced(gout.reshape(n_t, n_dp, out_per, width).swapaxes(0, 1), 0)
        g_pos = reduced(gpos.reshape(n_t, n_dp, pos_per, width).swapaxes(0, 1), 0)
        g_attn = reduced(gattn.reshape(n_t, n_dp, per, 3, group).swapaxes(0, 1), 0).swapaxes(0, 1)
        cut = gnorm[:4].reshape(4, n_dp, width // n_dp).swapaxes(0, 1).astype(BF16)
        g_norm = reduced(jnp.broadcast_to(cut[:, None], (n_dp, n_t, *cut.shape[1:])), 0)

    masters = (attn_proj, out_proj, up_proj, down_proj, pos_table, norm_params)
    gradients = (g_attn, g_out, g_up, g_down, g_pos, g_norm)
    firsts = (first_attn, first_out, first_up, first_down, first_pos, first_norm)
    seconds = (second_attn, second_out, second_up, second_down, second_pos, second_norm)
    updated = []
    for index in range(6):
        updated += adam_step(masters[index], gradients[index], firsts[index], seconds[index], RATES[index], DECAYS[index])
    return (outputs, grad_input, *updated)


def solution(mesh):
    acts = P("dp", "tensor", None)
    attn = P(None, "dp", "tensor")
    both = P(("tensor", "dp"), None)
    up = P("dp", "tensor")
    norm = P(None, "dp")
    return jax.shard_map(
        body,
        mesh=mesh,
        in_specs=(acts, P("dp", None), acts, attn, both, up, both, both, norm, *(attn,) * 2, *(both,) * 2, *(up,) * 2, *(both,) * 4, *(norm,) * 2),
        out_specs=(acts, acts, *(attn,) * 3, *(both,) * 3, *(up,) * 3, *(both,) * 6, *(norm,) * 3),
        check_vma=False,
    )
```

```python
import functools

import jax
import jax.numpy as jnp
from jax import lax
from jax.experimental import pallas as pl
from jax.experimental.pallas import tpu as pltpu
from jax.sharding import PartitionSpec as P

HD = 64
STEP = 10
LANES = 128

NORM_EPS = 1e-05
NEG_FILL = -1e30
BETA_ONE = 0.9
BETA_TWO = 0.95
ADAM_EPS = 1e-08
RATES = (0.03, 0.2, 0.03, 0.02, 0.3, 0.3)
DECAYS = (0.1, 0.1, 0.1, 0.1, 0.1, 0.0)
GELU_A = 0.7978845608028654
GELU_B = 0.044715

F32 = jnp.float32
BF16 = jnp.bfloat16
AXES = ("dp", "tensor")

NN = (((1,), (0,)), ((), ()))
NT = (((1,), (1,)), ((), ()))
TN = (((0,), (0,)), ((), ()))
QUERIES = 256


def total(*parts):
    return sum(p.astype(F32) for p in parts)


def low(*parts):
    return total(*parts).astype(BF16)


def adam_step(weight, gradient, moment_one, second, step_rate, decay_rate):
    first_new = BETA_ONE * moment_one + (1.0 - BETA_ONE) * gradient
    second_new = BETA_TWO * second + (1.0 - BETA_TWO) * gradient * gradient
    fixed_first = first_new / (1.0 - BETA_ONE**STEP)
    fixed_second = second_new / (1.0 - BETA_TWO**STEP)
    weight_new = weight - step_rate * (fixed_first / (jnp.sqrt(fixed_second) + ADAM_EPS) + decay_rate * weight)
    return (weight_new, first_new, second_new)


def mm(a, b, dims=NN):
    return lax.dot_general(a, b, dims, preferred_element_type=F32)


def swap(value, rd, rt):
    n_t = lax.axis_size("tensor")
    mask = rd * n_t + rt
    return lax.ppermute(value, AXES, [(i, i ^ mask) for i in range(lax.axis_size("dp") * n_t)])


def rows_at(start, size, step):
    return pl.ds(pl.multiple_of(start, step), size)


def by_head(rows):
    lane = lax.broadcasted_iota(jnp.int32, (rows, LANES), 1)

    def keep(h):
        here = (lane >= h * HD) & (lane < (h + 1) * HD)
        return lambda v: jnp.where(here, v, jnp.zeros_like(v))

    return [keep(h) for h in range(LANES // HD)]


def fill_window(me_t, which, parts, out_ref, sems):
    own, rx, c1, c3 = parts
    n = own.shape[1]
    sources = (own.at[me_t], c1.at[which], rx.at[which], c3.at[which])
    copies = [pltpu.make_async_copy(src, out_ref.at[rows_at((me_t ^ r) * n, n, n), :], sems.at[r]) for r, src in enumerate(sources)]
    for copy in copies:
        copy.start()
    return copies


def copies_in(moves, sems):
    copies = [pltpu.make_async_copy(src, dst, sems.at[i]) for i, (src, dst) in enumerate(moves)]
    for copy in copies:
        copy.start()
    return copies


def prepare_kernel(scal, inputs, cot, attn, pos, norm, out, up, down, ga, gb, xs, c1, attn_s, pos_s, norm_s, out_s, up_s, down_s, sems):
    me_t = scal[1]
    moves = [(attn, attn_s), (pos, pos_s), (norm, norm_s), (up, up_s), (down, down_s), (out, out_s)]
    for rel, ref, at in ((2, xs, 0), (3, xs, 2), (1, c1, 0)):
        moves += [(inputs.at[me_t ^ rel], ref.at[at]), (cot.at[me_t ^ rel], ref.at[at + 1])]
    copies = copies_in(moves, sems)
    for copy in copies[:3]:
        copy.wait()
    per = attn.shape[1]
    pos_per = pos.shape[0]
    tiles = pos.shape[1] // LANES
    for t in range(3):
        ga[0, t * per : (t + 1) * per, :] = attn_s[t].astype(BF16)
    for k in range(tiles):
        at = 3 * per + k * pos_per
        ga[0, at : at + pos_per, :] = pos_s[:, k * LANES : (k + 1) * LANES].astype(BF16)
    at = 3 * per + tiles * pos_per
    both = norm_s[...]
    both = jnp.concatenate([both, both], axis=1)
    both = jnp.concatenate([both, jnp.zeros_like(both)], axis=0)
    high = both.astype(BF16)
    rest = (both - high.astype(F32)).astype(BF16)
    ga[0, at : at + 16, :] = jnp.concatenate([high, rest], axis=0)
    for copy in copies[3:6]:
        copy.wait()
    gb[0, 0:per, :] = up_s[...].astype(BF16)
    gb[0, per : 2 * per, :] = down_s[...].astype(BF16)
    gb[0, 2 * per :, :] = out_s[...].astype(BF16)
    for copy in copies[6:]:
        copy.wait()


def stack_kernel(own, got, both):
    n = own.shape[0]
    both[:n] = own[...]
    both[n:] = got[...]


def attention_kernel(places, n_pieces, scal, *refs):
    own, rx, c1, c3, segs = refs[:5]
    pieces = refs[5 : 5 + n_pieces]
    hid_o, qkv_h, pt_h, mix_o, w_h, nrm_o, x_s, pos_s, bias_s, nrm_s, w_o, qkv_o, pt_o, sems, out_sems = refs[5 + n_pieces :]
    leaving = []

    def leave(src, dst):
        leaving.append(pltpu.make_async_copy(src, dst, out_sems.at[len(leaving)]))
        leaving[-1].start()

    me_dp, me_t = scal[0], scal[1]
    win, width = x_s.shape
    groups = w_o.shape[1] // (3 * LANES)
    filling = fill_window(me_t, 0, (own, rx, c1, c3), x_s, sems)
    if places is None:
        w_o[...] = pieces[0][...]
        pos_s[...] = pieces[1][...]
        nrm_o[...] = pieces[2][...]
    else:
        n_dp = nrm_s.shape[0]
        per = width // n_dp
        pos_per = win // (n_dp * groups)
        for ref, (xr, yr, zs, c) in zip(pieces, places, strict=True):
            tr = xr * 2 + c
            for i, zr in enumerate(zs):
                src = me_dp ^ (zr * 2 + yr)
                for t in range(3):
                    at = (tr * 3 + t) * LANES
                    w_o[rows_at(src * per, per, per), at : at + LANES] = ref[i, t * per : (t + 1) * per]
                where = (me_t ^ tr) * (win // groups) + src * pos_per
                for k in range(width // LANES):
                    at = 3 * per + k * pos_per
                    pos_s[rows_at(where, pos_per, pos_per), k * LANES : (k + 1) * LANES] = ref[i, at : at + pos_per]
                if tr == 0:
                    at = 3 * per + width // LANES * pos_per
                    nrm_s[src] = ref[i, at : at + 16].astype(F32)
        low_lane = lax.broadcasted_iota(jnp.int32, (8, LANES), 1) < per
        for j in range(n_dp // 2):
            left = nrm_s[2 * j]
            right = nrm_s[2 * j + 1]
            both = jnp.where(low_lane, left[0:8] + left[8:16], right[0:8] + right[8:16])
            nrm_o[:, j * LANES : (j + 1) * LANES] = both

    leave(w_o, w_h)

    seg = segs[pl.ds(me_t, 1), :].astype(F32)
    seg_col = jnp.transpose(jnp.broadcast_to(seg, (LANES, win)))
    for i in range(win // LANES):
        key_seg = seg_col[i * LANES : (i + 1) * LANES, 0:1]
        key_at = lax.broadcasted_iota(jnp.int32, (LANES, win), 0) + i * LANES
        query_at = lax.broadcasted_iota(jnp.int32, (LANES, win), 1)
        counts = (key_seg == seg) & (query_at >= key_at)
        bias_s[i * LANES : (i + 1) * LANES, :] = jnp.where(counts, 0.0, NEG_FILL)

    for copy in filling:
        copy.wait()
    hidden = x_s[...].astype(F32) + pos_s[...].astype(F32)
    hid_o[...] = hidden
    x_s[...] = hidden.astype(BF16)
    heads = by_head(win)
    for g in range(groups):
        at = g * 3 * LANES
        qkv = mm(x_s[...], w_o[:, at : at + 3 * LANES]).astype(BF16)
        q = qkv[:, :LANES] * jnp.asarray(HD**-0.5, BF16)
        k = qkv[:, LANES : 2 * LANES]
        v = qkv[:, 2 * LANES :]
        qkv_o[:, at : at + LANES] = q
        qkv_o[:, at + LANES : at + 3 * LANES] = qkv[:, LANES:]
        for j in range(win // QUERIES):
            ext = (j + 1) * QUERIES
            cols = slice(j * QUERIES, ext)
            mixed = jnp.zeros((QUERIES, LANES), F32)
            for h, only in enumerate(heads):
                s = mm(only(k)[:ext], q[cols], NT) + bias_s[:ext, cols]
                e = jnp.exp(s - jnp.max(s, axis=0, keepdims=True))
                p = (e * (1.0 / jnp.sum(e, axis=0, keepdims=True))).astype(BF16)
                pt_o[len(heads) * g + h, :ext, cols] = p
                mixed += mm(p, only(v)[:ext], TN)
            mix_o[cols, g * LANES : (g + 1) * LANES] = mixed.astype(BF16)
            for h in range(len(heads)):
                leave(pt_o.at[len(heads) * g + h, :ext, cols], pt_h.at[len(heads) * g + h, :ext, cols])
    leave(qkv_o, qkv_h)
    for copy in leaving:
        copy.wait()


def norm_forward(v):
    center = v - jnp.mean(v, axis=-1, keepdims=True)
    rs = lax.rsqrt(jnp.mean(center * center, axis=-1, keepdims=True) + NORM_EPS)
    return center * rs, rs


def norm_backward(g, xhat, rs, gain):
    e = g * gain
    return rs * (e - jnp.mean(e, axis=-1, keepdims=True) - xhat * jnp.mean(e * xhat, axis=-1, keepdims=True))


def put_blocks(me_t, value, keep, s1, sx):
    n = keep.shape[0]
    for r, ref in ((0, keep), (1, s1.at[0]), (2, sx.at[0]), (3, sx.at[1])):
        ref[...] = value[rows_at((me_t ^ r) * n, n, n), :].astype(ref.dtype)


CHUNK = 128


def chunk_of(refs, tr, r):
    c, xr, yr, zr = tr & 1, tr >> 1, r & 1, r >> 1
    half = refs[0].shape[0] // 4
    if zr < half:
        first, slot = xr == 1, yr * half + zr
    else:
        first, slot = yr == 1, 2 * half + xr * half + zr - half
    return refs[2 * c + (0 if first else 1)], slot


def ffn_kernel(places, n_pieces, scal, *refs):
    own, rx, c1, c3, hid, mixed, nrm = refs[:7]
    pieces = refs[7 : 7 + n_pieces]
    rest = refs[7 + n_pieces :]
    res_k, res_1, res_x, gone_o, gm_o, gnorm_o = rest[:6]
    if places is None:
        gup_o, gdown_o, gout_o = rest[6:9]
        rest = rest[9:]
    else:
        chunks_o = rest[6:10]
        rest = rest[10:]
    cot_s, out_s, up_s, down_s, a_s, b_s, g_s, xh1_s, r1_s, n1_s, sent_s, act_s, dg_s, low_s, xt_s, sems = rest
    me_dp, me_t = scal[0], scal[1]
    win, width = hid.shape
    groups = up_s.shape[0]
    filling = fill_window(me_t, 1, (own, rx, c1, c3), cot_s, sems)
    if places is None:
        n_dp = 1
        for src, dst in zip(pieces, (out_s, up_s, down_s), strict=True):
            dst[...] = src[...]
    else:
        n_dp = 2 * sum(len(zs) for _, yr, zs, c in places if yr == 0 and c == 0) // 2
        per = width // n_dp
        out_per = LANES // n_dp
        for ref, (xr, yr, zs, c) in zip(pieces, places, strict=True):
            tr = xr * 2 + c
            for i, zr in enumerate(zs):
                src = me_dp ^ (zr * 2 + yr)
                up_s[tr, rows_at(src * per, per, per), :] = ref[i, 0:per]
                down_s[tr, rows_at(src * per, per, per), :] = ref[i, per : 2 * per]
                out_s[rows_at(tr * LANES + src * out_per, out_per, out_per), :] = ref[i, 2 * per : 2 * per + out_per]

    def chunks(fn):
        for i in range(win // CHUNK):
            fn(slice(i * CHUNK, (i + 1) * CHUNK))

    a_s[0] = mm(mixed[...], out_s[...])

    def norm_one(at):
        xhat, rs = norm_forward(hid[at, :] + a_s[0, at, :])
        xh1_s[at, :] = xhat
        r1_s[at, :] = jnp.broadcast_to(rs, (CHUNK, LANES))
        normed = xhat * nrm[0:1, :] + nrm[1:2, :]
        n1_s[at, :] = normed
        sent_s[at, :] = normed.astype(BF16)

    chunks(norm_one)

    for g in range(groups):
        a_s[g % 2] = mm(sent_s[...], up_s[g])

        def gelu(at, g=g):
            v = a_s[g % 2, at, :]
            t = jnp.tanh(GELU_A * (v + GELU_B * v * v * v))
            act_s[g, at, :] = (0.5 * v * (1.0 + t)).astype(BF16)
            dg_s[g, at, :] = 0.5 * (1.0 + t) + 0.5 * v * (1.0 - t * t) * (GELU_A * (1.0 + 3.0 * GELU_B * v * v))

        chunks(gelu)
        n1_s[...] += mm(act_s[g], down_s[g])

    for copy in filling:
        copy.wait()

    def norm_two(i, sums):
        at = slice(i * CHUNK, (i + 1) * CHUNK)
        xhat, rs = norm_forward(n1_s[at, :])
        n1_s[at, :] = xhat * nrm[2:3, :] + nrm[3:4, :]
        g = cot_s[at, :].astype(F32)
        grad = norm_backward(g, xhat, rs, nrm[2:3, :])
        b_s[at, :] = grad
        low_s[at, :] = grad.astype(BF16)
        return (sums[0] + jnp.sum((g * xhat).reshape(-1, 8, width), axis=0), sums[1] + jnp.sum(g.reshape(-1, 8, width), axis=0))

    def every(step):
        sums = (jnp.zeros((8, width), F32),) * 2
        for i in range(win // CHUNK):
            sums = step(i, sums)
        return sums

    gain_two, shift_two = every(norm_two)
    put_blocks(me_t, n1_s, res_k, res_1, res_x)

    def put(g, first, height, source, base):
        for r in range(n_dp):
            ref, slot = chunk_of(chunks_o, g, r)
            ref[slot, first : first + height, :] = source[rows_at(base + (r ^ me_dp) * height, height, height), :]

    xt_s[...] = jnp.transpose(sent_s[...])
    for g in range(groups):
        gdown = mm(jnp.transpose(act_s[g]), low_s[...])
        if places is None:
            gdown_o[g] = gdown.astype(BF16)
        else:
            g_s[0] = gdown.astype(BF16)
            put(g, per, per, g_s.at[0], 0)
        act_s[g] = (mm(low_s[...], down_s[g], NT) * dg_s[g]).astype(BF16)
        gup = mm(xt_s[...], act_s[g])
        if places is None:
            gup_o[g] = gup.astype(BF16)
        else:
            g_s[1] = gup.astype(BF16)
            put(g, 0, per, g_s.at[1], 0)
        b_s[...] += mm(act_s[g], up_s[g], NT)

    def norm_one_back(i, sums):
        at = slice(i * CHUNK, (i + 1) * CHUNK)
        g = b_s[at, :]
        xhat = xh1_s[at, :]
        grad = norm_backward(g, xhat, r1_s[at, 0:1], nrm[0:1, :])
        gone_o[at, :] = grad
        low_s[at, :] = grad.astype(BF16)
        return (sums[0] + jnp.sum((g * xhat).reshape(-1, 8, width), axis=0), sums[1] + jnp.sum(g.reshape(-1, 8, width), axis=0))

    gain_one, shift_one = every(norm_one_back)
    for k, total in enumerate((gain_one, shift_one, gain_two, shift_two)):
        gnorm_o[k : k + 1, :] = jnp.sum(total, axis=0, keepdims=True)
    gnorm_o[4:8, :] = jnp.zeros((4, width), F32)

    gout = mm(jnp.transpose(mixed[...]), low_s[...])
    if places is None:
        gout_o[...] = gout.astype(BF16)
    else:
        g_s[0] = gout.astype(BF16)
        for g in range(groups):
            put(g, 2 * per, out_per, g_s.at[0], g * LANES)
    gm = mm(low_s[...], out_s[...], NT).astype(BF16)
    for g in range(groups):
        gm_o[g] = gm[:, g * LANES : (g + 1) * LANES]


def attention_back_kernel(fast, scal, hid, qkv_h, pt_h, gm, w_h, gone, gnorm, *rest):
    gi_k, gi_1, gi_x = rest[:3]
    if fast:
        chunks_o = rest[3:7]
        rest = rest[7:]
    else:
        gattn_o, gpos_o = rest[3:5]
        rest = rest[5:]
    ht_s, ds_s, dqkv_s, acc_s, g_s, qkv, pt, w, sems = rest
    me_dp, me_t = scal[0], scal[1]
    win, width = hid.shape
    groups = w.shape[1] // (3 * LANES)
    heads = by_head(win)
    arriving = [pltpu.make_async_copy(qkv_h, qkv, sems.at[0])]
    for n in range(pt.shape[0]):
        for j in range(win // QUERIES):
            ext = (j + 1) * QUERIES
            cols = slice(j * QUERIES, ext)
            arriving.append(pltpu.make_async_copy(pt_h.at[n, :ext, cols], pt.at[n, :ext, cols], sems.at[len(arriving)]))
    arriving.append(pltpu.make_async_copy(w_h, w, sems.at[len(arriving)]))
    for copy in arriving:
        copy.start()
    ht_s[...] = jnp.transpose(hid[...].astype(BF16))
    for g in range(groups):
        at = g * 3 * LANES
        if g == 0:
            arriving[0].wait()
        per_group = len(heads) * (win // QUERIES)
        for copy in arriving[1 + g * per_group : 1 + (g + 1) * per_group]:
            copy.wait()
        q = qkv[:, at : at + LANES]
        k = qkv[:, at + LANES : at + 2 * LANES]
        v = qkv[:, at + 2 * LANES : at + 3 * LANES]
        d_mixed = gm[g]
        for j in range(win // QUERIES):
            ext = (j + 1) * QUERIES
            cols = slice(j * QUERIES, ext)
            dq = jnp.zeros((QUERIES, LANES), F32)
            for h, only in enumerate(heads):
                p = pt[len(heads) * g + h, :ext, cols].astype(F32)
                dp = mm(v[:ext], only(d_mixed)[cols], NT)
                ds = (p * (dp - jnp.sum(p * dp, axis=0, keepdims=True))).astype(BF16)
                ds_s[len(heads) * g + h, :ext, cols] = ds
                dq += mm(ds, only(k)[:ext], TN)
            dqkv_s[cols, at : at + LANES] = (dq * HD**-0.5).astype(BF16)
        for i in range(win // QUERIES):
            rows = slice(i * QUERIES, (i + 1) * QUERIES)
            dk = jnp.zeros((QUERIES, LANES), F32)
            dv = jnp.zeros((QUERIES, LANES), F32)
            for h, only in enumerate(heads):
                dk += mm(ds_s[len(heads) * g + h, rows, i * QUERIES :], only(q)[i * QUERIES :])
                dv += mm(pt[len(heads) * g + h, rows, i * QUERIES :], only(d_mixed)[i * QUERIES :])
            dqkv_s[rows, at + LANES : at + 2 * LANES] = dk.astype(BF16)
            dqkv_s[rows, at + 2 * LANES : at + 3 * LANES] = dv.astype(BF16)
    arriving[-1].wait()
    acc_s[...] = gone[...] + mm(dqkv_s[...], w[...], NT)

    put_blocks(me_t, acc_s, gi_k, gi_1, gi_x)
    if not fast:
        for g in range(groups):
            gattn_o[g] = mm(ht_s[...], dqkv_s[:, g * 3 * LANES : (g + 1) * 3 * LANES]).astype(BF16)
        gpos_o[...] = acc_s[...].astype(BF16)
        return
    n_dp = chunks_o[0].shape[0]
    per = width // n_dp
    pos_per = win // (n_dp * groups)
    for g in range(groups):
        g_s[g % 2] = mm(ht_s[...], dqkv_s[:, g * 3 * LANES : (g + 1) * 3 * LANES]).astype(BF16)
        for r in range(n_dp):
            d = r ^ me_dp
            ref, slot = chunk_of(chunks_o, g, r)
            for t in range(3):
                ref[slot, t * per : (t + 1) * per, :] = g_s[g % 2, rows_at(d * per, per, per), t * LANES : (t + 1) * LANES]
            where = (me_t ^ g) * (win // groups) + d * pos_per
            for k in range(width // LANES):
                at = 3 * per + k * pos_per
                ref[slot, at : at + pos_per, :] = acc_s[rows_at(where, pos_per, pos_per), k * LANES : (k + 1) * LANES].astype(BF16)
            at = 3 * per + width // LANES * pos_per
            tile = gnorm[0:8, rows_at((d >> 1) * LANES, LANES, LANES)]
            ref[slot, at : at + 16, :] = jnp.concatenate([tile, tile], axis=0).astype(BF16)


def near_kernel(rest, got, x, y, x2, y2, own, far, odd):
    own[...] = total(rest[0], got[0], x[0], x2[0])
    far[...] = total(rest[4], got[4], y[0], y2[0])
    odd[0] = low(rest[1], got[1], x[1], x2[1])
    odd[1] = low(rest[5], got[5], y[1], y2[1])


def second_kernel(done, rest, got, x, y, a, b):
    del done
    for i in range(2):
        a[i] = low(rest[2 + i], got[2 + i], x[2 + i])
        b[i] = low(rest[6 + i], got[6 + i], y[2 + i])


def far_kernel(own, far, near, own_o, far_o):
    own_o[...] = total(own[...], near[0])
    far_o[0] = low(far[...], near[1])


def far_near_kernel(own, far, near, rest, got, x, y, x2, y2, own_o, far_o, *others):
    far_kernel(own, far, near, own_o, far_o)
    near_kernel(rest, got, x, y, x2, y2, *others)


def update(refs, gradient, rate, decay):
    weight, one, two, new_weight, new_one, new_two = refs
    new_weight[...], new_one[...], new_two[...] = adam_step(weight[...], gradient, one[...], two[...], rate, decay)


def rows_update_kernel(which, own, far, *refs):
    n = len(which)
    *refs, token = refs
    token[...] = jnp.zeros_like(token)
    grad = total(own[...], far[0])
    at = 0
    for i, index in enumerate(which):
        height = refs[i].shape[0]
        update(refs[i :: n], grad[at : at + height], RATES[index], DECAYS[index])
        at += height


def tiles_update_kernel(scal, done, own, far, *refs):
    del done
    attn, pos, norm = refs[0::3], refs[1::3], refs[2::3]
    grad = total(own[...], far[0])
    per = attn[0].shape[1]
    pos_per, width = pos[0].shape
    update(attn, grad[: 3 * per].reshape(attn[0].shape), RATES[0], DECAYS[0])
    at = 3 * per
    rows = [grad[at + k * pos_per : at + (k + 1) * pos_per] for k in range(width // LANES)]
    update(pos, jnp.concatenate(rows, axis=1), RATES[4], DECAYS[4])
    at += width // LANES * pos_per
    tile = grad[at : at + 8]
    half = jnp.where((scal[0] & 1) == 1, tile[:4, LANES // 2 :], tile[:4, : LANES // 2])
    update(norm, half, RATES[5], DECAYS[5])


def finish_kernel(scal, done, res_k, gi_k, res_1, gi_1, r2, r3, res_o, gi_o, token):
    token[...] = done[...]
    me_t = scal[1]
    for r, (res, gi) in enumerate(((res_k[...], gi_k[...]), (res_1[0], gi_1[0]), (r2[0], r2[1]), (r3[0], r3[1]))):
        res_o[me_t ^ r] = res
        gi_o[me_t ^ r] = gi.astype(F32)


def after(value, *others):
    return lax.optimization_barrier((value, *others))[0]


def gather_z(value, *others):
    nz = lax.axis_size("dp") // 2
    q, order = value, [0]
    step = nz // 2
    while step:
        if step == 1:
            q = after(q, *others)
        out = jax.ShapeDtypeStruct((2 * q.shape[0], *q.shape[1:]), q.dtype)
        q = call(stack_kernel, [out], [], [q, swap(q, step * 2, 0)], "vv", 6, 1_000)[0]
        order = order + [z ^ step for z in order]
        step //= 2
    return q, tuple(order)


def gather_xy(q, order, qx=None, qy=None, *others):
    half = len(order) // 2
    if qx is None:
        qx, qy = swap(q, 0, 2), swap(q, 1, 0)
    a, b = after(qx[:half], *others), after(qy[half:], *others)
    return [(q, (0, 0, order)), (qx, (1, 0, order)), (qy, (0, 1, order)), (swap(a, 1, 0), (1, 1, order[:half])), (swap(b, 0, 2), (1, 1, order[half:]))]


def both_cores(found):
    out = []
    for array, place in found:
        out.append((array, (*place, 0)))
        out.append((swap(array, 0, 1), (*place, 1)))
    return [f[0] for f in out], tuple(f[1] for f in out)


class Reduction:
    def __init__(self, keep_first, keep_rest, send_first, send_rest):
        self.half = keep_first.shape[0] // 4
        self.n = keep_first.shape[0] // 2
        self.sums = [(keep_rest,)]
        self.send_rest = send_rest
        got = swap(send_first, 0, 1)
        self.a = low(keep_first[: self.n], got[: self.n])
        self.b = low(keep_first[self.n :], got[self.n :])

    def terms(self, a, start, stop):
        at = 0 if a else self.n
        found = [k[at + start : at + stop] for k in self.rest]
        for pair in self.got:
            g = pair[0 if a else 1]
            if g.shape[0] >= stop:
                found.append(g[start:stop])
        return found

    def first(self):
        self.rest = [self.sums[0][0], swap(self.send_rest, 0, 1)]
        self.got = [(swap(self.a, 0, 2), swap(self.b, 1, 0))]
        return self.got[0]

    def second(self, *others):
        h = self.half
        a, b = [after(low(*self.terms(part, h, 2 * h)), *others) for part in (True, False)]
        self.got.append((swap(a, 1, 0), swap(b, 0, 2)))
        return self.got[1]

    def over_z(self, *others):
        h = self.half
        arrived = []
        for z in range(1, 2 * h):
            chunk = low(*self.terms(z < h, z % h, z % h + 1))
            arrived.append(swap(after(chunk, *others), 2 * z, 0))
        return arrived

    def result(self, arrived):
        return total(*self.terms(True, 0, 1), *arrived)[0]


def call(kernel, outs, scratch, args, spaces, mib, flops):
    vmem = pl.BlockSpec(memory_space=pltpu.VMEM)
    args = [pltpu.with_memory_space_constraint(v, pltpu.HBM) if k == "h" else v for v, k in zip(args, spaces, strict=True)]
    kinds = {"s": pl.BlockSpec(memory_space=pltpu.SMEM), "v": vmem, "a": pl.BlockSpec(memory_space=pl.ANY), "h": pl.BlockSpec(memory_space=pltpu.HBM)}
    return pl.pallas_call(
        kernel,
        out_shape=outs,
        in_specs=[kinds[k] for k in spaces],
        out_specs=[vmem if isinstance(v, jax.ShapeDtypeStruct) else kinds["h"] for v in outs],
        scratch_shapes=[pltpu.VMEM(*s) if isinstance(s, tuple) else pltpu.SemaphoreType.DMA(tuple(s)) for s in scratch],
        compiler_params=pltpu.CompilerParams(vmem_limit_bytes=mib * 1024 * 1024),
        cost_estimate=pl.CostEstimate(flops=flops, bytes_accessed=0, transcendentals=0),
    )(*args)


def body(
    inputs,
    segment_ids,
    cotangent,
    attn_proj,
    out_proj,
    up_proj,
    down_proj,
    pos_table,
    norm_params,
    first_attn,
    second_attn,
    first_out,
    second_out,
    first_up,
    second_up,
    first_down,
    second_down,
    first_pos,
    second_pos,
    first_norm,
    second_norm,
):
    n_dp, n_t = lax.axis_size("dp"), lax.axis_size("tensor")
    me_dp, me_t = lax.axis_index("dp"), lax.axis_index("tensor")
    scal = jnp.stack([me_dp, me_t]).astype(jnp.int32)
    windows, block, width = inputs.shape
    win = block * n_t
    inner = up_proj.shape[1]
    group = attn_proj.shape[2]
    per, out_per, pos_per = attn_proj.shape[1], out_proj.shape[0], pos_table.shape[0]
    fast = out_per % 16 == 0 and pos_per % 16 == 0 and 2 * per == LANES
    sds = jax.ShapeDtypeStruct

    if fast:
        ga, gb, xs, c1 = call(
            prepare_kernel,
            [
                sds((1, 3 * per + width // LANES * pos_per + 16, LANES), BF16),
                sds((1, 2 * per + out_per, width), BF16),
                sds((4, block, width), BF16),
                sds((2, block, width), BF16),
            ],
            [(v.shape, F32) for v in (attn_proj, pos_table, norm_params, out_proj, up_proj, down_proj)] + [[12]],
            [scal, inputs, cotangent, attn_proj, pos_table, norm_params, out_proj, up_proj, down_proj],
            "s" + "h" * 8,
            8,
            1_000,
        )
        qa, za = gather_z(ga)
        rx = swap(xs, 0, 2)
        qb, zb = gather_z(gb, qa)
        c1 = swap(c1, 0, 1)
        c3 = swap(rx[2:], 0, 1)
        qax, qay, qaxy = swap(qa, 0, 2), swap(qa, 1, 0), swap(qa, 1, 2)
        a_args, a_places = both_cores([(qa, (0, 0, za)), (qax, (1, 0, za)), (qay, (0, 1, za)), (qaxy, (1, 1, za))])
        qb = after(qb, rx, qax, qay)
        qbx, qby = swap(qb, 0, 2), swap(qb, 1, 0)
    else:

        def pair(rel):
            return jnp.concatenate([lax.dynamic_slice_in_dim(v, me_t ^ rel, 1, 0) for v in (inputs, cotangent)])

        rx = swap(jnp.concatenate([pair(2), pair(3)]), 0, 2)
        c1 = swap(pair(1), 0, 1)
        c3 = swap(rx[2:], 0, 1)
        relative = me_t ^ jnp.arange(n_t)
        whole = [lax.all_gather(lax.all_gather(v.astype(BF16), "dp"), "tensor") for v in (attn_proj, out_proj, up_proj, down_proj)]
        attn_w, out_w, up_w, down_w = [jnp.take(v, relative, axis=0) for v in whole]
        attn_w = attn_w.transpose(1, 3, 0, 2, 4).reshape(width, n_t * 3 * group)
        pos_w = lax.all_gather(lax.all_gather(pos_table.astype(BF16), "dp", axis=0, tiled=True), "tensor", axis=0, tiled=True)
        norm_w = lax.all_gather(norm_params, "dp", axis=1, tiled=True)
        norm_w = jnp.concatenate([norm_w, jnp.zeros_like(norm_w)])
        a_args, a_places = [attn_w, pos_w, norm_w], None
        b_args, b_places = [out_w.reshape(n_t * group, width), up_w.reshape(n_t, width, inner), down_w.reshape(n_t, inner, width)], None

    hid, qkv, pt, mixed, attn_all, norm_all = call(
        functools.partial(attention_kernel, a_places, len(a_args)),
        [
            sds((win, width), F32),
            pltpu.HBM((win, n_t * 3 * group), BF16),
            pltpu.HBM((n_t * group // HD, win, win), BF16),
            sds((win, n_t * group), BF16),
            pltpu.HBM((width, n_t * 3 * group), BF16),
            sds((8, width), F32),
        ],
        [((win, width), BF16), ((win, width), BF16), ((win, win), F32), ((n_dp, 16, LANES), F32), ((width, n_t * 3 * group), BF16), ((win, n_t * 3 * group), BF16), ((n_t * group // HD, win, win), BF16), [4], [32]],
        [scal, inputs, rx, c1, c3, segment_ids, *a_args],
        "shaaav" + "v" * len(a_args),
        14,
        1_000_000,
    )
    if fast:
        b_args, b_places = both_cores(gather_xy(qb, zb, qbx, qby, hid))

    blocks = [sds((block, width), BF16), sds((1, block, width), BF16), sds((2, block, width), BF16)]
    if fast:
        rows_b = 2 * per + out_per
        grads_b = [sds((n_dp, rows_b, width), BF16)] * 4
    else:
        grads_b = [sds((n_t, width, inner), BF16), sds((n_t, inner, width), BF16), sds((n_t * group, width), BF16)]
    res_k, res_1, res_x, gone, gm, gnorm, *got_b = call(
        functools.partial(ffn_kernel, b_places, len(b_args)),
        [*blocks, sds((win, width), F32), sds((n_t, win, group), BF16), sds((8, width), F32), *grads_b],
        [
            ((win, width), BF16),
            ((n_t * group, width), BF16),
            ((n_t, width, inner), BF16),
            ((n_t, inner, width), BF16),
            ((2, win, width), F32),
            ((win, width), F32),
            ((2, win, width), BF16),
            ((win, width), F32),
            ((win, LANES), F32),
            ((win, width), F32),
            ((win, width), BF16),
            ((n_t, win, inner), BF16),
            ((n_t, win, inner), F32),
            ((win, width), BF16),
            ((width, win), BF16),
            [4],
        ],
        [scal, cotangent, rx, c1, c3, hid, mixed, norm_all, *b_args],
        "shaaavvv" + "v" * len(b_args),
        22,
        1_000_000,
    )
    if fast:
        red_b = Reduction(*got_b)
        gone = after(gone, red_b.a, red_b.b)
        first_b = red_b.first()

    blocks = [sds((block, width), F32), *blocks[1:]]
    if fast:
        rows_a = 3 * per + width // LANES * pos_per + 16
        grads_a = [sds((n_dp, rows_a, LANES), BF16)] * 4
    else:
        grads_a = [sds((n_t, width, 3 * group), BF16), sds((win, width), BF16)]
    gi_k, gi_1, gi_x, *got_a = call(
        functools.partial(attention_back_kernel, fast),
        [*blocks, *grads_a],
        [
            ((width, win), BF16),
            ((n_t * group // HD, win, win), BF16),
            ((win, n_t * 3 * group), BF16),
            ((win, width), F32),
            ((2, width, 3 * group), BF16),
            ((win, n_t * 3 * group), BF16),
            ((n_t * group // HD, win, win), BF16),
            ((width, n_t * 3 * group), BF16),
            [2 + 2 * n_t * group // HD],
        ],
        [scal, hid, qkv, pt, gm, attn_all, gone, gnorm],
        "svhhvhvv",
        18,
        1_000_000,
    )
    leaving = jnp.concatenate([res_x[:1], gi_x[:1], res_x[1:], gi_x[1:]])
    if fast:
        keep_first, keep_rest, send_first, send_rest = got_a
        red_a = Reduction(keep_first, keep_rest, after(send_first, *first_b), send_rest)
        first_a, second_b = red_a.first(), red_b.second()
        chunk_b, chunk_a = got_b[0].shape[1:], got_a[0].shape[1:]
        before_z = [[sds(chunk, F32), sds(chunk, F32), sds((2, *chunk), BF16)] for chunk in (chunk_b, chunk_a)]
        last = [[sds(chunk, F32), sds((1, *chunk), BF16)] for chunk in (chunk_b, chunk_a)]
        own_b, far_b, odd_b = call(near_kernel, before_z[0], [], [*red_b.rest, *first_b, *second_b], "v" * 6, 8, 1_000)
        a_y, a_x = call(second_kernel, [sds((2, *chunk_a), BF16)] * 2, [], [own_b, *red_a.rest, *first_a], "avvvv", 8, 1_000)
        second_a = swap(a_y, 1, 0), swap(a_x, 0, 2)
        near_b = swap(odd_b, 2, 0)
        own_b, far_b, own_a, far_a, odd_a = call(
            far_near_kernel,
            last[0] + before_z[1],
            [],
            [own_b, far_b, near_b, *red_a.rest, *first_a, *second_a],
            "v" * 9,
            8,
            1_000,
        )
        far_b = swap(far_b, 4, 0)
        r2 = swap(after(leaving, own_a), 0, 2)
        own_a, far_a = call(far_kernel, last[1], [], [own_a, far_a, swap(odd_a, 2, 0)], "vvv", 4, 1_000)
        r2 = after(r2, far_a)
        far_a = swap(far_a, 4, 0)
    else:
        r2 = swap(leaving, 0, 2)
    r3 = swap(r2[2:], 0, 1)
    r1 = [swap(res_1, 0, 1), swap(gi_1, 0, 1)]
    masters = (attn_proj, out_proj, up_proj, down_proj, pos_table, norm_params)
    firsts = (first_attn, first_out, first_up, first_down, first_pos, first_norm)
    seconds = (second_attn, second_out, second_up, second_down, second_pos, second_norm)
    updated = [None] * 6
    token = sds((8, LANES), F32)
    done = jnp.zeros(token.shape, F32)
    if fast:
        which = (2, 3, 1)
        state = [group[i] for group in (masters, firsts, seconds) for i in which]
        new = call(
            functools.partial(rows_update_kernel, which),
            [sds(v.shape, F32) for v in state] + [token],
            [],
            [own_b, far_b, *state],
            "v" * 11,
            8,
            2_000_000_000,
        )
        for i, index in enumerate(which):
            updated[index] = new[i:9:3]
        done = new[9]
    outputs, grad_input, done = call(
        finish_kernel,
        [sds(inputs.shape, BF16), sds(inputs.shape, F32), token],
        [],
        [scal, done, res_k, gi_k, *r1, r2, r3],
        "sv" + "v" * 6,
        8,
        2_000_000_000,
    )
    if fast:
        which = (0, 4, 5)
        state = [group[i] for group in (masters, firsts, seconds) for i in which]
        new = call(
            tiles_update_kernel,
            [sds(v.shape, F32) for v in state],
            [],
            [scal, done, own_a, far_a, *state],
            "sv" + "v" * 11,
            8,
            1_000_000,
        )
        for i, index in enumerate(which):
            updated[index] = new[i::3]
    else:

        def reduced(value, own_axis):
            arrived = lax.all_to_all(value, "dp", split_axis=0, concat_axis=0, tiled=True)
            part = arrived.astype(F32).sum(axis=0).astype(BF16)
            arrived = lax.all_to_all(part, "tensor", split_axis=0, concat_axis=0, tiled=True)
            return arrived.astype(F32).sum(axis=0)

        gup, gdown, gout = got_b
        gattn, gpos = got_a
        gup, gdown, gout, gattn = [jnp.take(v, relative, axis=0) for v in (gup, gdown, gout.reshape(n_t, group, width), gattn)]
        g_up = reduced(gup.reshape(n_t, n_dp, per, inner).swapaxes(0, 1), 0)
        g_down = reduced(gdown.reshape(n_t, n_dp, inner // n_dp, width).swapaxes(0, 1), 0)
        g_out = reduced(gout.reshape(n_t, n_dp, out_per, width).swapaxes(0, 1), 0)
        g_pos = reduced(gpos.reshape(n_t, n_dp, pos_per, width).swapaxes(0, 1), 0)
        g_attn = reduced(gattn.reshape(n_t, n_dp, per, 3, group).swapaxes(0, 1), 0).swapaxes(0, 1)
        cut = gnorm[:4].reshape(4, n_dp, width // n_dp).swapaxes(0, 1).astype(BF16)
        g_norm = reduced(jnp.broadcast_to(cut[:, None], (n_dp, n_t, *cut.shape[1:])), 0)

        gradients = (g_attn, g_out, g_up, g_down, g_pos, g_norm)
        for index in range(6):
            updated[index] = adam_step(masters[index], gradients[index], firsts[index], seconds[index], RATES[index], DECAYS[index])
    return (outputs, grad_input, *[v for new in updated for v in new])


def solution(mesh):
    acts = P("dp", "tensor", None)
    attn = P(None, "dp", "tensor")
    both = P(("tensor", "dp"), None)
    up = P("dp", "tensor")
    norm = P(None, "dp")
    return jax.shard_map(
        body,
        mesh=mesh,
        in_specs=(acts, P("dp", None), acts, attn, both, up, both, both, norm, *(attn,) * 2, *(both,) * 2, *(up,) * 2, *(both,) * 4, *(norm,) * 2),
        out_specs=(acts, acts, *(attn,) * 3, *(both,) * 3, *(up,) * 3, *(both,) * 6, *(norm,) * 3),
        check_vma=False,
    )
```

```python
import functools

import jax
import jax.numpy as jnp
from jax import lax
from jax.experimental import pallas as pl
from jax.experimental.pallas import tpu as pltpu
from jax.sharding import PartitionSpec as P

HD = 64
STEP = 10
LANES = 128

NORM_EPS = 1e-05
NEG_FILL = -1e30
BETA_ONE = 0.9
BETA_TWO = 0.95
ADAM_EPS = 1e-08
RATES = (0.03, 0.2, 0.03, 0.02, 0.3, 0.3)
DECAYS = (0.1, 0.1, 0.1, 0.1, 0.1, 0.0)
GELU_A = 0.7978845608028654
GELU_B = 0.044715

F32 = jnp.float32
BF16 = jnp.bfloat16
AXES = ("dp", "tensor")

NN = (((1,), (0,)), ((), ()))
NT = (((1,), (1,)), ((), ()))
TN = (((0,), (0,)), ((), ()))
QUERIES = 256


def total(*parts):
    return sum(p.astype(F32) for p in parts)


def low(*parts):
    return total(*parts).astype(BF16)


def adam_step(weight, gradient, moment_one, second, step_rate, decay_rate):
    first_new = BETA_ONE * moment_one + (1.0 - BETA_ONE) * gradient
    second_new = BETA_TWO * second + (1.0 - BETA_TWO) * gradient * gradient
    fixed_first = first_new / (1.0 - BETA_ONE**STEP)
    fixed_second = second_new / (1.0 - BETA_TWO**STEP)
    weight_new = weight - step_rate * (fixed_first / (jnp.sqrt(fixed_second) + ADAM_EPS) + decay_rate * weight)
    return (weight_new, first_new, second_new)


def mm(a, b, dims=NN):
    return lax.dot_general(a, b, dims, preferred_element_type=F32)


def swap(value, rd, rt):
    n_t = lax.axis_size("tensor")
    mask = rd * n_t + rt
    return lax.ppermute(value, AXES, [(i, i ^ mask) for i in range(lax.axis_size("dp") * n_t)])


def rows_at(start, size, step):
    return pl.ds(pl.multiple_of(start, step), size)


def by_head(rows):
    lane = lax.broadcasted_iota(jnp.int32, (rows, LANES), 1)

    def keep(h):
        here = (lane >= h * HD) & (lane < (h + 1) * HD)
        return lambda v: jnp.where(here, v, jnp.zeros_like(v))

    return [keep(h) for h in range(LANES // HD)]


def fill_window(me_t, which, parts, out_ref, sems):
    own, rx, c1, c3 = parts
    n = own.shape[1]
    sources = (own.at[me_t], c1.at[which], rx.at[which], c3.at[which])
    copies = [pltpu.make_async_copy(src, out_ref.at[rows_at((me_t ^ r) * n, n, n), :], sems.at[r]) for r, src in enumerate(sources)]
    for copy in copies:
        copy.start()
    return copies


def copies_in(moves, sems):
    copies = [pltpu.make_async_copy(src, dst, sems.at[i]) for i, (src, dst) in enumerate(moves)]
    for copy in copies:
        copy.start()
    return copies


def prepare_kernel(scal, inputs, cot, attn, pos, norm, out, up, down, ga, gb, xs, c1, attn_s, pos_s, norm_s, out_s, up_s, down_s, sems):
    me_t = scal[1]
    moves = [(attn, attn_s), (pos, pos_s), (norm, norm_s), (up, up_s), (down, down_s), (out, out_s)]
    for rel, ref, at in ((2, xs, 0), (3, xs, 2), (1, c1, 0)):
        moves += [(inputs.at[me_t ^ rel], ref.at[at]), (cot.at[me_t ^ rel], ref.at[at + 1])]
    copies = copies_in(moves, sems)
    for copy in copies[:3]:
        copy.wait()
    per = attn.shape[1]
    pos_per = pos.shape[0]
    tiles = pos.shape[1] // LANES
    for t in range(3):
        ga[0, t * per : (t + 1) * per, :] = attn_s[t].astype(BF16)
    for k in range(tiles):
        at = 3 * per + k * pos_per
        ga[0, at : at + pos_per, :] = pos_s[:, k * LANES : (k + 1) * LANES].astype(BF16)
    at = 3 * per + tiles * pos_per
    both = norm_s[...]
    both = jnp.concatenate([both, both], axis=1)
    both = jnp.concatenate([both, jnp.zeros_like(both)], axis=0)
    high = both.astype(BF16)
    rest = (both - high.astype(F32)).astype(BF16)
    ga[0, at : at + 16, :] = jnp.concatenate([high, rest], axis=0)
    for copy in copies[3:6]:
        copy.wait()
    gb[0, 0:per, :] = up_s[...].astype(BF16)
    gb[0, per : 2 * per, :] = down_s[...].astype(BF16)
    gb[0, 2 * per :, :] = out_s[...].astype(BF16)
    for copy in copies[6:]:
        copy.wait()


def stack_kernel(own, got, both):
    n = own.shape[0]
    both[:n] = own[...]
    both[n:] = got[...]


def attention_kernel(places, n_pieces, scal, *refs):
    own, rx, c1, c3, segs = refs[:5]
    pieces = refs[5 : 5 + n_pieces]
    hid_o, qkv_h, pt_h, mix_o, w_h, nrm_o, x_s, pos_s, bias_s, nrm_s, w_o, qkv_o, pt_o, sems, out_sems = refs[5 + n_pieces :]
    leaving = []

    def leave(src, dst):
        leaving.append(pltpu.make_async_copy(src, dst, out_sems.at[len(leaving)]))
        leaving[-1].start()

    me_dp, me_t = scal[0], scal[1]
    win, width = x_s.shape
    groups = w_o.shape[1] // (3 * LANES)
    filling = fill_window(me_t, 0, (own, rx, c1, c3), x_s, sems)
    if places is None:
        w_o[...] = pieces[0][...]
        pos_s[...] = pieces[1][...]
        nrm_o[...] = pieces[2][...]
    else:
        n_dp = nrm_s.shape[0]
        per = width // n_dp
        pos_per = win // (n_dp * groups)
        for ref, (xr, yr, zs, c) in zip(pieces, places, strict=True):
            tr = xr * 2 + c
            for i, zr in enumerate(zs):
                src = me_dp ^ (zr * 2 + yr)
                for t in range(3):
                    at = (tr * 3 + t) * LANES
                    w_o[rows_at(src * per, per, per), at : at + LANES] = ref[i, t * per : (t + 1) * per]
                where = (me_t ^ tr) * (win // groups) + src * pos_per
                for k in range(width // LANES):
                    at = 3 * per + k * pos_per
                    pos_s[rows_at(where, pos_per, pos_per), k * LANES : (k + 1) * LANES] = ref[i, at : at + pos_per]
                if tr == 0:
                    at = 3 * per + width // LANES * pos_per
                    nrm_s[src] = ref[i, at : at + 16].astype(F32)
        low_lane = lax.broadcasted_iota(jnp.int32, (8, LANES), 1) < per
        for j in range(n_dp // 2):
            left = nrm_s[2 * j]
            right = nrm_s[2 * j + 1]
            both = jnp.where(low_lane, left[0:8] + left[8:16], right[0:8] + right[8:16])
            nrm_o[:, j * LANES : (j + 1) * LANES] = both

    leave(w_o, w_h)

    seg = segs[pl.ds(me_t, 1), :].astype(F32)
    seg_col = jnp.transpose(jnp.broadcast_to(seg, (LANES, win)))
    for i in range(win // LANES):
        key_seg = seg_col[i * LANES : (i + 1) * LANES, 0:1]
        key_at = lax.broadcasted_iota(jnp.int32, (LANES, win), 0) + i * LANES
        query_at = lax.broadcasted_iota(jnp.int32, (LANES, win), 1)
        counts = (key_seg == seg) & (query_at >= key_at)
        bias_s[i * LANES : (i + 1) * LANES, :] = jnp.where(counts, 0.0, NEG_FILL)

    for copy in filling:
        copy.wait()
    hidden = x_s[...].astype(F32) + pos_s[...].astype(F32)
    hid_o[...] = hidden
    x_s[...] = hidden.astype(BF16)
    heads = by_head(win)
    for g in range(groups):
        at = g * 3 * LANES
        qkv = mm(x_s[...], w_o[:, at : at + 3 * LANES]).astype(BF16)
        q = qkv[:, :LANES] * jnp.asarray(HD**-0.5, BF16)
        k = qkv[:, LANES : 2 * LANES]
        v = qkv[:, 2 * LANES :]
        qkv_o[:, at : at + LANES] = q
        qkv_o[:, at + LANES : at + 3 * LANES] = qkv[:, LANES:]
        for j in range(win // QUERIES):
            ext = (j + 1) * QUERIES
            cols = slice(j * QUERIES, ext)
            mixed = jnp.zeros((QUERIES, LANES), F32)
            for h, only in enumerate(heads):
                s = mm(only(k)[:ext], q[cols], NT) + bias_s[:ext, cols]
                e = jnp.exp(s - jnp.max(s, axis=0, keepdims=True))
                p = (e * (1.0 / jnp.sum(e, axis=0, keepdims=True))).astype(BF16)
                pt_o[len(heads) * g + h, :ext, cols] = p
                mixed += mm(p, only(v)[:ext], TN)
            mix_o[cols, g * LANES : (g + 1) * LANES] = mixed.astype(BF16)
            for h in range(len(heads)):
                leave(pt_o.at[len(heads) * g + h, :ext, cols], pt_h.at[len(heads) * g + h, :ext, cols])
    leave(qkv_o, qkv_h)
    for copy in leaving:
        copy.wait()


def norm_forward(v):
    center = v - jnp.mean(v, axis=-1, keepdims=True)
    rs = lax.rsqrt(jnp.mean(center * center, axis=-1, keepdims=True) + NORM_EPS)
    return center * rs, rs


def norm_backward(g, xhat, rs, gain):
    e = g * gain
    return rs * (e - jnp.mean(e, axis=-1, keepdims=True) - xhat * jnp.mean(e * xhat, axis=-1, keepdims=True))


def put_blocks(me_t, value, keep, s1, sx):
    n = keep.shape[0]
    for r, ref in ((0, keep), (1, s1.at[0]), (2, sx.at[0]), (3, sx.at[1])):
        ref[...] = value[rows_at((me_t ^ r) * n, n, n), :].astype(ref.dtype)


CHUNK = 128


def chunk_of(refs, tr, r):
    c, xr, yr, zr = tr & 1, tr >> 1, r & 1, r >> 1
    half = refs[0].shape[0] // 4
    if zr < half:
        first, slot = xr == 1, yr * half + zr
    else:
        first, slot = yr == 1, 2 * half + xr * half + zr - half
    return refs[2 * c + (0 if first else 1)], slot


def ffn_kernel(places, n_pieces, scal, *refs):
    own, rx, c1, c3, hid, mixed, nrm = refs[:7]
    pieces = refs[7 : 7 + n_pieces]
    rest = refs[7 + n_pieces :]
    res_k, res_1, res_x, gone_o, gm_o, gnorm_o = rest[:6]
    if places is None:
        gup_o, gdown_o, gout_o = rest[6:9]
        rest = rest[9:]
    else:
        chunks_o = rest[6:10]
        rest = rest[10:]
    cot_s, out_s, up_s, down_s, a_s, b_s, g_s, xh1_s, r1_s, n1_s, sent_s, act_s, dg_s, low_s, xt_s, sems = rest
    me_dp, me_t = scal[0], scal[1]
    win, width = hid.shape
    groups = up_s.shape[0]
    filling = fill_window(me_t, 1, (own, rx, c1, c3), cot_s, sems)
    if places is None:
        n_dp = 1
        for src, dst in zip(pieces, (out_s, up_s, down_s), strict=True):
            dst[...] = src[...]
    else:
        n_dp = 2 * sum(len(zs) for _, yr, zs, c in places if yr == 0 and c == 0) // 2
        per = width // n_dp
        out_per = LANES // n_dp
        for ref, (xr, yr, zs, c) in zip(pieces, places, strict=True):
            tr = xr * 2 + c
            for i, zr in enumerate(zs):
                src = me_dp ^ (zr * 2 + yr)
                up_s[tr, rows_at(src * per, per, per), :] = ref[i, 0:per]
                down_s[tr, rows_at(src * per, per, per), :] = ref[i, per : 2 * per]
                out_s[rows_at(tr * LANES + src * out_per, out_per, out_per), :] = ref[i, 2 * per : 2 * per + out_per]

    def chunks(fn):
        for i in range(win // CHUNK):
            fn(slice(i * CHUNK, (i + 1) * CHUNK))

    a_s[0] = mm(mixed[...], out_s[...])

    def norm_one(at):
        xhat, rs = norm_forward(hid[at, :] + a_s[0, at, :])
        xh1_s[at, :] = xhat
        r1_s[at, :] = jnp.broadcast_to(rs, (CHUNK, LANES))
        normed = xhat * nrm[0:1, :] + nrm[1:2, :]
        n1_s[at, :] = normed
        sent_s[at, :] = normed.astype(BF16)

    chunks(norm_one)

    for g in range(groups):
        a_s[g % 2] = mm(sent_s[...], up_s[g])

        def gelu(at, g=g):
            v = a_s[g % 2, at, :]
            square = v * v
            half = 0.5 + 0.5 * jnp.tanh(v * (GELU_A + GELU_A * GELU_B * square))
            act_s[g, at, :] = (v * half).astype(BF16)
            dg_s[g, at, :] = half + (half - half * half) * (v * (2.0 * GELU_A + 6.0 * GELU_A * GELU_B * square))

        chunks(gelu)
        n1_s[...] += mm(act_s[g], down_s[g])

    for copy in filling:
        copy.wait()

    def norm_two(i, sums):
        at = slice(i * CHUNK, (i + 1) * CHUNK)
        xhat, rs = norm_forward(n1_s[at, :])
        n1_s[at, :] = xhat * nrm[2:3, :] + nrm[3:4, :]
        g = cot_s[at, :].astype(F32)
        grad = norm_backward(g, xhat, rs, nrm[2:3, :])
        b_s[at, :] = grad
        low_s[at, :] = grad.astype(BF16)
        return (sums[0] + jnp.sum((g * xhat).reshape(-1, 8, width), axis=0), sums[1] + jnp.sum(g.reshape(-1, 8, width), axis=0))

    def every(step):
        sums = (jnp.zeros((8, width), F32),) * 2
        for i in range(win // CHUNK):
            sums = step(i, sums)
        return sums

    gain_two, shift_two = every(norm_two)
    put_blocks(me_t, n1_s, res_k, res_1, res_x)

    def put(g, first, height, source, base):
        for r in range(n_dp):
            ref, slot = chunk_of(chunks_o, g, r)
            ref[slot, first : first + height, :] = source[rows_at(base + (r ^ me_dp) * height, height, height), :]

    xt_s[...] = jnp.transpose(sent_s[...])
    for g in range(groups):
        gdown = mm(jnp.transpose(act_s[g]), low_s[...])
        if places is None:
            gdown_o[g] = gdown.astype(BF16)
        else:
            g_s[0] = gdown.astype(BF16)
            put(g, per, per, g_s.at[0], 0)
        act_s[g] = (mm(low_s[...], down_s[g], NT) * dg_s[g]).astype(BF16)
        gup = mm(xt_s[...], act_s[g])
        if places is None:
            gup_o[g] = gup.astype(BF16)
        else:
            g_s[1] = gup.astype(BF16)
            put(g, 0, per, g_s.at[1], 0)
        b_s[...] += mm(act_s[g], up_s[g], NT)

    def norm_one_back(i, sums):
        at = slice(i * CHUNK, (i + 1) * CHUNK)
        g = b_s[at, :]
        xhat = xh1_s[at, :]
        grad = norm_backward(g, xhat, r1_s[at, 0:1], nrm[0:1, :])
        gone_o[at, :] = grad
        low_s[at, :] = grad.astype(BF16)
        return (sums[0] + jnp.sum((g * xhat).reshape(-1, 8, width), axis=0), sums[1] + jnp.sum(g.reshape(-1, 8, width), axis=0))

    gain_one, shift_one = every(norm_one_back)
    for k, total in enumerate((gain_one, shift_one, gain_two, shift_two)):
        gnorm_o[k : k + 1, :] = jnp.sum(total, axis=0, keepdims=True)
    gnorm_o[4:8, :] = jnp.zeros((4, width), F32)

    gout = mm(jnp.transpose(mixed[...]), low_s[...])
    if places is None:
        gout_o[...] = gout.astype(BF16)
    else:
        g_s[0] = gout.astype(BF16)
        for g in range(groups):
            put(g, 2 * per, out_per, g_s.at[0], g * LANES)
    gm = mm(low_s[...], out_s[...], NT).astype(BF16)
    for g in range(groups):
        gm_o[g] = gm[:, g * LANES : (g + 1) * LANES]


def attention_back_kernel(fast, scal, hid, qkv_h, pt_h, gm, w_h, gone, gnorm, *rest):
    gi_k, gi_1, gi_x = rest[:3]
    if fast:
        chunks_o = rest[3:7]
        rest = rest[7:]
    else:
        gattn_o, gpos_o = rest[3:5]
        rest = rest[5:]
    ht_s, ds_s, dqkv_s, acc_s, g_s, qkv, pt, w, sems = rest
    me_dp, me_t = scal[0], scal[1]
    win, width = hid.shape
    groups = w.shape[1] // (3 * LANES)
    heads = by_head(win)
    arriving = [pltpu.make_async_copy(qkv_h, qkv, sems.at[0])]
    for n in range(pt.shape[0]):
        for j in range(win // QUERIES):
            ext = (j + 1) * QUERIES
            cols = slice(j * QUERIES, ext)
            arriving.append(pltpu.make_async_copy(pt_h.at[n, :ext, cols], pt.at[n, :ext, cols], sems.at[len(arriving)]))
    arriving.append(pltpu.make_async_copy(w_h, w, sems.at[len(arriving)]))
    for copy in arriving:
        copy.start()
    ht_s[...] = jnp.transpose(hid[...].astype(BF16))
    for g in range(groups):
        at = g * 3 * LANES
        if g == 0:
            arriving[0].wait()
        per_group = len(heads) * (win // QUERIES)
        for copy in arriving[1 + g * per_group : 1 + (g + 1) * per_group]:
            copy.wait()
        q = qkv[:, at : at + LANES]
        k = qkv[:, at + LANES : at + 2 * LANES]
        v = qkv[:, at + 2 * LANES : at + 3 * LANES]
        d_mixed = gm[g]
        for j in range(win // QUERIES):
            ext = (j + 1) * QUERIES
            cols = slice(j * QUERIES, ext)
            dq = jnp.zeros((QUERIES, LANES), F32)
            for h, only in enumerate(heads):
                p = pt[len(heads) * g + h, :ext, cols].astype(F32)
                dp = mm(v[:ext], only(d_mixed)[cols], NT)
                ds = (p * (dp - jnp.sum(p * dp, axis=0, keepdims=True))).astype(BF16)
                ds_s[len(heads) * g + h, :ext, cols] = ds
                dq += mm(ds, only(k)[:ext], TN)
            dqkv_s[cols, at : at + LANES] = (dq * HD**-0.5).astype(BF16)
        for i in range(win // QUERIES):
            rows = slice(i * QUERIES, (i + 1) * QUERIES)
            dk = jnp.zeros((QUERIES, LANES), F32)
            dv = jnp.zeros((QUERIES, LANES), F32)
            for h, only in enumerate(heads):
                dk += mm(ds_s[len(heads) * g + h, rows, i * QUERIES :], only(q)[i * QUERIES :])
                dv += mm(pt[len(heads) * g + h, rows, i * QUERIES :], only(d_mixed)[i * QUERIES :])
            dqkv_s[rows, at + LANES : at + 2 * LANES] = dk.astype(BF16)
            dqkv_s[rows, at + 2 * LANES : at + 3 * LANES] = dv.astype(BF16)
    arriving[-1].wait()
    acc_s[...] = gone[...] + mm(dqkv_s[...], w[...], NT)

    put_blocks(me_t, acc_s, gi_k, gi_1, gi_x)
    if not fast:
        for g in range(groups):
            gattn_o[g] = mm(ht_s[...], dqkv_s[:, g * 3 * LANES : (g + 1) * 3 * LANES]).astype(BF16)
        gpos_o[...] = acc_s[...].astype(BF16)
        return
    n_dp = chunks_o[0].shape[0]
    per = width // n_dp
    pos_per = win // (n_dp * groups)
    for g in range(groups):
        g_s[g % 2] = mm(ht_s[...], dqkv_s[:, g * 3 * LANES : (g + 1) * 3 * LANES]).astype(BF16)
        for r in range(n_dp):
            d = r ^ me_dp
            ref, slot = chunk_of(chunks_o, g, r)
            for t in range(3):
                ref[slot, t * per : (t + 1) * per, :] = g_s[g % 2, rows_at(d * per, per, per), t * LANES : (t + 1) * LANES]
            where = (me_t ^ g) * (win // groups) + d * pos_per
            for k in range(width // LANES):
                at = 3 * per + k * pos_per
                ref[slot, at : at + pos_per, :] = acc_s[rows_at(where, pos_per, pos_per), k * LANES : (k + 1) * LANES].astype(BF16)
            at = 3 * per + width // LANES * pos_per
            tile = gnorm[0:8, rows_at((d >> 1) * LANES, LANES, LANES)]
            ref[slot, at : at + 16, :] = jnp.concatenate([tile, tile], axis=0).astype(BF16)


def near_kernel(rest, got, x, y, x2, y2, own, far, odd):
    own[...] = total(rest[0], got[0], x[0], x2[0])
    far[...] = total(rest[4], got[4], y[0], y2[0])
    odd[0] = low(rest[1], got[1], x[1], x2[1])
    odd[1] = low(rest[5], got[5], y[1], y2[1])


def second_kernel(done, rest, got, x, y, a, b):
    del done
    for i in range(2):
        a[i] = low(rest[2 + i], got[2 + i], x[2 + i])
        b[i] = low(rest[6 + i], got[6 + i], y[2 + i])


def far_kernel(own, far, near, own_o, far_o):
    own_o[...] = total(own[...], near[0])
    far_o[0] = low(far[...], near[1])


def far_near_kernel(own, far, near, rest, got, x, y, x2, y2, own_o, far_o, *others):
    far_kernel(own, far, near, own_o, far_o)
    near_kernel(rest, got, x, y, x2, y2, *others)


def update(refs, gradient, rate, decay):
    weight, one, two, new_weight, new_one, new_two = refs
    new_weight[...], new_one[...], new_two[...] = adam_step(weight[...], gradient, one[...], two[...], rate, decay)


def rows_update_kernel(which, own, far, *refs):
    n = len(which)
    *refs, token = refs
    token[...] = jnp.zeros_like(token)
    grad = total(own[...], far[0])
    at = 0
    for i, index in enumerate(which):
        height = refs[i].shape[0]
        update(refs[i :: n], grad[at : at + height], RATES[index], DECAYS[index])
        at += height


def tiles_update_kernel(scal, done, own, far, *refs):
    *refs, token = refs
    token[...] = done[...]
    attn, pos, norm = refs[0::3], refs[1::3], refs[2::3]
    grad = total(own[...], far[0])
    per = attn[0].shape[1]
    pos_per, width = pos[0].shape
    update(attn, grad[: 3 * per].reshape(attn[0].shape), RATES[0], DECAYS[0])
    at = 3 * per
    rows = [grad[at + k * pos_per : at + (k + 1) * pos_per] for k in range(width // LANES)]
    update(pos, jnp.concatenate(rows, axis=1), RATES[4], DECAYS[4])
    at += width // LANES * pos_per
    tile = grad[at : at + 8]
    half = jnp.where((scal[0] & 1) == 1, tile[:4, LANES // 2 :], tile[:4, : LANES // 2])
    update(norm, half, RATES[5], DECAYS[5])


def finish_kernel(scal, done, res_k, gi_k, res_1, gi_1, r2, r3, res_o, gi_o):
    del done
    me_t = scal[1]
    for r, (res, gi) in enumerate(((res_k[...], gi_k[...]), (res_1[0], gi_1[0]), (r2[0], r2[1]), (r3[0], r3[1]))):
        res_o[me_t ^ r] = res
        gi_o[me_t ^ r] = gi.astype(F32)


def after(value, *others):
    return lax.optimization_barrier((value, *others))[0]


def gather_z(value, *others):
    nz = lax.axis_size("dp") // 2
    q, order = value, [0]
    step = nz // 2
    while step:
        if step == 1:
            q = after(q, *others)
        out = jax.ShapeDtypeStruct((2 * q.shape[0], *q.shape[1:]), q.dtype)
        q = call(stack_kernel, [out], [], [q, swap(q, step * 2, 0)], "vv", 6, 1_000)[0]
        order = order + [z ^ step for z in order]
        step //= 2
    return q, tuple(order)


def gather_xy(q, order, qx=None, qy=None, *others):
    half = len(order) // 2
    if qx is None:
        qx, qy = swap(q, 0, 2), swap(q, 1, 0)
    a, b = after(qx[:half], *others), after(qy[half:], *others)
    return [(q, (0, 0, order)), (qx, (1, 0, order)), (qy, (0, 1, order)), (swap(a, 1, 0), (1, 1, order[:half])), (swap(b, 0, 2), (1, 1, order[half:]))]


def both_cores(found):
    out = []
    for array, place in found:
        out.append((array, (*place, 0)))
        out.append((swap(array, 0, 1), (*place, 1)))
    return [f[0] for f in out], tuple(f[1] for f in out)


class Reduction:
    def __init__(self, keep_first, keep_rest, send_first, send_rest):
        self.half = keep_first.shape[0] // 4
        self.n = keep_first.shape[0] // 2
        self.sums = [(keep_rest,)]
        self.send_rest = send_rest
        got = swap(send_first, 0, 1)
        self.a = low(keep_first[: self.n], got[: self.n])
        self.b = low(keep_first[self.n :], got[self.n :])

    def terms(self, a, start, stop):
        at = 0 if a else self.n
        found = [k[at + start : at + stop] for k in self.rest]
        for pair in self.got:
            g = pair[0 if a else 1]
            if g.shape[0] >= stop:
                found.append(g[start:stop])
        return found

    def first(self):
        self.rest = [self.sums[0][0], swap(self.send_rest, 0, 1)]
        self.got = [(swap(self.a, 0, 2), swap(self.b, 1, 0))]
        return self.got[0]

    def second(self, *others):
        h = self.half
        a, b = [after(low(*self.terms(part, h, 2 * h)), *others) for part in (True, False)]
        self.got.append((swap(a, 1, 0), swap(b, 0, 2)))
        return self.got[1]

    def over_z(self, *others):
        h = self.half
        arrived = []
        for z in range(1, 2 * h):
            chunk = low(*self.terms(z < h, z % h, z % h + 1))
            arrived.append(swap(after(chunk, *others), 2 * z, 0))
        return arrived

    def result(self, arrived):
        return total(*self.terms(True, 0, 1), *arrived)[0]


def call(kernel, outs, scratch, args, spaces, mib, flops):
    vmem = pl.BlockSpec(memory_space=pltpu.VMEM)
    args = [pltpu.with_memory_space_constraint(v, pltpu.HBM) if k == "h" else v for v, k in zip(args, spaces, strict=True)]
    kinds = {"s": pl.BlockSpec(memory_space=pltpu.SMEM), "v": vmem, "a": pl.BlockSpec(memory_space=pl.ANY), "h": pl.BlockSpec(memory_space=pltpu.HBM)}
    return pl.pallas_call(
        kernel,
        out_shape=outs,
        in_specs=[kinds[k] for k in spaces],
        out_specs=[vmem if isinstance(v, jax.ShapeDtypeStruct) else kinds["h"] for v in outs],
        scratch_shapes=[pltpu.VMEM(*s) if isinstance(s, tuple) else pltpu.SemaphoreType.DMA(tuple(s)) for s in scratch],
        compiler_params=pltpu.CompilerParams(vmem_limit_bytes=mib * 1024 * 1024),
        cost_estimate=pl.CostEstimate(flops=flops, bytes_accessed=0, transcendentals=0),
    )(*args)


def body(
    inputs,
    segment_ids,
    cotangent,
    attn_proj,
    out_proj,
    up_proj,
    down_proj,
    pos_table,
    norm_params,
    first_attn,
    second_attn,
    first_out,
    second_out,
    first_up,
    second_up,
    first_down,
    second_down,
    first_pos,
    second_pos,
    first_norm,
    second_norm,
):
    n_dp, n_t = lax.axis_size("dp"), lax.axis_size("tensor")
    me_dp, me_t = lax.axis_index("dp"), lax.axis_index("tensor")
    scal = jnp.stack([me_dp, me_t]).astype(jnp.int32)
    windows, block, width = inputs.shape
    win = block * n_t
    inner = up_proj.shape[1]
    group = attn_proj.shape[2]
    per, out_per, pos_per = attn_proj.shape[1], out_proj.shape[0], pos_table.shape[0]
    fast = out_per % 16 == 0 and pos_per % 16 == 0 and 2 * per == LANES
    sds = jax.ShapeDtypeStruct

    if fast:
        ga, gb, xs, c1 = call(
            prepare_kernel,
            [
                sds((1, 3 * per + width // LANES * pos_per + 16, LANES), BF16),
                sds((1, 2 * per + out_per, width), BF16),
                sds((4, block, width), BF16),
                sds((2, block, width), BF16),
            ],
            [(v.shape, F32) for v in (attn_proj, pos_table, norm_params, out_proj, up_proj, down_proj)] + [[12]],
            [scal, inputs, cotangent, attn_proj, pos_table, norm_params, out_proj, up_proj, down_proj],
            "s" + "h" * 8,
            8,
            1_000,
        )
        qa, za = gather_z(ga)
        rx = swap(xs, 0, 2)
        qb, zb = gather_z(gb, qa)
        c1 = swap(c1, 0, 1)
        c3 = swap(rx[2:], 0, 1)
        qax, qay, qaxy = swap(qa, 0, 2), swap(qa, 1, 0), swap(qa, 1, 2)
        a_args, a_places = both_cores([(qa, (0, 0, za)), (qax, (1, 0, za)), (qay, (0, 1, za)), (qaxy, (1, 1, za))])
        qb = after(qb, rx, qax, qay)
        qbx, qby = swap(qb, 0, 2), swap(qb, 1, 0)
    else:

        def pair(rel):
            return jnp.concatenate([lax.dynamic_slice_in_dim(v, me_t ^ rel, 1, 0) for v in (inputs, cotangent)])

        rx = swap(jnp.concatenate([pair(2), pair(3)]), 0, 2)
        c1 = swap(pair(1), 0, 1)
        c3 = swap(rx[2:], 0, 1)
        relative = me_t ^ jnp.arange(n_t)
        whole = [lax.all_gather(lax.all_gather(v.astype(BF16), "dp"), "tensor") for v in (attn_proj, out_proj, up_proj, down_proj)]
        attn_w, out_w, up_w, down_w = [jnp.take(v, relative, axis=0) for v in whole]
        attn_w = attn_w.transpose(1, 3, 0, 2, 4).reshape(width, n_t * 3 * group)
        pos_w = lax.all_gather(lax.all_gather(pos_table.astype(BF16), "dp", axis=0, tiled=True), "tensor", axis=0, tiled=True)
        norm_w = lax.all_gather(norm_params, "dp", axis=1, tiled=True)
        norm_w = jnp.concatenate([norm_w, jnp.zeros_like(norm_w)])
        a_args, a_places = [attn_w, pos_w, norm_w], None
        b_args, b_places = [out_w.reshape(n_t * group, width), up_w.reshape(n_t, width, inner), down_w.reshape(n_t, inner, width)], None

    hid, qkv, pt, mixed, attn_all, norm_all = call(
        functools.partial(attention_kernel, a_places, len(a_args)),
        [
            sds((win, width), F32),
            pltpu.HBM((win, n_t * 3 * group), BF16),
            pltpu.HBM((n_t * group // HD, win, win), BF16),
            sds((win, n_t * group), BF16),
            pltpu.HBM((width, n_t * 3 * group), BF16),
            sds((8, width), F32),
        ],
        [((win, width), BF16), ((win, width), BF16), ((win, win), F32), ((n_dp, 16, LANES), F32), ((width, n_t * 3 * group), BF16), ((win, n_t * 3 * group), BF16), ((n_t * group // HD, win, win), BF16), [4], [32]],
        [scal, inputs, rx, c1, c3, segment_ids, *a_args],
        "shaaav" + "v" * len(a_args),
        14,
        1_000_000,
    )
    if fast:
        b_args, b_places = both_cores(gather_xy(qb, zb, qbx, qby, hid))

    blocks = [sds((block, width), BF16), sds((1, block, width), BF16), sds((2, block, width), BF16)]
    if fast:
        rows_b = 2 * per + out_per
        grads_b = [sds((n_dp, rows_b, width), BF16)] * 4
    else:
        grads_b = [sds((n_t, width, inner), BF16), sds((n_t, inner, width), BF16), sds((n_t * group, width), BF16)]
    res_k, res_1, res_x, gone, gm, gnorm, *got_b = call(
        functools.partial(ffn_kernel, b_places, len(b_args)),
        [*blocks, sds((win, width), F32), sds((n_t, win, group), BF16), sds((8, width), F32), *grads_b],
        [
            ((win, width), BF16),
            ((n_t * group, width), BF16),
            ((n_t, width, inner), BF16),
            ((n_t, inner, width), BF16),
            ((2, win, width), F32),
            ((win, width), F32),
            ((2, win, width), BF16),
            ((win, width), F32),
            ((win, LANES), F32),
            ((win, width), F32),
            ((win, width), BF16),
            ((n_t, win, inner), BF16),
            ((n_t, win, inner), F32),
            ((win, width), BF16),
            ((width, win), BF16),
            [4],
        ],
        [scal, cotangent, rx, c1, c3, hid, mixed, norm_all, *b_args],
        "shaaavvv" + "v" * len(b_args),
        22,
        1_000_000,
    )
    if fast:
        red_b = Reduction(*got_b)
        gone = after(gone, red_b.a, red_b.b)
        first_b = red_b.first()

    blocks = [sds((block, width), F32), *blocks[1:]]
    if fast:
        rows_a = 3 * per + width // LANES * pos_per + 16
        grads_a = [sds((n_dp, rows_a, LANES), BF16)] * 4
    else:
        grads_a = [sds((n_t, width, 3 * group), BF16), sds((win, width), BF16)]
    gi_k, gi_1, gi_x, *got_a = call(
        functools.partial(attention_back_kernel, fast),
        [*blocks, *grads_a],
        [
            ((width, win), BF16),
            ((n_t * group // HD, win, win), BF16),
            ((win, n_t * 3 * group), BF16),
            ((win, width), F32),
            ((2, width, 3 * group), BF16),
            ((win, n_t * 3 * group), BF16),
            ((n_t * group // HD, win, win), BF16),
            ((width, n_t * 3 * group), BF16),
            [2 + 2 * n_t * group // HD],
        ],
        [scal, hid, qkv, pt, gm, attn_all, gone, gnorm],
        "svhhvhvv",
        18,
        1_000_000,
    )
    leaving = [jnp.concatenate([res_x[i : i + 1], gi_x[i : i + 1]]) for i in range(2)]
    if fast:
        keep_first, keep_rest, send_first, send_rest = got_a
        red_a = Reduction(keep_first, keep_rest, after(send_first, *first_b), send_rest)
        first_a, second_b = red_a.first(), red_b.second()
        chunk_b, chunk_a = got_b[0].shape[1:], got_a[0].shape[1:]
        before_z = [[sds(chunk, F32), sds(chunk, F32), sds((2, *chunk), BF16)] for chunk in (chunk_b, chunk_a)]
        last = [[sds(chunk, F32), sds((1, *chunk), BF16)] for chunk in (chunk_b, chunk_a)]
        own_b, far_b, odd_b = call(near_kernel, before_z[0], [], [*red_b.rest, *first_b, *second_b], "v" * 6, 8, 1_000)
        a_y, a_x = call(second_kernel, [sds((2, *chunk_a), BF16)] * 2, [], [own_b, *red_a.rest, *first_a], "avvvv", 8, 1_000)
        second_a = swap(a_y, 1, 0), swap(a_x, 0, 2)
        near_b = swap(odd_b, 2, 0)
        own_b, far_b, own_a, far_a, odd_a = call(
            far_near_kernel,
            last[0] + before_z[1],
            [],
            [own_b, far_b, near_b, *red_a.rest, *first_a, *second_a],
            "v" * 9,
            8,
            1_000,
        )
        far_b = swap(far_b, 4, 0)
        r2, r3 = [swap(after(v, own_a), 0, m) for v, m in zip(leaving, (2, 3), strict=True)]
        own_a, far_a = call(far_kernel, last[1], [], [own_a, far_a, swap(odd_a, 2, 0)], "vvv", 4, 1_000)
        far_a = swap(far_a, 4, 0)
    else:
        r2, r3 = [swap(v, 0, m) for v, m in zip(leaving, (2, 3), strict=True)]
    r1 = [swap(res_1, 0, 1), swap(gi_1, 0, 1)]
    masters = (attn_proj, out_proj, up_proj, down_proj, pos_table, norm_params)
    firsts = (first_attn, first_out, first_up, first_down, first_pos, first_norm)
    seconds = (second_attn, second_out, second_up, second_down, second_pos, second_norm)
    updated = [None] * 6
    token = sds((8, LANES), F32)
    done = jnp.zeros(token.shape, F32)
    if fast:
        which = (2, 3, 1)
        state = [group[i] for group in (masters, firsts, seconds) for i in which]
        new = call(
            functools.partial(rows_update_kernel, which),
            [sds(v.shape, F32) for v in state] + [token],
            [],
            [own_b, far_b, *state],
            "v" * 11,
            8,
            2_000_000_000,
        )
        for i, index in enumerate(which):
            updated[index] = new[i:9:3]
        done = new[9]
    if fast:
        which = (0, 4, 5)
        state = [group[i] for group in (masters, firsts, seconds) for i in which]
        new = call(
            tiles_update_kernel,
            [sds(v.shape, F32) for v in state] + [token],
            [],
            [scal, done, own_a, far_a, *state],
            "sv" + "v" * 11,
            8,
            1_000_000,
        )
        for i, index in enumerate(which):
            updated[index] = new[i:9:3]
        done = new[9]
    outputs, grad_input = call(
        finish_kernel,
        [sds(inputs.shape, BF16), sds(inputs.shape, F32)],
        [],
        [scal, done, res_k, gi_k, *r1, r2, r3],
        "sv" + "v" * 6,
        8,
        1_000,
    )
    if not fast:

        def reduced(value, own_axis):
            arrived = lax.all_to_all(value, "dp", split_axis=0, concat_axis=0, tiled=True)
            part = arrived.astype(F32).sum(axis=0).astype(BF16)
            arrived = lax.all_to_all(part, "tensor", split_axis=0, concat_axis=0, tiled=True)
            return arrived.astype(F32).sum(axis=0)

        gup, gdown, gout = got_b
        gattn, gpos = got_a
        gup, gdown, gout, gattn = [jnp.take(v, relative, axis=0) for v in (gup, gdown, gout.reshape(n_t, group, width), gattn)]
        g_up = reduced(gup.reshape(n_t, n_dp, per, inner).swapaxes(0, 1), 0)
        g_down = reduced(gdown.reshape(n_t, n_dp, inner // n_dp, width).swapaxes(0, 1), 0)
        g_out = reduced(gout.reshape(n_t, n_dp, out_per, width).swapaxes(0, 1), 0)
        g_pos = reduced(gpos.reshape(n_t, n_dp, pos_per, width).swapaxes(0, 1), 0)
        g_attn = reduced(gattn.reshape(n_t, n_dp, per, 3, group).swapaxes(0, 1), 0).swapaxes(0, 1)
        cut = gnorm[:4].reshape(4, n_dp, width // n_dp).swapaxes(0, 1).astype(BF16)
        g_norm = reduced(jnp.broadcast_to(cut[:, None], (n_dp, n_t, *cut.shape[1:])), 0)

        gradients = (g_attn, g_out, g_up, g_down, g_pos, g_norm)
        for index in range(6):
            updated[index] = adam_step(masters[index], gradients[index], firsts[index], seconds[index], RATES[index], DECAYS[index])
    return (outputs, grad_input, *[v for new in updated for v in new])


def solution(mesh):
    acts = P("dp", "tensor", None)
    attn = P(None, "dp", "tensor")
    both = P(("tensor", "dp"), None)
    up = P("dp", "tensor")
    norm = P(None, "dp")
    return jax.shard_map(
        body,
        mesh=mesh,
        in_specs=(acts, P("dp", None), acts, attn, both, up, both, both, norm, *(attn,) * 2, *(both,) * 2, *(up,) * 2, *(both,) * 4, *(norm,) * 2),
        out_specs=(acts, acts, *(attn,) * 3, *(both,) * 3, *(up,) * 3, *(both,) * 6, *(norm,) * 3),
        check_vma=False,
    )
```

```python
import functools

import jax
import jax.numpy as jnp
from jax import lax
from jax.experimental import pallas as pl
from jax.experimental.pallas import tpu as pltpu
from jax.sharding import PartitionSpec as P

HD = 64
STEP = 10
LANES = 128

NORM_EPS = 1e-05
NEG_FILL = -1e30
BETA_ONE = 0.9
BETA_TWO = 0.95
ADAM_EPS = 1e-08
RATES = (0.03, 0.2, 0.03, 0.02, 0.3, 0.3)
DECAYS = (0.1, 0.1, 0.1, 0.1, 0.1, 0.0)
GELU_A = 0.7978845608028654
GELU_B = 0.044715

F32 = jnp.float32
BF16 = jnp.bfloat16
AXES = ("dp", "tensor")

NN = (((1,), (0,)), ((), ()))
NT = (((1,), (1,)), ((), ()))
TN = (((0,), (0,)), ((), ()))
QUERIES = 256


def total(*parts):
    return sum(p.astype(F32) for p in parts)


def low(*parts):
    return total(*parts).astype(BF16)


def adam_step(weight, gradient, moment_one, second, step_rate, decay_rate):
    first_new = BETA_ONE * moment_one + (1.0 - BETA_ONE) * gradient
    second_new = BETA_TWO * second + (1.0 - BETA_TWO) * gradient * gradient
    fixed_first = first_new / (1.0 - BETA_ONE**STEP)
    fixed_second = second_new / (1.0 - BETA_TWO**STEP)
    weight_new = weight - step_rate * (fixed_first / (jnp.sqrt(fixed_second) + ADAM_EPS) + decay_rate * weight)
    return (weight_new, first_new, second_new)


def mm(a, b, dims=NN):
    return lax.dot_general(a, b, dims, preferred_element_type=F32)


def swap(value, rd, rt):
    n_t = lax.axis_size("tensor")
    mask = rd * n_t + rt
    return lax.ppermute(value, AXES, [(i, i ^ mask) for i in range(lax.axis_size("dp") * n_t)])


def rows_at(start, size, step):
    return pl.ds(pl.multiple_of(start, step), size)


def by_head(rows):
    lane = lax.broadcasted_iota(jnp.int32, (rows, LANES), 1)

    def keep(h):
        here = (lane >= h * HD) & (lane < (h + 1) * HD)
        return lambda v: jnp.where(here, v, jnp.zeros_like(v))

    return [keep(h) for h in range(LANES // HD)]


def fill_window(me_t, which, parts, out_ref, sems):
    own, rx, c1, c3 = parts
    n = own.shape[1]
    sources = (own.at[me_t], c1.at[which], rx.at[which], c3.at[which])
    copies = [pltpu.make_async_copy(src, out_ref.at[rows_at((me_t ^ r) * n, n, n), :], sems.at[r]) for r, src in enumerate(sources)]
    for copy in copies:
        copy.start()
    return copies


def copies_in(moves, sems):
    copies = [pltpu.make_async_copy(src, dst, sems.at[i]) for i, (src, dst) in enumerate(moves)]
    for copy in copies:
        copy.start()
    return copies


def prepare_kernel(scal, inputs, cot, attn, pos, norm, out, up, down, ga, gb, xs, c1, attn_s, pos_s, norm_s, out_s, up_s, down_s, sems):
    me_t = scal[1]
    moves = [(attn, attn_s), (pos, pos_s), (norm, norm_s), (up, up_s), (down, down_s), (out, out_s)]
    for rel, ref, at in ((2, xs, 0), (3, xs, 2), (1, c1, 0)):
        moves += [(inputs.at[me_t ^ rel], ref.at[at]), (cot.at[me_t ^ rel], ref.at[at + 1])]
    copies = copies_in(moves, sems)
    for copy in copies[:3]:
        copy.wait()
    per = attn.shape[1]
    pos_per = pos.shape[0]
    tiles = pos.shape[1] // LANES
    for t in range(3):
        ga[0, t * per : (t + 1) * per, :] = attn_s[t].astype(BF16)
    for k in range(tiles):
        at = 3 * per + k * pos_per
        ga[0, at : at + pos_per, :] = pos_s[:, k * LANES : (k + 1) * LANES].astype(BF16)
    at = 3 * per + tiles * pos_per
    both = norm_s[...]
    both = jnp.concatenate([both, both], axis=1)
    both = jnp.concatenate([both, jnp.zeros_like(both)], axis=0)
    high = both.astype(BF16)
    rest = (both - high.astype(F32)).astype(BF16)
    ga[0, at : at + 16, :] = jnp.concatenate([high, rest], axis=0)
    for copy in copies[3:6]:
        copy.wait()
    gb[0, 0:per, :] = up_s[...].astype(BF16)
    gb[0, per : 2 * per, :] = down_s[...].astype(BF16)
    gb[0, 2 * per :, :] = out_s[...].astype(BF16)
    for copy in copies[6:]:
        copy.wait()


def stack_kernel(own, got, both):
    n = own.shape[0]
    both[:n] = own[...]
    both[n:] = got[...]


def attention_kernel(places, n_pieces, scal, *refs):
    own, rx, c1, c3, segs = refs[:5]
    pieces = refs[5 : 5 + n_pieces]
    hid_o, qkv_h, pt_h, mix_o, w_h, nrm_o, x_s, pos_s, bias_s, nrm_s, w_o, qkv_o, pt_o, sems, out_sems = refs[5 + n_pieces :]
    leaving = []

    def leave(src, dst):
        leaving.append(pltpu.make_async_copy(src, dst, out_sems.at[len(leaving)]))
        leaving[-1].start()

    me_dp, me_t = scal[0], scal[1]
    win, width = x_s.shape
    groups = w_o.shape[1] // (3 * LANES)
    filling = fill_window(me_t, 0, (own, rx, c1, c3), x_s, sems)
    if places is None:
        w_o[...] = pieces[0][...]
        pos_s[...] = pieces[1][...]
        nrm_o[...] = pieces[2][...]
    else:
        n_dp = nrm_s.shape[0]
        per = width // n_dp
        pos_per = win // (n_dp * groups)
        for ref, (xr, yr, zs, c) in zip(pieces, places, strict=True):
            tr = xr * 2 + c
            for i, zr in enumerate(zs):
                src = me_dp ^ (zr * 2 + yr)
                for t in range(3):
                    at = (tr * 3 + t) * LANES
                    w_o[rows_at(src * per, per, per), at : at + LANES] = ref[i, t * per : (t + 1) * per]
                where = (me_t ^ tr) * (win // groups) + src * pos_per
                for k in range(width // LANES):
                    at = 3 * per + k * pos_per
                    pos_s[rows_at(where, pos_per, pos_per), k * LANES : (k + 1) * LANES] = ref[i, at : at + pos_per]
                if tr == 0:
                    at = 3 * per + width // LANES * pos_per
                    nrm_s[src] = ref[i, at : at + 16].astype(F32)
        low_lane = lax.broadcasted_iota(jnp.int32, (8, LANES), 1) < per
        for j in range(n_dp // 2):
            left = nrm_s[2 * j]
            right = nrm_s[2 * j + 1]
            both = jnp.where(low_lane, left[0:8] + left[8:16], right[0:8] + right[8:16])
            nrm_o[:, j * LANES : (j + 1) * LANES] = both

    leave(w_o, w_h)

    seg = segs[pl.ds(me_t, 1), :].astype(F32)
    seg_col = jnp.transpose(jnp.broadcast_to(seg, (LANES, win)))
    for i in range(win // LANES):
        key_seg = seg_col[i * LANES : (i + 1) * LANES, 0:1]
        key_at = lax.broadcasted_iota(jnp.int32, (LANES, win), 0) + i * LANES
        query_at = lax.broadcasted_iota(jnp.int32, (LANES, win), 1)
        counts = (key_seg == seg) & (query_at >= key_at)
        bias_s[i * LANES : (i + 1) * LANES, :] = jnp.where(counts, 0.0, NEG_FILL)

    for copy in filling:
        copy.wait()
    hidden = x_s[...].astype(F32) + pos_s[...].astype(F32)
    hid_o[...] = hidden
    x_s[...] = hidden.astype(BF16)
    heads = by_head(win)
    for g in range(groups):
        at = g * 3 * LANES
        qkv = mm(x_s[...], w_o[:, at : at + 3 * LANES]).astype(BF16)
        q = qkv[:, :LANES] * jnp.asarray(HD**-0.5, BF16)
        k = qkv[:, LANES : 2 * LANES]
        v = qkv[:, 2 * LANES :]
        qkv_o[:, at : at + LANES] = q
        qkv_o[:, at + LANES : at + 3 * LANES] = qkv[:, LANES:]
        for j in range(win // QUERIES):
            ext = (j + 1) * QUERIES
            cols = slice(j * QUERIES, ext)
            mixed = jnp.zeros((QUERIES, LANES), F32)
            for h, only in enumerate(heads):
                s = mm(only(k)[:ext], q[cols], NT) + bias_s[:ext, cols]
                e = jnp.exp(s - jnp.max(s, axis=0, keepdims=True))
                p = (e * (1.0 / jnp.sum(e, axis=0, keepdims=True))).astype(BF16)
                pt_o[len(heads) * g + h, :ext, cols] = p
                mixed += mm(p, only(v)[:ext], TN)
            mix_o[cols, g * LANES : (g + 1) * LANES] = mixed.astype(BF16)
            for h in range(len(heads)):
                leave(pt_o.at[len(heads) * g + h, :ext, cols], pt_h.at[len(heads) * g + h, :ext, cols])
    leave(qkv_o, qkv_h)
    for copy in leaving:
        copy.wait()


def norm_forward(v):
    center = v - jnp.mean(v, axis=-1, keepdims=True)
    rs = lax.rsqrt(jnp.mean(center * center, axis=-1, keepdims=True) + NORM_EPS)
    return center * rs, rs


def norm_backward(g, xhat, rs, gain):
    e = g * gain
    return rs * (e - jnp.mean(e, axis=-1, keepdims=True) - xhat * jnp.mean(e * xhat, axis=-1, keepdims=True))


def put_blocks(me_t, value, keep, s1, sx):
    n = keep.shape[0]
    for r, ref in ((0, keep), (1, s1.at[0]), (2, sx.at[0]), (3, sx.at[1])):
        ref[...] = value[rows_at((me_t ^ r) * n, n, n), :].astype(ref.dtype)


CHUNK = 128


def chunk_of(refs, tr, r):
    c, xr, yr, zr = tr & 1, tr >> 1, r & 1, r >> 1
    half = refs[0].shape[0] // 4
    if zr < half:
        first, slot = xr == 1, yr * half + zr
    else:
        first, slot = yr == 1, 2 * half + xr * half + zr - half
    return refs[2 * c + (0 if first else 1)], slot


def ffn_kernel(places, n_pieces, scal, *refs):
    own, rx, c1, c3, hid, mixed, nrm = refs[:7]
    pieces = refs[7 : 7 + n_pieces]
    rest = refs[7 + n_pieces :]
    res_k, res_1, res_x, gone_o, gm_o, gnorm_o = rest[:6]
    if places is None:
        gup_o, gdown_o, gout_o = rest[6:9]
        rest = rest[9:]
    else:
        chunks_o = rest[6:10]
        rest = rest[10:]
    cot_s, out_s, up_s, down_s, a_s, b_s, g_s, xh1_s, r1_s, n1_s, sent_s, act_s, dg_s, low_s, xt_s, sems = rest
    me_dp, me_t = scal[0], scal[1]
    win, width = hid.shape
    groups = up_s.shape[0]
    filling = fill_window(me_t, 1, (own, rx, c1, c3), cot_s, sems)
    if places is None:
        n_dp = 1
        for src, dst in zip(pieces, (out_s, up_s, down_s), strict=True):
            dst[...] = src[...]
    else:
        n_dp = 2 * sum(len(zs) for _, yr, zs, c in places if yr == 0 and c == 0) // 2
        per = width // n_dp
        out_per = LANES // n_dp
        for ref, (xr, yr, zs, c) in zip(pieces, places, strict=True):
            tr = xr * 2 + c
            for i, zr in enumerate(zs):
                src = me_dp ^ (zr * 2 + yr)
                up_s[tr, rows_at(src * per, per, per), :] = ref[i, 0:per]
                down_s[tr, rows_at(src * per, per, per), :] = ref[i, per : 2 * per]
                out_s[rows_at(tr * LANES + src * out_per, out_per, out_per), :] = ref[i, 2 * per : 2 * per + out_per]

    def chunks(fn):
        for i in range(win // CHUNK):
            fn(slice(i * CHUNK, (i + 1) * CHUNK))

    a_s[0] = mm(mixed[...], out_s[...])

    def norm_one(at):
        xhat, rs = norm_forward(hid[at, :] + a_s[0, at, :])
        xh1_s[at, :] = xhat
        r1_s[at, :] = jnp.broadcast_to(rs, (CHUNK, LANES))
        normed = xhat * nrm[0:1, :] + nrm[1:2, :]
        n1_s[at, :] = normed
        sent_s[at, :] = normed.astype(BF16)

    chunks(norm_one)

    for g in range(groups):
        a_s[g % 2] = mm(sent_s[...], up_s[g])

        def gelu(at, g=g):
            v = a_s[g % 2, at, :]
            square = v * v
            half = 0.5 + 0.5 * jnp.tanh(v * (GELU_A + GELU_A * GELU_B * square))
            act_s[g, at, :] = (v * half).astype(BF16)
            dg_s[g, at, :] = half + (half - half * half) * (v * (2.0 * GELU_A + 6.0 * GELU_A * GELU_B * square))

        chunks(gelu)
        n1_s[...] += mm(act_s[g], down_s[g])

    for copy in filling:
        copy.wait()

    def norm_two(i, sums):
        at = slice(i * CHUNK, (i + 1) * CHUNK)
        xhat, rs = norm_forward(n1_s[at, :])
        n1_s[at, :] = xhat * nrm[2:3, :] + nrm[3:4, :]
        g = cot_s[at, :].astype(F32)
        grad = norm_backward(g, xhat, rs, nrm[2:3, :])
        b_s[at, :] = grad
        low_s[at, :] = grad.astype(BF16)
        return (sums[0] + jnp.sum((g * xhat).reshape(-1, 8, width), axis=0), sums[1] + jnp.sum(g.reshape(-1, 8, width), axis=0))

    def every(step):
        sums = (jnp.zeros((8, width), F32),) * 2
        for i in range(win // CHUNK):
            sums = step(i, sums)
        return sums

    gain_two, shift_two = every(norm_two)
    put_blocks(me_t, n1_s, res_k, res_1, res_x)

    def put(g, first, height, source, base):
        for r in range(n_dp):
            ref, slot = chunk_of(chunks_o, g, r)
            ref[slot, first : first + height, :] = source[rows_at(base + (r ^ me_dp) * height, height, height), :]

    xt_s[...] = jnp.transpose(sent_s[...])
    for g in range(groups):
        gdown = mm(jnp.transpose(act_s[g]), low_s[...])
        if places is None:
            gdown_o[g] = gdown.astype(BF16)
        else:
            g_s[0] = gdown.astype(BF16)
            put(g, per, per, g_s.at[0], 0)
        act_s[g] = (mm(low_s[...], down_s[g], NT) * dg_s[g]).astype(BF16)
        gup = mm(xt_s[...], act_s[g])
        if places is None:
            gup_o[g] = gup.astype(BF16)
        else:
            g_s[1] = gup.astype(BF16)
            put(g, 0, per, g_s.at[1], 0)
        b_s[...] += mm(act_s[g], up_s[g], NT)

    def norm_one_back(i, sums):
        at = slice(i * CHUNK, (i + 1) * CHUNK)
        g = b_s[at, :]
        xhat = xh1_s[at, :]
        grad = norm_backward(g, xhat, r1_s[at, 0:1], nrm[0:1, :])
        gone_o[at, :] = grad
        low_s[at, :] = grad.astype(BF16)
        return (sums[0] + jnp.sum((g * xhat).reshape(-1, 8, width), axis=0), sums[1] + jnp.sum(g.reshape(-1, 8, width), axis=0))

    gain_one, shift_one = every(norm_one_back)
    for k, total in enumerate((gain_one, shift_one, gain_two, shift_two)):
        gnorm_o[k : k + 1, :] = jnp.sum(total, axis=0, keepdims=True)
    gnorm_o[4:8, :] = jnp.zeros((4, width), F32)

    gout = mm(jnp.transpose(mixed[...]), low_s[...])
    if places is None:
        gout_o[...] = gout.astype(BF16)
    else:
        g_s[0] = gout.astype(BF16)
        for g in range(groups):
            put(g, 2 * per, out_per, g_s.at[0], g * LANES)
    gm = mm(low_s[...], out_s[...], NT).astype(BF16)
    for g in range(groups):
        gm_o[g] = gm[:, g * LANES : (g + 1) * LANES]


def attention_back_kernel(fast, scal, hid, qkv_h, pt_h, gm, w_h, gone, gnorm, *rest):
    gi_k, gi_1, gi_x = rest[:3]
    if fast:
        chunks_o = rest[3:7]
        rest = rest[7:]
    else:
        gattn_o, gpos_o = rest[3:5]
        rest = rest[5:]
    ht_s, ds_s, dqkv_s, acc_s, g_s, qkv, pt, w, sems = rest
    me_dp, me_t = scal[0], scal[1]
    win, width = hid.shape
    groups = w.shape[1] // (3 * LANES)
    heads = by_head(win)
    arriving = [pltpu.make_async_copy(qkv_h, qkv, sems.at[0])]
    for n in range(pt.shape[0]):
        for j in range(win // QUERIES):
            ext = (j + 1) * QUERIES
            cols = slice(j * QUERIES, ext)
            arriving.append(pltpu.make_async_copy(pt_h.at[n, :ext, cols], pt.at[n, :ext, cols], sems.at[len(arriving)]))
    arriving.append(pltpu.make_async_copy(w_h, w, sems.at[len(arriving)]))
    for copy in arriving:
        copy.start()
    ht_s[...] = jnp.transpose(hid[...].astype(BF16))
    for g in range(groups):
        at = g * 3 * LANES
        if g == 0:
            arriving[0].wait()
        per_group = len(heads) * (win // QUERIES)
        for copy in arriving[1 + g * per_group : 1 + (g + 1) * per_group]:
            copy.wait()
        q = qkv[:, at : at + LANES]
        k = qkv[:, at + LANES : at + 2 * LANES]
        v = qkv[:, at + 2 * LANES : at + 3 * LANES]
        d_mixed = gm[g]
        for j in range(win // QUERIES):
            ext = (j + 1) * QUERIES
            cols = slice(j * QUERIES, ext)
            dq = jnp.zeros((QUERIES, LANES), F32)
            for h, only in enumerate(heads):
                p = pt[len(heads) * g + h, :ext, cols].astype(F32)
                dp = mm(v[:ext], only(d_mixed)[cols], NT)
                ds = (p * (dp - jnp.sum(p * dp, axis=0, keepdims=True))).astype(BF16)
                ds_s[len(heads) * g + h, :ext, cols] = ds
                dq += mm(ds, only(k)[:ext], TN)
            dqkv_s[cols, at : at + LANES] = (dq * HD**-0.5).astype(BF16)
        for i in range(win // QUERIES):
            rows = slice(i * QUERIES, (i + 1) * QUERIES)
            dk = jnp.zeros((QUERIES, LANES), F32)
            dv = jnp.zeros((QUERIES, LANES), F32)
            for h, only in enumerate(heads):
                dk += mm(ds_s[len(heads) * g + h, rows, i * QUERIES :], only(q)[i * QUERIES :])
                dv += mm(pt[len(heads) * g + h, rows, i * QUERIES :], only(d_mixed)[i * QUERIES :])
            dqkv_s[rows, at + LANES : at + 2 * LANES] = dk.astype(BF16)
            dqkv_s[rows, at + 2 * LANES : at + 3 * LANES] = dv.astype(BF16)
    arriving[-1].wait()
    acc_s[...] = gone[...] + mm(dqkv_s[...], w[...], NT)

    put_blocks(me_t, acc_s, gi_k, gi_1, gi_x)
    if not fast:
        for g in range(groups):
            gattn_o[g] = mm(ht_s[...], dqkv_s[:, g * 3 * LANES : (g + 1) * 3 * LANES]).astype(BF16)
        gpos_o[...] = acc_s[...].astype(BF16)
        return
    n_dp = chunks_o[0].shape[0]
    per = width // n_dp
    pos_per = win // (n_dp * groups)
    for g in range(groups):
        g_s[g % 2] = mm(ht_s[...], dqkv_s[:, g * 3 * LANES : (g + 1) * 3 * LANES]).astype(BF16)
        for r in range(n_dp):
            d = r ^ me_dp
            ref, slot = chunk_of(chunks_o, g, r)
            for t in range(3):
                ref[slot, t * per : (t + 1) * per, :] = g_s[g % 2, rows_at(d * per, per, per), t * LANES : (t + 1) * LANES]
            where = (me_t ^ g) * (win // groups) + d * pos_per
            for k in range(width // LANES):
                at = 3 * per + k * pos_per
                ref[slot, at : at + pos_per, :] = acc_s[rows_at(where, pos_per, pos_per), k * LANES : (k + 1) * LANES].astype(BF16)
            at = 3 * per + width // LANES * pos_per
            tile = gnorm[0:8, rows_at((d >> 1) * LANES, LANES, LANES)]
            ref[slot, at : at + 16, :] = jnp.concatenate([tile, tile], axis=0).astype(BF16)


def near_kernel(rest, got, x, y, x2, y2, own, far, odd):
    own[...] = total(rest[0], got[0], x[0], x2[0])
    far[...] = total(rest[4], got[4], y[0], y2[0])
    odd[0] = low(rest[1], got[1], x[1], x2[1])
    odd[1] = low(rest[5], got[5], y[1], y2[1])


def second_kernel(done, rest, got, x, y, a, b):
    del done
    for i in range(2):
        a[i] = low(rest[2 + i], got[2 + i], x[2 + i])
        b[i] = low(rest[6 + i], got[6 + i], y[2 + i])


def far_kernel(own, far, near, own_o, far_o):
    own_o[...] = total(own[...], near[0])
    far_o[0] = low(far[...], near[1])


def far_near_kernel(own, far, near, rest, got, x, y, x2, y2, own_o, far_o, *others):
    far_kernel(own, far, near, own_o, far_o)
    near_kernel(rest, got, x, y, x2, y2, *others)


def update(refs, gradient, rate, decay):
    weight, one, two, new_weight, new_one, new_two = refs
    new_weight[...], new_one[...], new_two[...] = adam_step(weight[...], gradient, one[...], two[...], rate, decay)


def rows_update_kernel(which, own, far, *refs):
    n = len(which)
    *refs, token = refs
    token[...] = jnp.zeros_like(token)
    grad = total(own[...], far[0])
    at = 0
    for i, index in enumerate(which):
        height = refs[i].shape[0]
        update(refs[i :: n], grad[at : at + height], RATES[index], DECAYS[index])
        at += height


def tiles_update_kernel(scal, done, own, far, *refs):
    *refs, token = refs
    token[...] = done[...]
    attn, pos, norm = refs[0::3], refs[1::3], refs[2::3]
    grad = total(own[...], far[0])
    per = attn[0].shape[1]
    pos_per, width = pos[0].shape
    update(attn, grad[: 3 * per].reshape(attn[0].shape), RATES[0], DECAYS[0])
    at = 3 * per
    rows = [grad[at + k * pos_per : at + (k + 1) * pos_per] for k in range(width // LANES)]
    update(pos, jnp.concatenate(rows, axis=1), RATES[4], DECAYS[4])
    at += width // LANES * pos_per
    tile = grad[at : at + 8]
    half = jnp.where((scal[0] & 1) == 1, tile[:4, LANES // 2 :], tile[:4, : LANES // 2])
    update(norm, half, RATES[5], DECAYS[5])


def finish_kernel(scal, done, res_k, gi_k, res_1, gi_1, r2, r3, res_o, gi_o):
    del done
    me_t = scal[1]
    for r, (res, gi) in enumerate(((res_k[...], gi_k[...]), (res_1[0], gi_1[0]), (r2[0], r2[1]), (r3[0], r3[1]))):
        res_o[me_t ^ r] = res
        gi_o[me_t ^ r] = gi.astype(F32)


def after(value, *others):
    return lax.optimization_barrier((value, *others))[0]


def stacked(q, got):
    out = jax.ShapeDtypeStruct((2 * q.shape[0], *q.shape[1:]), q.dtype)
    return call(stack_kernel, [out], [], [q, got], "vv", 6, 1_000)[0]


def gather_z(value, *others):
    nz = lax.axis_size("dp") // 2
    q, order = value, [0]
    step = nz // 2
    while step:
        if step == 1:
            q = after(q, *others)
        q = stacked(q, swap(q, step * 2, 0))
        order = order + [z ^ step for z in order]
        step //= 2
    return q, tuple(order)


def gather_xy(q, order, qx=None, qy=None, *others):
    half = len(order) // 2
    if qx is None:
        qx, qy = swap(q, 0, 2), swap(q, 1, 0)
    a, b = after(qx[:half], *others), after(qy[half:], *others)
    return [(q, (0, 0, order)), (qx, (1, 0, order)), (qy, (0, 1, order)), (swap(a, 1, 0), (1, 1, order[:half])), (swap(b, 0, 2), (1, 1, order[half:]))]


def both_cores(found):
    out = []
    for array, place in found:
        out.append((array, (*place, 0)))
        out.append((swap(array, 0, 1), (*place, 1)))
    return [f[0] for f in out], tuple(f[1] for f in out)


class Reduction:
    def __init__(self, keep_first, keep_rest, send_first, send_rest):
        self.half = keep_first.shape[0] // 4
        self.n = keep_first.shape[0] // 2
        self.sums = [(keep_rest,)]
        self.send_rest = send_rest
        got = swap(send_first, 0, 1)
        self.a = low(keep_first[: self.n], got[: self.n])
        self.b = low(keep_first[self.n :], got[self.n :])

    def terms(self, a, start, stop):
        at = 0 if a else self.n
        found = [k[at + start : at + stop] for k in self.rest]
        for pair in self.got:
            g = pair[0 if a else 1]
            if g.shape[0] >= stop:
                found.append(g[start:stop])
        return found

    def first(self):
        self.rest = [self.sums[0][0], swap(self.send_rest, 0, 1)]
        self.got = [(swap(self.a, 0, 2), swap(self.b, 1, 0))]
        return self.got[0]

    def second(self, *others):
        h = self.half
        a, b = [after(low(*self.terms(part, h, 2 * h)), *others) for part in (True, False)]
        self.got.append((swap(a, 1, 0), swap(b, 0, 2)))
        return self.got[1]

    def over_z(self, *others):
        h = self.half
        arrived = []
        for z in range(1, 2 * h):
            chunk = low(*self.terms(z < h, z % h, z % h + 1))
            arrived.append(swap(after(chunk, *others), 2 * z, 0))
        return arrived

    def result(self, arrived):
        return total(*self.terms(True, 0, 1), *arrived)[0]


def call(kernel, outs, scratch, args, spaces, mib, flops):
    vmem = pl.BlockSpec(memory_space=pltpu.VMEM)
    args = [pltpu.with_memory_space_constraint(v, pltpu.HBM) if k == "h" else v for v, k in zip(args, spaces, strict=True)]
    kinds = {"s": pl.BlockSpec(memory_space=pltpu.SMEM), "v": vmem, "a": pl.BlockSpec(memory_space=pl.ANY), "h": pl.BlockSpec(memory_space=pltpu.HBM)}
    return pl.pallas_call(
        kernel,
        out_shape=outs,
        in_specs=[kinds[k] for k in spaces],
        out_specs=[vmem if isinstance(v, jax.ShapeDtypeStruct) else kinds["h"] for v in outs],
        scratch_shapes=[pltpu.VMEM(*s) if isinstance(s, tuple) else pltpu.SemaphoreType.DMA(tuple(s)) for s in scratch],
        compiler_params=pltpu.CompilerParams(vmem_limit_bytes=mib * 1024 * 1024),
        cost_estimate=pl.CostEstimate(flops=flops, bytes_accessed=0, transcendentals=0),
    )(*args)


def body(
    inputs,
    segment_ids,
    cotangent,
    attn_proj,
    out_proj,
    up_proj,
    down_proj,
    pos_table,
    norm_params,
    first_attn,
    second_attn,
    first_out,
    second_out,
    first_up,
    second_up,
    first_down,
    second_down,
    first_pos,
    second_pos,
    first_norm,
    second_norm,
):
    n_dp, n_t = lax.axis_size("dp"), lax.axis_size("tensor")
    me_dp, me_t = lax.axis_index("dp"), lax.axis_index("tensor")
    scal = jnp.stack([me_dp, me_t]).astype(jnp.int32)
    windows, block, width = inputs.shape
    win = block * n_t
    inner = up_proj.shape[1]
    group = attn_proj.shape[2]
    per, out_per, pos_per = attn_proj.shape[1], out_proj.shape[0], pos_table.shape[0]
    fast = out_per % 16 == 0 and pos_per % 16 == 0 and 2 * per == LANES and n_dp == 8 and n_t == 4
    sds = jax.ShapeDtypeStruct

    if fast:
        ga, gb, xs, c1 = call(
            prepare_kernel,
            [
                sds((1, 3 * per + width // LANES * pos_per + 16, LANES), BF16),
                sds((1, 2 * per + out_per, width), BF16),
                sds((4, block, width), BF16),
                sds((2, block, width), BF16),
            ],
            [(v.shape, F32) for v in (attn_proj, pos_table, norm_params, out_proj, up_proj, down_proj)] + [[12]],
            [scal, inputs, cotangent, attn_proj, pos_table, norm_params, out_proj, up_proj, down_proj],
            "s" + "h" * 8,
            8,
            1_000,
        )
        a2 = stacked(ga, swap(ga, 4, 0))
        qa, za = stacked(a2, swap(a2, 2, 0)), (0, 2, 1, 3)
        gb = after(gb, a2)
        rx = swap(xs, 0, 2)
        qb, zb = gather_z(gb, qa)
        c1 = swap(c1, 0, 1)
        c3 = swap(rx[2:], 0, 1)
        qax, qay, qaxy = swap(qa, 0, 2), swap(qa, 1, 0), swap(qa, 1, 2)
        a_args, a_places = both_cores([(qa, (0, 0, za)), (qax, (1, 0, za)), (qay, (0, 1, za)), (qaxy, (1, 1, za))])
        qb = after(qb, rx, qax, qay)
        qbx, qby = swap(qb, 0, 2), swap(qb, 1, 0)
    else:

        def pair(rel):
            return jnp.concatenate([lax.dynamic_slice_in_dim(v, me_t ^ rel, 1, 0) for v in (inputs, cotangent)])

        rx = swap(jnp.concatenate([pair(2), pair(3)]), 0, 2)
        c1 = swap(pair(1), 0, 1)
        c3 = swap(rx[2:], 0, 1)
        relative = me_t ^ jnp.arange(n_t)
        whole = [lax.all_gather(lax.all_gather(v.astype(BF16), "dp"), "tensor") for v in (attn_proj, out_proj, up_proj, down_proj)]
        attn_w, out_w, up_w, down_w = [jnp.take(v, relative, axis=0) for v in whole]
        attn_w = attn_w.transpose(1, 3, 0, 2, 4).reshape(width, n_t * 3 * group)
        pos_w = lax.all_gather(lax.all_gather(pos_table.astype(BF16), "dp", axis=0, tiled=True), "tensor", axis=0, tiled=True)
        norm_w = lax.all_gather(norm_params, "dp", axis=1, tiled=True)
        norm_w = jnp.concatenate([norm_w, jnp.zeros_like(norm_w)])
        a_args, a_places = [attn_w, pos_w, norm_w], None
        b_args, b_places = [out_w.reshape(n_t * group, width), up_w.reshape(n_t, width, inner), down_w.reshape(n_t, inner, width)], None

    hid, qkv, pt, mixed, attn_all, norm_all = call(
        functools.partial(attention_kernel, a_places, len(a_args)),
        [
            sds((win, width), F32),
            pltpu.HBM((win, n_t * 3 * group), BF16),
            pltpu.HBM((n_t * group // HD, win, win), BF16),
            sds((win, n_t * group), BF16),
            pltpu.HBM((width, n_t * 3 * group), BF16),
            sds((8, width), F32),
        ],
        [((win, width), BF16), ((win, width), BF16), ((win, win), F32), ((n_dp, 16, LANES), F32), ((width, n_t * 3 * group), BF16), ((win, n_t * 3 * group), BF16), ((n_t * group // HD, win, win), BF16), [4], [32]],
        [scal, inputs, rx, c1, c3, segment_ids, *a_args],
        "shaaav" + "v" * len(a_args),
        14,
        1_000_000,
    )
    if fast:
        b_args, b_places = both_cores(gather_xy(qb, zb, qbx, qby, hid))

    blocks = [sds((block, width), BF16), sds((1, block, width), BF16), sds((2, block, width), BF16)]
    if fast:
        rows_b = 2 * per + out_per
        grads_b = [sds((n_dp, rows_b, width), BF16)] * 4
    else:
        grads_b = [sds((n_t, width, inner), BF16), sds((n_t, inner, width), BF16), sds((n_t * group, width), BF16)]
    res_k, res_1, res_x, gone, gm, gnorm, *got_b = call(
        functools.partial(ffn_kernel, b_places, len(b_args)),
        [*blocks, sds((win, width), F32), sds((n_t, win, group), BF16), sds((8, width), F32), *grads_b],
        [
            ((win, width), BF16),
            ((n_t * group, width), BF16),
            ((n_t, width, inner), BF16),
            ((n_t, inner, width), BF16),
            ((2, win, width), F32),
            ((win, width), F32),
            ((2, win, width), BF16),
            ((win, width), F32),
            ((win, LANES), F32),
            ((win, width), F32),
            ((win, width), BF16),
            ((n_t, win, inner), BF16),
            ((n_t, win, inner), F32),
            ((win, width), BF16),
            ((width, win), BF16),
            [4],
        ],
        [scal, cotangent, rx, c1, c3, hid, mixed, norm_all, *b_args],
        "shaaavvv" + "v" * len(b_args),
        22,
        1_000_000,
    )
    if fast:
        red_b = Reduction(*got_b)
        gone = after(gone, red_b.a, red_b.b)
        first_b = red_b.first()

    blocks = [sds((block, width), F32), *blocks[1:]]
    if fast:
        rows_a = 3 * per + width // LANES * pos_per + 16
        grads_a = [sds((n_dp, rows_a, LANES), BF16)] * 4
    else:
        grads_a = [sds((n_t, width, 3 * group), BF16), sds((win, width), BF16)]
    gi_k, gi_1, gi_x, *got_a = call(
        functools.partial(attention_back_kernel, fast),
        [*blocks, *grads_a],
        [
            ((width, win), BF16),
            ((n_t * group // HD, win, win), BF16),
            ((win, n_t * 3 * group), BF16),
            ((win, width), F32),
            ((2, width, 3 * group), BF16),
            ((win, n_t * 3 * group), BF16),
            ((n_t * group // HD, win, win), BF16),
            ((width, n_t * 3 * group), BF16),
            [2 + 2 * n_t * group // HD],
        ],
        [scal, hid, qkv, pt, gm, attn_all, gone, gnorm],
        "svhhvhvv",
        18,
        1_000_000,
    )
    leaving = [jnp.concatenate([res_x[i : i + 1], gi_x[i : i + 1]]) for i in range(2)]
    if fast:
        keep_first, keep_rest, send_first, send_rest = got_a
        red_a = Reduction(keep_first, keep_rest, send_first, send_rest)
        first_a, second_b = red_a.first(), red_b.second()
        chunk_b, chunk_a = got_b[0].shape[1:], got_a[0].shape[1:]
        before_z = [[sds(chunk, F32), sds(chunk, F32), sds((2, *chunk), BF16)] for chunk in (chunk_b, chunk_a)]
        last = [[sds(chunk, F32), sds((1, *chunk), BF16)] for chunk in (chunk_b, chunk_a)]
        own_b, far_b, odd_b = call(near_kernel, before_z[0], [], [*red_b.rest, *first_b, *second_b], "v" * 6, 8, 1_000)
        a_y, a_x = call(second_kernel, [sds((2, *chunk_a), BF16)] * 2, [], [own_b, *red_a.rest, *first_a], "avvvv", 8, 1_000)
        second_a = swap(a_y, 1, 0), swap(a_x, 0, 2)
        near_b = swap(odd_b, 2, 0)
        own_b, far_b, own_a, far_a, odd_a = call(
            far_near_kernel,
            last[0] + before_z[1],
            [],
            [own_b, far_b, near_b, *red_a.rest, *first_a, *second_a],
            "v" * 9,
            8,
            1_000,
        )
        far_b = swap(far_b, 4, 0)
        r2, r3 = [swap(after(v, own_a), 0, m) for v, m in zip(leaving, (2, 3), strict=True)]
        own_a, far_a = call(far_kernel, last[1], [], [own_a, far_a, swap(odd_a, 2, 0)], "vvv", 4, 1_000)
        far_a = swap(far_a, 4, 0)
    else:
        r2, r3 = [swap(v, 0, m) for v, m in zip(leaving, (2, 3), strict=True)]
    r1 = [swap(res_1, 0, 1), swap(gi_1, 0, 1)]
    masters = (attn_proj, out_proj, up_proj, down_proj, pos_table, norm_params)
    firsts = (first_attn, first_out, first_up, first_down, first_pos, first_norm)
    seconds = (second_attn, second_out, second_up, second_down, second_pos, second_norm)
    updated = [None] * 6
    token = sds((8, LANES), F32)
    done = jnp.zeros(token.shape, F32)
    if fast:
        which = (2, 3, 1)
        state = [group[i] for group in (masters, firsts, seconds) for i in which]
        new = call(
            functools.partial(rows_update_kernel, which),
            [sds(v.shape, F32) for v in state] + [token],
            [],
            [own_b, far_b, *state],
            "v" * 11,
            8,
            2_000_000_000,
        )
        for i, index in enumerate(which):
            updated[index] = new[i:9:3]
        done = new[9]
    if fast:
        which = (0, 4, 5)
        state = [group[i] for group in (masters, firsts, seconds) for i in which]
        new = call(
            tiles_update_kernel,
            [sds(v.shape, F32) for v in state] + [token],
            [],
            [scal, done, own_a, far_a, *state],
            "sv" + "v" * 11,
            8,
            1_000_000,
        )
        for i, index in enumerate(which):
            updated[index] = new[i:9:3]
        done = new[9]
    outputs, grad_input = call(
        finish_kernel,
        [sds(inputs.shape, BF16), sds(inputs.shape, F32)],
        [],
        [scal, done, res_k, gi_k, *r1, r2, r3],
        "sv" + "v" * 6,
        8,
        1_000,
    )
    if not fast:

        def reduced(value, own_axis):
            arrived = lax.all_to_all(value, "dp", split_axis=0, concat_axis=0, tiled=True)
            part = arrived.astype(F32).sum(axis=0).astype(BF16)
            arrived = lax.all_to_all(part, "tensor", split_axis=0, concat_axis=0, tiled=True)
            return arrived.astype(F32).sum(axis=0)

        gup, gdown, gout = got_b
        gattn, gpos = got_a
        gup, gdown, gout, gattn = [jnp.take(v, relative, axis=0) for v in (gup, gdown, gout.reshape(n_t, group, width), gattn)]
        g_up = reduced(gup.reshape(n_t, n_dp, per, inner).swapaxes(0, 1), 0)
        g_down = reduced(gdown.reshape(n_t, n_dp, inner // n_dp, width).swapaxes(0, 1), 0)
        g_out = reduced(gout.reshape(n_t, n_dp, out_per, width).swapaxes(0, 1), 0)
        g_pos = reduced(gpos.reshape(n_t, n_dp, pos_per, width).swapaxes(0, 1), 0)
        g_attn = reduced(gattn.reshape(n_t, n_dp, per, 3, group).swapaxes(0, 1), 0).swapaxes(0, 1)
        cut = gnorm[:4].reshape(4, n_dp, width // n_dp).swapaxes(0, 1).astype(BF16)
        g_norm = reduced(jnp.broadcast_to(cut[:, None], (n_dp, n_t, *cut.shape[1:])), 0)

        gradients = (g_attn, g_out, g_up, g_down, g_pos, g_norm)
        for index in range(6):
            updated[index] = adam_step(masters[index], gradients[index], firsts[index], seconds[index], RATES[index], DECAYS[index])
    return (outputs, grad_input, *[v for new in updated for v in new])


def solution(mesh):
    acts = P("dp", "tensor", None)
    attn = P(None, "dp", "tensor")
    both = P(("tensor", "dp"), None)
    up = P("dp", "tensor")
    norm = P(None, "dp")
    return jax.shard_map(
        body,
        mesh=mesh,
        in_specs=(acts, P("dp", None), acts, attn, both, up, both, both, norm, *(attn,) * 2, *(both,) * 2, *(up,) * 2, *(both,) * 4, *(norm,) * 2),
        out_specs=(acts, acts, *(attn,) * 3, *(both,) * 3, *(up,) * 3, *(both,) * 6, *(norm,) * 3),
        check_vma=False,
    )
```

```python
import functools

import jax
import jax.numpy as jnp
from jax import lax
from jax.experimental import pallas as pl
from jax.experimental.pallas import tpu as pltpu
from jax.sharding import PartitionSpec as P

HD = 64
STEP = 10
LANES = 128

NORM_EPS = 1e-05
NEG_FILL = -1e30
BETA_ONE = 0.9
BETA_TWO = 0.95
ADAM_EPS = 1e-08
RATES = (0.03, 0.2, 0.03, 0.02, 0.3, 0.3)
DECAYS = (0.1, 0.1, 0.1, 0.1, 0.1, 0.0)
GELU_A = 0.7978845608028654
GELU_B = 0.044715

F32 = jnp.float32
BF16 = jnp.bfloat16
AXES = ("dp", "tensor")

NN = (((1,), (0,)), ((), ()))
NT = (((1,), (1,)), ((), ()))
TN = (((0,), (0,)), ((), ()))
QUERIES = 256


def total(*parts):
    return sum(p.astype(F32) for p in parts)


def low(*parts):
    return total(*parts).astype(BF16)


def adam_step(weight, gradient, moment_one, second, step_rate, decay_rate):
    first_new = BETA_ONE * moment_one + (1.0 - BETA_ONE) * gradient
    second_new = BETA_TWO * second + (1.0 - BETA_TWO) * gradient * gradient
    fixed_first = first_new / (1.0 - BETA_ONE**STEP)
    fixed_second = second_new / (1.0 - BETA_TWO**STEP)
    weight_new = weight - step_rate * (fixed_first / (jnp.sqrt(fixed_second) + ADAM_EPS) + decay_rate * weight)
    return (weight_new, first_new, second_new)


def mm(a, b, dims=NN):
    return lax.dot_general(a, b, dims, preferred_element_type=F32)


def swap(value, rd, rt):
    n_t = lax.axis_size("tensor")
    mask = rd * n_t + rt
    return lax.ppermute(value, AXES, [(i, i ^ mask) for i in range(lax.axis_size("dp") * n_t)])


def rows_at(start, size, step):
    return pl.ds(pl.multiple_of(start, step), size)


def by_head(rows):
    lane = lax.broadcasted_iota(jnp.int32, (rows, LANES), 1)

    def keep(h):
        here = (lane >= h * HD) & (lane < (h + 1) * HD)
        return lambda v: jnp.where(here, v, jnp.zeros_like(v))

    return [keep(h) for h in range(LANES // HD)]


def fill_window(me_t, which, parts, out_ref):
    own, rx, c1, c3 = parts
    n = own.shape[1]
    for r, ref in enumerate((own, c1, rx, c3)):
        out_ref[rows_at((me_t ^ r) * n, n, n), :] = ref[which]


def copies_in(moves, sems):
    copies = [pltpu.make_async_copy(src, dst, sems.at[i]) for i, (src, dst) in enumerate(moves)]
    for copy in copies:
        copy.start()
    return copies


def prepare_kernel(scal, inputs, cot, attn, pos, norm, out, up, down, ga, gb, xs, c1, own, attn_s, pos_s, norm_s, out_s, up_s, down_s, sems):
    me_t = scal[1]
    moves = [(attn, attn_s), (pos, pos_s), (norm, norm_s), (up, up_s), (down, down_s), (out, out_s)]
    for rel, ref, at in ((2, xs, 0), (3, xs, 2), (1, c1, 0), (0, own, 0)):
        moves += [(inputs.at[me_t ^ rel], ref.at[at]), (cot.at[me_t ^ rel], ref.at[at + 1])]
    copies = copies_in(moves, sems)
    for copy in copies[:3]:
        copy.wait()
    per = attn.shape[1]
    pos_per = pos.shape[0]
    tiles = pos.shape[1] // LANES
    for t in range(3):
        ga[0, t * per : (t + 1) * per, :] = attn_s[t].astype(BF16)
    for k in range(tiles):
        at = 3 * per + k * pos_per
        ga[0, at : at + pos_per, :] = pos_s[:, k * LANES : (k + 1) * LANES].astype(BF16)
    at = 3 * per + tiles * pos_per
    both = norm_s[...]
    both = jnp.concatenate([both, both], axis=1)
    both = jnp.concatenate([both, jnp.zeros_like(both)], axis=0)
    high = both.astype(BF16)
    rest = (both - high.astype(F32)).astype(BF16)
    ga[0, at : at + 16, :] = jnp.concatenate([high, rest], axis=0)
    for copy in copies[3:6]:
        copy.wait()
    gb[0, 0:per, :] = up_s[...].astype(BF16)
    gb[0, per : 2 * per, :] = down_s[...].astype(BF16)
    gb[0, 2 * per :, :] = out_s[...].astype(BF16)
    for copy in copies[6:]:
        copy.wait()


def stack_kernel(own, got, both):
    n = own.shape[0]
    both[:n] = own[...]
    both[n:] = got[...]


def attention_kernel(places, n_pieces, scal, *refs):
    own, rx, c1, c3, segs = refs[:5]
    pieces = refs[5 : 5 + n_pieces]
    hid_o, qkv_h, pt_h, mix_o, w_h, nrm_o, x_s, pos_s, bias_s, nrm_s, w_o, qkv_o, pt_o, out_sems = refs[5 + n_pieces :]
    leaving = []

    def leave(src, dst):
        leaving.append(pltpu.make_async_copy(src, dst, out_sems.at[len(leaving)]))
        leaving[-1].start()

    me_dp, me_t = scal[0], scal[1]
    win, width = x_s.shape
    groups = w_o.shape[1] // (3 * LANES)
    fill_window(me_t, 0, (own, rx, c1, c3), x_s)
    if places is None:
        w_o[...] = pieces[0][...]
        pos_s[...] = pieces[1][...]
        nrm_o[...] = pieces[2][...]
    else:
        n_dp = nrm_s.shape[0]
        per = width // n_dp
        pos_per = win // (n_dp * groups)
        for ref, (xr, yr, zs, c) in zip(pieces, places, strict=True):
            tr = xr * 2 + c
            for i, zr in enumerate(zs):
                src = me_dp ^ (zr * 2 + yr)
                for t in range(3):
                    at = (tr * 3 + t) * LANES
                    w_o[rows_at(src * per, per, per), at : at + LANES] = ref[i, t * per : (t + 1) * per]
                where = (me_t ^ tr) * (win // groups) + src * pos_per
                for k in range(width // LANES):
                    at = 3 * per + k * pos_per
                    pos_s[rows_at(where, pos_per, pos_per), k * LANES : (k + 1) * LANES] = ref[i, at : at + pos_per]
                if tr == 0:
                    at = 3 * per + width // LANES * pos_per
                    nrm_s[src] = ref[i, at : at + 16].astype(F32)
        low_lane = lax.broadcasted_iota(jnp.int32, (8, LANES), 1) < per
        for j in range(n_dp // 2):
            left = nrm_s[2 * j]
            right = nrm_s[2 * j + 1]
            both = jnp.where(low_lane, left[0:8] + left[8:16], right[0:8] + right[8:16])
            nrm_o[:, j * LANES : (j + 1) * LANES] = both

    leave(w_o, w_h)

    seg = segs[pl.ds(me_t, 1), :].astype(F32)
    seg_col = jnp.transpose(jnp.broadcast_to(seg, (LANES, win)))
    for i in range(win // LANES):
        key_seg = seg_col[i * LANES : (i + 1) * LANES, 0:1]
        key_at = lax.broadcasted_iota(jnp.int32, (LANES, win), 0) + i * LANES
        query_at = lax.broadcasted_iota(jnp.int32, (LANES, win), 1)
        counts = (key_seg == seg) & (query_at >= key_at)
        bias_s[i * LANES : (i + 1) * LANES, :] = jnp.where(counts, 0.0, NEG_FILL)

    hidden = x_s[...].astype(F32) + pos_s[...].astype(F32)
    hid_o[...] = hidden
    x_s[...] = hidden.astype(BF16)
    heads = by_head(win)
    for g in range(groups):
        at = g * 3 * LANES
        qkv = mm(x_s[...], w_o[:, at : at + 3 * LANES]).astype(BF16)
        q = qkv[:, :LANES] * jnp.asarray(HD**-0.5, BF16)
        k = qkv[:, LANES : 2 * LANES]
        v = qkv[:, 2 * LANES :]
        qkv_o[:, at : at + LANES] = q
        qkv_o[:, at + LANES : at + 3 * LANES] = qkv[:, LANES:]
        leave(qkv_o.at[:, at : at + 3 * LANES], qkv_h.at[:, at : at + 3 * LANES])
        for j in range(win // QUERIES):
            ext = (j + 1) * QUERIES
            cols = slice(j * QUERIES, ext)
            mixed = jnp.zeros((QUERIES, LANES), F32)
            for h, only in enumerate(heads):
                s = mm(only(k)[:ext], q[cols], NT) + bias_s[:ext, cols]
                e = jnp.exp(s - jnp.max(s, axis=0, keepdims=True))
                p = (e * (1.0 / jnp.sum(e, axis=0, keepdims=True))).astype(BF16)
                pt_o[len(heads) * g + h, :ext, cols] = p
                mixed += mm(p, only(v)[:ext], TN)
            mix_o[cols, g * LANES : (g + 1) * LANES] = mixed.astype(BF16)
            for h in range(len(heads)):
                leave(pt_o.at[len(heads) * g + h, :ext, cols], pt_h.at[len(heads) * g + h, :ext, cols])
    for copy in leaving:
        copy.wait()


def norm_forward(v):
    center = v - jnp.mean(v, axis=-1, keepdims=True)
    rs = lax.rsqrt(jnp.mean(center * center, axis=-1, keepdims=True) + NORM_EPS)
    return center * rs, rs


def norm_backward(g, xhat, rs, gain):
    e = g * gain
    return rs * (e - jnp.mean(e, axis=-1, keepdims=True) - xhat * jnp.mean(e * xhat, axis=-1, keepdims=True))


def put_blocks(me_t, value, keep, s1, sx):
    n = keep.shape[0]
    for r, ref in ((0, keep), (1, s1.at[0]), (2, sx.at[0]), (3, sx.at[1])):
        ref[...] = value[rows_at((me_t ^ r) * n, n, n), :].astype(ref.dtype)


CHUNK = 128


def chunk_of(refs, tr, r):
    c, xr, yr, zr = tr & 1, tr >> 1, r & 1, r >> 1
    half = refs[0].shape[0] // 4
    if zr < half:
        first, slot = xr == 1, yr * half + zr
    else:
        first, slot = yr == 1, 2 * half + xr * half + zr - half
    return refs[2 * c + (0 if first else 1)], slot


def ffn_kernel(places, n_pieces, scal, *refs):
    own, rx, c1, c3, hid, mixed, nrm = refs[:7]
    pieces = refs[7 : 7 + n_pieces]
    rest = refs[7 + n_pieces :]
    res_k, res_1, res_x, gone_o, gm_o, gnorm_o = rest[:6]
    if places is None:
        gup_o, gdown_o, gout_o = rest[6:9]
        rest = rest[9:]
    else:
        chunks_o = rest[6:10]
        rest = rest[10:]
    cot_s, out_s, up_s, down_s, a_s, b_s, g_s, xh1_s, r1_s, n1_s, sent_s, act_s, dg_s, low_s, xt_s = rest
    me_dp, me_t = scal[0], scal[1]
    win, width = hid.shape
    groups = up_s.shape[0]
    fill_window(me_t, 1, (own, rx, c1, c3), cot_s)
    if places is None:
        n_dp = 1
        for src, dst in zip(pieces, (out_s, up_s, down_s), strict=True):
            dst[...] = src[...]
    else:
        n_dp = 2 * sum(len(zs) for _, yr, zs, c in places if yr == 0 and c == 0) // 2
        per = width // n_dp
        out_per = LANES // n_dp
        for ref, (xr, yr, zs, c) in zip(pieces, places, strict=True):
            tr = xr * 2 + c
            for i, zr in enumerate(zs):
                src = me_dp ^ (zr * 2 + yr)
                up_s[tr, rows_at(src * per, per, per), :] = ref[i, 0:per]
                down_s[tr, rows_at(src * per, per, per), :] = ref[i, per : 2 * per]
                out_s[rows_at(tr * LANES + src * out_per, out_per, out_per), :] = ref[i, 2 * per : 2 * per + out_per]

    def chunks(fn):
        for i in range(win // CHUNK):
            fn(slice(i * CHUNK, (i + 1) * CHUNK))

    a_s[0] = mm(mixed[...], out_s[...])

    def norm_one(at):
        xhat, rs = norm_forward(hid[at, :] + a_s[0, at, :])
        xh1_s[at, :] = xhat
        r1_s[at, :] = jnp.broadcast_to(rs, (CHUNK, LANES))
        normed = xhat * nrm[0:1, :] + nrm[1:2, :]
        n1_s[at, :] = normed
        sent_s[at, :] = normed.astype(BF16)

    chunks(norm_one)

    for g in range(groups):
        a_s[g % 2] = mm(sent_s[...], up_s[g])

        def gelu(at, g=g):
            v = a_s[g % 2, at, :]
            square = v * v
            half = 0.5 + 0.5 * jnp.tanh(v * (GELU_A + GELU_A * GELU_B * square))
            act_s[g, at, :] = (v * half).astype(BF16)
            dg_s[g, at, :] = half + (half - half * half) * (v * (2.0 * GELU_A + 6.0 * GELU_A * GELU_B * square))

        chunks(gelu)
        n1_s[...] += mm(act_s[g], down_s[g])

    def norm_two(i, sums):
        at = slice(i * CHUNK, (i + 1) * CHUNK)
        xhat, rs = norm_forward(n1_s[at, :])
        n1_s[at, :] = xhat * nrm[2:3, :] + nrm[3:4, :]
        g = cot_s[at, :].astype(F32)
        grad = norm_backward(g, xhat, rs, nrm[2:3, :])
        b_s[at, :] = grad
        low_s[at, :] = grad.astype(BF16)
        return (sums[0] + jnp.sum((g * xhat).reshape(-1, 8, width), axis=0), sums[1] + jnp.sum(g.reshape(-1, 8, width), axis=0))

    def every(step):
        sums = (jnp.zeros((8, width), F32),) * 2
        for i in range(win // CHUNK):
            sums = step(i, sums)
        return sums

    gain_two, shift_two = every(norm_two)
    put_blocks(me_t, n1_s, res_k, res_1, res_x)

    def put(g, first, height, source, base):
        for r in range(n_dp):
            ref, slot = chunk_of(chunks_o, g, r)
            ref[slot, first : first + height, :] = source[rows_at(base + (r ^ me_dp) * height, height, height), :]

    xt_s[...] = jnp.transpose(sent_s[...])
    for g in range(groups):
        gdown = mm(jnp.transpose(act_s[g]), low_s[...])
        if places is None:
            gdown_o[g] = gdown.astype(BF16)
        else:
            g_s[0] = gdown.astype(BF16)
            put(g, per, per, g_s.at[0], 0)
        act_s[g] = (mm(low_s[...], down_s[g], NT) * dg_s[g]).astype(BF16)
        gup = mm(xt_s[...], act_s[g])
        if places is None:
            gup_o[g] = gup.astype(BF16)
        else:
            g_s[1] = gup.astype(BF16)
            put(g, 0, per, g_s.at[1], 0)
        b_s[...] += mm(act_s[g], up_s[g], NT)

    def norm_one_back(i, sums):
        at = slice(i * CHUNK, (i + 1) * CHUNK)
        g = b_s[at, :]
        xhat = xh1_s[at, :]
        grad = norm_backward(g, xhat, r1_s[at, 0:1], nrm[0:1, :])
        gone_o[at, :] = grad
        low_s[at, :] = grad.astype(BF16)
        return (sums[0] + jnp.sum((g * xhat).reshape(-1, 8, width), axis=0), sums[1] + jnp.sum(g.reshape(-1, 8, width), axis=0))

    gain_one, shift_one = every(norm_one_back)
    for k, total in enumerate((gain_one, shift_one, gain_two, shift_two)):
        gnorm_o[k : k + 1, :] = jnp.sum(total, axis=0, keepdims=True)
    gnorm_o[4:8, :] = jnp.zeros((4, width), F32)

    gout = mm(jnp.transpose(mixed[...]), low_s[...])
    if places is None:
        gout_o[...] = gout.astype(BF16)
    else:
        g_s[0] = gout.astype(BF16)
        for g in range(groups):
            put(g, 2 * per, out_per, g_s.at[0], g * LANES)
    gm = mm(low_s[...], out_s[...], NT).astype(BF16)
    for g in range(groups):
        gm_o[g] = gm[:, g * LANES : (g + 1) * LANES]


def attention_back_kernel(fast, scal, hid, qkv_h, pt_h, gm, w_h, gone, gnorm, *rest):
    gi_k, gi_1, gi_x = rest[:3]
    if fast:
        chunks_o = rest[3:7]
        rest = rest[7:]
    else:
        gattn_o, gpos_o = rest[3:5]
        rest = rest[5:]
    ht_s, ds_s, dqkv_s, acc_s, g_s, qkv, pt, w, sems = rest
    me_dp, me_t = scal[0], scal[1]
    win, width = hid.shape
    groups = w.shape[1] // (3 * LANES)
    heads = by_head(win)
    arriving = []
    for g in range(groups):
        lanes = slice(g * 3 * LANES, (g + 1) * 3 * LANES)
        arriving.append(pltpu.make_async_copy(qkv_h.at[:, lanes], qkv.at[:, lanes], sems.at[len(arriving)]))
        for n in range(g * len(heads), (g + 1) * len(heads)):
            for j in range(win // QUERIES):
                ext = (j + 1) * QUERIES
                cols = slice(j * QUERIES, ext)
                arriving.append(pltpu.make_async_copy(pt_h.at[n, :ext, cols], pt.at[n, :ext, cols], sems.at[len(arriving)]))
    arriving.append(pltpu.make_async_copy(w_h, w, sems.at[len(arriving)]))
    for copy in arriving:
        copy.start()
    ht_s[...] = jnp.transpose(hid[...].astype(BF16))
    for g in range(groups):
        at = g * 3 * LANES
        per_group = 1 + len(heads) * (win // QUERIES)
        for copy in arriving[g * per_group : (g + 1) * per_group]:
            copy.wait()
        q = qkv[:, at : at + LANES]
        k = qkv[:, at + LANES : at + 2 * LANES]
        v = qkv[:, at + 2 * LANES : at + 3 * LANES]
        d_mixed = gm[g]
        for j in range(win // QUERIES):
            ext = (j + 1) * QUERIES
            cols = slice(j * QUERIES, ext)
            dq = jnp.zeros((QUERIES, LANES), F32)
            for h, only in enumerate(heads):
                p = pt[len(heads) * g + h, :ext, cols].astype(F32)
                dp = mm(v[:ext], only(d_mixed)[cols], NT)
                ds = (p * (dp - jnp.sum(p * dp, axis=0, keepdims=True))).astype(BF16)
                ds_s[len(heads) * g + h, :ext, cols] = ds
                dq += mm(ds, only(k)[:ext], TN)
            dqkv_s[cols, at : at + LANES] = (dq * HD**-0.5).astype(BF16)
        for i in range(win // QUERIES):
            rows = slice(i * QUERIES, (i + 1) * QUERIES)
            dk = jnp.zeros((QUERIES, LANES), F32)
            dv = jnp.zeros((QUERIES, LANES), F32)
            for h, only in enumerate(heads):
                dk += mm(ds_s[len(heads) * g + h, rows, i * QUERIES :], only(q)[i * QUERIES :])
                dv += mm(pt[len(heads) * g + h, rows, i * QUERIES :], only(d_mixed)[i * QUERIES :])
            dqkv_s[rows, at + LANES : at + 2 * LANES] = dk.astype(BF16)
            dqkv_s[rows, at + 2 * LANES : at + 3 * LANES] = dv.astype(BF16)
    arriving[-1].wait()
    acc_s[...] = gone[...] + mm(dqkv_s[...], w[...], NT)

    put_blocks(me_t, acc_s, gi_k, gi_1, gi_x)
    if not fast:
        for g in range(groups):
            gattn_o[g] = mm(ht_s[...], dqkv_s[:, g * 3 * LANES : (g + 1) * 3 * LANES]).astype(BF16)
        gpos_o[...] = acc_s[...].astype(BF16)
        return
    n_dp = chunks_o[0].shape[0]
    per = width // n_dp
    pos_per = win // (n_dp * groups)
    for g in range(groups):
        g_s[g % 2] = mm(ht_s[...], dqkv_s[:, g * 3 * LANES : (g + 1) * 3 * LANES]).astype(BF16)
        for r in range(n_dp):
            d = r ^ me_dp
            ref, slot = chunk_of(chunks_o, g, r)
            for t in range(3):
                ref[slot, t * per : (t + 1) * per, :] = g_s[g % 2, rows_at(d * per, per, per), t * LANES : (t + 1) * LANES]
            where = (me_t ^ g) * (win // groups) + d * pos_per
            for k in range(width // LANES):
                at = 3 * per + k * pos_per
                ref[slot, at : at + pos_per, :] = acc_s[rows_at(where, pos_per, pos_per), k * LANES : (k + 1) * LANES].astype(BF16)
            at = 3 * per + width // LANES * pos_per
            tile = gnorm[0:8, rows_at((d >> 1) * LANES, LANES, LANES)]
            ref[slot, at : at + 16, :] = jnp.concatenate([tile, tile], axis=0).astype(BF16)


def near_kernel(rest, got, x, y, x2, y2, own, far, odd):
    own[...] = total(rest[0], got[0], x[0], x2[0])
    far[...] = total(rest[4], got[4], y[0], y2[0])
    odd[0] = low(rest[1], got[1], x[1], x2[1])
    odd[1] = low(rest[5], got[5], y[1], y2[1])


def second_kernel(done, rest, got, x, y, a, b):
    del done
    for i in range(2):
        a[i] = low(rest[2 + i], got[2 + i], x[2 + i])
        b[i] = low(rest[6 + i], got[6 + i], y[2 + i])


def far_kernel(own, far, near, own_o, far_o):
    own_o[...] = total(own[...], near[0])
    far_o[0] = low(far[...], near[1])


def far_near_kernel(own, far, near, rest, got, x, y, x2, y2, own_o, far_o, *others):
    far_kernel(own, far, near, own_o, far_o)
    near_kernel(rest, got, x, y, x2, y2, *others)


def update(refs, gradient, rate, decay):
    weight, one, two, new_weight, new_one, new_two = refs
    new_weight[...], new_one[...], new_two[...] = adam_step(weight[...], gradient, one[...], two[...], rate, decay)


def rows_update_kernel(which, own, far, *refs):
    n = len(which)
    *refs, token = refs
    token[...] = jnp.zeros_like(token)
    grad = total(own[...], far[0])
    at = 0
    for i, index in enumerate(which):
        height = refs[i].shape[0]
        update(refs[i :: n], grad[at : at + height], RATES[index], DECAYS[index])
        at += height


def tiles_update_kernel(scal, done, own, far, *refs):
    *refs, token = refs
    token[...] = done[...]
    attn, pos, norm = refs[0::3], refs[1::3], refs[2::3]
    grad = total(own[...], far[0])
    per = attn[0].shape[1]
    pos_per, width = pos[0].shape
    update(attn, grad[: 3 * per].reshape(attn[0].shape), RATES[0], DECAYS[0])
    at = 3 * per
    rows = [grad[at + k * pos_per : at + (k + 1) * pos_per] for k in range(width // LANES)]
    update(pos, jnp.concatenate(rows, axis=1), RATES[4], DECAYS[4])
    at += width // LANES * pos_per
    tile = grad[at : at + 8]
    half = jnp.where((scal[0] & 1) == 1, tile[:4, LANES // 2 :], tile[:4, : LANES // 2])
    update(norm, half, RATES[5], DECAYS[5])


def finish_kernel(scal, done, res_k, gi_k, res_1, gi_1, r2, r3, res_o, gi_o, gi_s, sems):
    del done
    me_t = scal[1]
    moves = [(gi_k, gi_o.at[me_t])]
    moves += [(res, res_o.at[me_t ^ r]) for r, res in enumerate((res_k, res_1.at[0], r2.at[0], r3.at[0]))]
    copies = copies_in(moves, sems)
    for r, gi in ((1, gi_1.at[0]), (2, r2.at[1]), (3, r3.at[1])):
        gi_s[r - 1] = gi[...].astype(F32)
        copies.append(pltpu.make_async_copy(gi_s.at[r - 1], gi_o.at[me_t ^ r], sems.at[4 + r]))
        copies[-1].start()
    for copy in copies:
        copy.wait()


def after(value, *others):
    return lax.optimization_barrier((value, *others))[0]


def stacked(q, got):
    out = jax.ShapeDtypeStruct((2 * q.shape[0], *q.shape[1:]), q.dtype)
    return call(stack_kernel, [out], [], [q, got], "vv", 6, 1_000)[0]


def gather_z(value, *others):
    nz = lax.axis_size("dp") // 2
    q, order = value, [0]
    step = nz // 2
    while step:
        if step == 1:
            q = after(q, *others)
        q = stacked(q, swap(q, step * 2, 0))
        order = order + [z ^ step for z in order]
        step //= 2
    return q, tuple(order)


def gather_xy(q, order, qx=None, qy=None, *others):
    half = len(order) // 2
    if qx is None:
        qx, qy = swap(q, 0, 2), swap(q, 1, 0)
    a, b = after(qx[:half], *others), after(qy[half:], *others)
    return [(q, (0, 0, order)), (qx, (1, 0, order)), (qy, (0, 1, order)), (swap(a, 1, 0), (1, 1, order[:half])), (swap(b, 0, 2), (1, 1, order[half:]))]


def both_cores(found):
    out = []
    for array, place in found:
        out.append((array, (*place, 0)))
        out.append((swap(array, 0, 1), (*place, 1)))
    return [f[0] for f in out], tuple(f[1] for f in out)


class Reduction:
    def __init__(self, keep_first, keep_rest, send_first, send_rest):
        self.half = keep_first.shape[0] // 4
        self.n = keep_first.shape[0] // 2
        self.sums = [(keep_rest,)]
        self.send_rest = send_rest
        got = swap(send_first, 0, 1)
        self.a = low(keep_first[: self.n], got[: self.n])
        self.b = low(keep_first[self.n :], got[self.n :])

    def terms(self, a, start, stop):
        at = 0 if a else self.n
        found = [k[at + start : at + stop] for k in self.rest]
        for pair in self.got:
            g = pair[0 if a else 1]
            if g.shape[0] >= stop:
                found.append(g[start:stop])
        return found

    def first(self):
        self.rest = [self.sums[0][0], swap(self.send_rest, 0, 1)]
        self.got = [(swap(self.a, 0, 2), swap(self.b, 1, 0))]
        return self.got[0]

    def second(self, *others):
        h = self.half
        a, b = [after(low(*self.terms(part, h, 2 * h)), *others) for part in (True, False)]
        self.got.append((swap(a, 1, 0), swap(b, 0, 2)))
        return self.got[1]

    def over_z(self, *others):
        h = self.half
        arrived = []
        for z in range(1, 2 * h):
            chunk = low(*self.terms(z < h, z % h, z % h + 1))
            arrived.append(swap(after(chunk, *others), 2 * z, 0))
        return arrived

    def result(self, arrived):
        return total(*self.terms(True, 0, 1), *arrived)[0]


def call(kernel, outs, scratch, args, spaces, mib, flops):
    vmem = pl.BlockSpec(memory_space=pltpu.VMEM)
    args = [pltpu.with_memory_space_constraint(v, pltpu.HBM) if k == "h" else v for v, k in zip(args, spaces, strict=True)]
    kinds = {"s": pl.BlockSpec(memory_space=pltpu.SMEM), "v": vmem, "a": pl.BlockSpec(memory_space=pl.ANY), "h": pl.BlockSpec(memory_space=pltpu.HBM)}
    return pl.pallas_call(
        kernel,
        out_shape=outs,
        in_specs=[kinds[k] for k in spaces],
        out_specs=[vmem if isinstance(v, jax.ShapeDtypeStruct) else kinds["h"] for v in outs],
        scratch_shapes=[pltpu.VMEM(*s) if isinstance(s, tuple) else pltpu.SemaphoreType.DMA(tuple(s)) for s in scratch],
        compiler_params=pltpu.CompilerParams(vmem_limit_bytes=mib * 1024 * 1024),
        cost_estimate=pl.CostEstimate(flops=flops, bytes_accessed=0, transcendentals=0),
    )(*args)


def body(
    inputs,
    segment_ids,
    cotangent,
    attn_proj,
    out_proj,
    up_proj,
    down_proj,
    pos_table,
    norm_params,
    first_attn,
    second_attn,
    first_out,
    second_out,
    first_up,
    second_up,
    first_down,
    second_down,
    first_pos,
    second_pos,
    first_norm,
    second_norm,
):
    n_dp, n_t = lax.axis_size("dp"), lax.axis_size("tensor")
    me_dp, me_t = lax.axis_index("dp"), lax.axis_index("tensor")
    scal = jnp.stack([me_dp, me_t]).astype(jnp.int32)
    windows, block, width = inputs.shape
    win = block * n_t
    inner = up_proj.shape[1]
    group = attn_proj.shape[2]
    per, out_per, pos_per = attn_proj.shape[1], out_proj.shape[0], pos_table.shape[0]
    fast = out_per % 16 == 0 and pos_per % 16 == 0 and 2 * per == LANES and n_dp == 8 and n_t == 4
    sds = jax.ShapeDtypeStruct

    if fast:
        ga, gb, xs, c1, own = call(
            prepare_kernel,
            [
                sds((1, 3 * per + width // LANES * pos_per + 16, LANES), BF16),
                sds((1, 2 * per + out_per, width), BF16),
                sds((4, block, width), BF16),
                sds((2, block, width), BF16),
                sds((2, block, width), BF16),
            ],
            [(v.shape, F32) for v in (attn_proj, pos_table, norm_params, out_proj, up_proj, down_proj)] + [[14]],
            [scal, inputs, cotangent, attn_proj, pos_table, norm_params, out_proj, up_proj, down_proj],
            "s" + "h" * 8,
            8,
            1_000,
        )
        a2 = stacked(ga, swap(ga, 4, 0))
        qa, za = stacked(a2, swap(a2, 2, 0)), (0, 2, 1, 3)
        gb = after(gb, a2)
        rx = swap(xs, 0, 2)
        qb, zb = gather_z(gb, qa)
        c1 = swap(c1, 0, 1)
        c3 = swap(rx[2:], 0, 1)
        qax, qay, qaxy = swap(qa, 0, 2), swap(qa, 1, 0), swap(qa, 1, 2)
        a_args, a_places = both_cores([(qa, (0, 0, za)), (qax, (1, 0, za)), (qay, (0, 1, za)), (qaxy, (1, 1, za))])
        qb = after(qb, rx, qax, qay)
        qbx, qby = swap(qb, 0, 2), swap(qb, 1, 0)
    else:

        def pair(rel):
            return jnp.concatenate([lax.dynamic_slice_in_dim(v, me_t ^ rel, 1, 0) for v in (inputs, cotangent)])

        rx = swap(jnp.concatenate([pair(2), pair(3)]), 0, 2)
        own, c1 = pair(0), swap(pair(1), 0, 1)
        c3 = swap(rx[2:], 0, 1)
        relative = me_t ^ jnp.arange(n_t)
        whole = [lax.all_gather(lax.all_gather(v.astype(BF16), "dp"), "tensor") for v in (attn_proj, out_proj, up_proj, down_proj)]
        attn_w, out_w, up_w, down_w = [jnp.take(v, relative, axis=0) for v in whole]
        attn_w = attn_w.transpose(1, 3, 0, 2, 4).reshape(width, n_t * 3 * group)
        pos_w = lax.all_gather(lax.all_gather(pos_table.astype(BF16), "dp", axis=0, tiled=True), "tensor", axis=0, tiled=True)
        norm_w = lax.all_gather(norm_params, "dp", axis=1, tiled=True)
        norm_w = jnp.concatenate([norm_w, jnp.zeros_like(norm_w)])
        a_args, a_places = [attn_w, pos_w, norm_w], None
        b_args, b_places = [out_w.reshape(n_t * group, width), up_w.reshape(n_t, width, inner), down_w.reshape(n_t, inner, width)], None

    hid, qkv, pt, mixed, attn_all, norm_all = call(
        functools.partial(attention_kernel, a_places, len(a_args)),
        [
            sds((win, width), F32),
            pltpu.HBM((win, n_t * 3 * group), BF16),
            pltpu.HBM((n_t * group // HD, win, win), BF16),
            sds((win, n_t * group), BF16),
            pltpu.HBM((width, n_t * 3 * group), BF16),
            sds((8, width), F32),
        ],
        [((win, width), BF16), ((win, width), BF16), ((win, win), F32), ((n_dp, 16, LANES), F32), ((width, n_t * 3 * group), BF16), ((win, n_t * 3 * group), BF16), ((n_t * group // HD, win, win), BF16), [32]],
        [scal, own, rx, c1, c3, segment_ids, *a_args],
        "svvvvv" + "v" * len(a_args),
        14,
        1_000_000,
    )
    if fast:
        b_args, b_places = both_cores(gather_xy(qb, zb, qbx, qby, hid))

    blocks = [sds((block, width), BF16), sds((1, block, width), BF16), sds((2, block, width), BF16)]
    if fast:
        rows_b = 2 * per + out_per
        grads_b = [sds((n_dp, rows_b, width), BF16)] * 4
    else:
        grads_b = [sds((n_t, width, inner), BF16), sds((n_t, inner, width), BF16), sds((n_t * group, width), BF16)]
    res_k, res_1, res_x, gone, gm, gnorm, *got_b = call(
        functools.partial(ffn_kernel, b_places, len(b_args)),
        [*blocks, sds((win, width), F32), sds((n_t, win, group), BF16), sds((8, width), F32), *grads_b],
        [
            ((win, width), BF16),
            ((n_t * group, width), BF16),
            ((n_t, width, inner), BF16),
            ((n_t, inner, width), BF16),
            ((2, win, width), F32),
            ((win, width), F32),
            ((2, win, width), BF16),
            ((win, width), F32),
            ((win, LANES), F32),
            ((win, width), F32),
            ((win, width), BF16),
            ((n_t, win, inner), BF16),
            ((n_t, win, inner), F32),
            ((win, width), BF16),
            ((width, win), BF16),
        ],
        [scal, own, rx, c1, c3, hid, mixed, norm_all, *b_args],
        "svvvvvvv" + "v" * len(b_args),
        26,
        1_000_000,
    )
    if fast:
        red_b = Reduction(*got_b)
        gone = after(gone, red_b.a, red_b.b)
        first_b = red_b.first()

    blocks = [sds((block, width), F32), *blocks[1:]]
    if fast:
        rows_a = 3 * per + width // LANES * pos_per + 16
        grads_a = [sds((n_dp, rows_a, LANES), BF16)] * 4
    else:
        grads_a = [sds((n_t, width, 3 * group), BF16), sds((win, width), BF16)]
    gi_k, gi_1, gi_x, *got_a = call(
        functools.partial(attention_back_kernel, fast),
        [*blocks, *grads_a],
        [
            ((width, win), BF16),
            ((n_t * group // HD, win, win), BF16),
            ((win, n_t * 3 * group), BF16),
            ((win, width), F32),
            ((2, width, 3 * group), BF16),
            ((win, n_t * 3 * group), BF16),
            ((n_t * group // HD, win, win), BF16),
            ((width, n_t * 3 * group), BF16),
            [1 + n_t + 2 * n_t * group // HD],
        ],
        [scal, hid, qkv, pt, gm, attn_all, gone, gnorm],
        "svhhvhvv",
        18,
        1_000_000,
    )
    leaving = [jnp.concatenate([res_x[i : i + 1], gi_x[i : i + 1]]) for i in range(2)]
    if fast:
        keep_first, keep_rest, send_first, send_rest = got_a
        red_a = Reduction(keep_first, keep_rest, send_first, send_rest)
        first_a, second_b = red_a.first(), red_b.second()
        chunk_b, chunk_a = got_b[0].shape[1:], got_a[0].shape[1:]
        before_z = [[sds(chunk, F32), sds(chunk, F32), sds((2, *chunk), BF16)] for chunk in (chunk_b, chunk_a)]
        last = [[sds(chunk, F32), sds((1, *chunk), BF16)] for chunk in (chunk_b, chunk_a)]
        own_b, far_b, odd_b = call(near_kernel, before_z[0], [], [*red_b.rest, *first_b, *second_b], "v" * 6, 8, 1_000)
        a_y, a_x = call(second_kernel, [sds((2, *chunk_a), BF16)] * 2, [], [own_b, *red_a.rest, *first_a], "avvvv", 8, 1_000)
        second_a = swap(a_y, 1, 0), swap(a_x, 0, 2)
        near_b = swap(odd_b, 2, 0)
        own_b, far_b, own_a, far_a, odd_a = call(
            far_near_kernel,
            last[0] + before_z[1],
            [],
            [own_b, far_b, near_b, *red_a.rest, *first_a, *second_a],
            "v" * 9,
            8,
            1_000,
        )
        far_b = swap(far_b, 4, 0)
        r2, r3 = [swap(after(v, own_a), 0, m) for v, m in zip(leaving, (2, 3), strict=True)]
        own_a, far_a = call(far_kernel, last[1], [], [own_a, far_a, swap(odd_a, 2, 0)], "vvv", 4, 1_000)
        far_a = swap(far_a, 4, 0)
    else:
        r2, r3 = [swap(v, 0, m) for v, m in zip(leaving, (2, 3), strict=True)]
    r1 = [swap(res_1, 0, 1), swap(gi_1, 0, 1)]
    masters = (attn_proj, out_proj, up_proj, down_proj, pos_table, norm_params)
    firsts = (first_attn, first_out, first_up, first_down, first_pos, first_norm)
    seconds = (second_attn, second_out, second_up, second_down, second_pos, second_norm)
    updated = [None] * 6
    token = sds((8, LANES), F32)
    done = jnp.zeros(token.shape, F32)
    if fast:
        which = (2, 3, 1)
        state = [group[i] for group in (masters, firsts, seconds) for i in which]
        new = call(
            functools.partial(rows_update_kernel, which),
            [sds(v.shape, F32) for v in state] + [token],
            [],
            [own_b, far_b, *state],
            "v" * 11,
            8,
            2_000_000_000,
        )
        for i, index in enumerate(which):
            updated[index] = new[i:9:3]
        done = new[9]
    if fast:
        which = (0, 4, 5)
        state = [group[i] for group in (masters, firsts, seconds) for i in which]
        new = call(
            tiles_update_kernel,
            [sds(v.shape, F32) for v in state] + [token],
            [],
            [scal, done, own_a, far_a, *state],
            "sv" + "v" * 11,
            8,
            1_000_000,
        )
        for i, index in enumerate(which):
            updated[index] = new[i:9:3]
        done = new[9]
    outputs, grad_input = call(
        finish_kernel,
        [pltpu.HBM(inputs.shape, BF16), pltpu.HBM(inputs.shape, F32)],
        [((3, block, width), F32), [8]],
        [scal, done, res_k, gi_k, *r1, r2, r3],
        "sv" + "v" * 6,
        8,
        1_000,
    )
    if not fast:

        def reduced(value, own_axis):
            arrived = lax.all_to_all(value, "dp", split_axis=0, concat_axis=0, tiled=True)
            part = arrived.astype(F32).sum(axis=0).astype(BF16)
            arrived = lax.all_to_all(part, "tensor", split_axis=0, concat_axis=0, tiled=True)
            return arrived.astype(F32).sum(axis=0)

        gup, gdown, gout = got_b
        gattn, gpos = got_a
        gup, gdown, gout, gattn = [jnp.take(v, relative, axis=0) for v in (gup, gdown, gout.reshape(n_t, group, width), gattn)]
        g_up = reduced(gup.reshape(n_t, n_dp, per, inner).swapaxes(0, 1), 0)
        g_down = reduced(gdown.reshape(n_t, n_dp, inner // n_dp, width).swapaxes(0, 1), 0)
        g_out = reduced(gout.reshape(n_t, n_dp, out_per, width).swapaxes(0, 1), 0)
        g_pos = reduced(gpos.reshape(n_t, n_dp, pos_per, width).swapaxes(0, 1), 0)
        g_attn = reduced(gattn.reshape(n_t, n_dp, per, 3, group).swapaxes(0, 1), 0).swapaxes(0, 1)
        cut = gnorm[:4].reshape(4, n_dp, width // n_dp).swapaxes(0, 1).astype(BF16)
        g_norm = reduced(jnp.broadcast_to(cut[:, None], (n_dp, n_t, *cut.shape[1:])), 0)

        gradients = (g_attn, g_out, g_up, g_down, g_pos, g_norm)
        for index in range(6):
            updated[index] = adam_step(masters[index], gradients[index], firsts[index], seconds[index], RATES[index], DECAYS[index])
    return (outputs, grad_input, *[v for new in updated for v in new])


def solution(mesh):
    acts = P("dp", "tensor", None)
    attn = P(None, "dp", "tensor")
    both = P(("tensor", "dp"), None)
    up = P("dp", "tensor")
    norm = P(None, "dp")
    return jax.shard_map(
        body,
        mesh=mesh,
        in_specs=(acts, P("dp", None), acts, attn, both, up, both, both, norm, *(attn,) * 2, *(both,) * 2, *(up,) * 2, *(both,) * 4, *(norm,) * 2),
        out_specs=(acts, acts, *(attn,) * 3, *(both,) * 3, *(up,) * 3, *(both,) * 6, *(norm,) * 3),
        check_vma=False,
    )
```

```python
import functools

import jax
import jax.numpy as jnp
from jax import lax
from jax.experimental import pallas as pl
from jax.experimental.pallas import tpu as pltpu
from jax.sharding import PartitionSpec as P

HD = 64
STEP = 10
LANES = 128

NORM_EPS = 1e-05
NEG_FILL = -1e30
BETA_ONE = 0.9
BETA_TWO = 0.95
ADAM_EPS = 1e-08
RATES = (0.03, 0.2, 0.03, 0.02, 0.3, 0.3)
DECAYS = (0.1, 0.1, 0.1, 0.1, 0.1, 0.0)
GELU_A = 0.7978845608028654
GELU_B = 0.044715

F32 = jnp.float32
BF16 = jnp.bfloat16
AXES = ("dp", "tensor")

NN = (((1,), (0,)), ((), ()))
NT = (((1,), (1,)), ((), ()))
TN = (((0,), (0,)), ((), ()))
QUERIES = 256


def total(*parts):
    return sum(p.astype(F32) for p in parts)


def low(*parts):
    return total(*parts).astype(BF16)


def adam_step(weight, gradient, moment_one, second, step_rate, decay_rate):
    first_new = BETA_ONE * moment_one + (1.0 - BETA_ONE) * gradient
    second_new = BETA_TWO * second + (1.0 - BETA_TWO) * gradient * gradient
    fixed_first = first_new / (1.0 - BETA_ONE**STEP)
    fixed_second = second_new / (1.0 - BETA_TWO**STEP)
    weight_new = weight - step_rate * (fixed_first / (jnp.sqrt(fixed_second) + ADAM_EPS) + decay_rate * weight)
    return (weight_new, first_new, second_new)


def mm(a, b, dims=NN):
    return lax.dot_general(a, b, dims, preferred_element_type=F32)


def swap(value, rd, rt):
    n_t = lax.axis_size("tensor")
    mask = rd * n_t + rt
    return lax.ppermute(value, AXES, [(i, i ^ mask) for i in range(lax.axis_size("dp") * n_t)])


def rows_at(start, size, step):
    return pl.ds(pl.multiple_of(start, step), size)


def by_head(rows):
    lane = lax.broadcasted_iota(jnp.int32, (rows, LANES), 1)

    def keep(h):
        here = (lane >= h * HD) & (lane < (h + 1) * HD)
        return lambda v: jnp.where(here, v, jnp.zeros_like(v))

    return [keep(h) for h in range(LANES // HD)]


def fill_window(me_t, which, parts, out_ref):
    own, rx, c1, c3 = parts
    n = own.shape[1]
    for r, ref in enumerate((own, c1, rx, c3)):
        out_ref[rows_at((me_t ^ r) * n, n, n), :] = ref[which]


def copies_in(moves, sems):
    copies = [pltpu.make_async_copy(src, dst, sems.at[i]) for i, (src, dst) in enumerate(moves)]
    for copy in copies:
        copy.start()
    return copies


def prepare_kernel(scal, inputs, cot, attn, pos, norm, out, up, down, ga, gb, xs, c1, own, attn_s, pos_s, norm_s, out_s, up_s, down_s, sems):
    me_t = scal[1]
    moves = [(attn, attn_s), (pos, pos_s), (norm, norm_s), (up, up_s), (down, down_s), (out, out_s)]
    for rel, ref, at in ((2, xs, 0), (3, xs, 2), (1, c1, 0), (0, own, 0)):
        moves += [(inputs.at[me_t ^ rel], ref.at[at]), (cot.at[me_t ^ rel], ref.at[at + 1])]
    copies = copies_in(moves, sems)
    for copy in copies[:3]:
        copy.wait()
    per = attn.shape[1]
    pos_per = pos.shape[0]
    tiles = pos.shape[1] // LANES
    for t in range(3):
        ga[0, t * per : (t + 1) * per, :] = attn_s[t].astype(BF16)
    for k in range(tiles):
        at = 3 * per + k * pos_per
        ga[0, at : at + pos_per, :] = pos_s[:, k * LANES : (k + 1) * LANES].astype(BF16)
    at = 3 * per + tiles * pos_per
    both = norm_s[...]
    both = jnp.concatenate([both, both], axis=1)
    both = jnp.concatenate([both, jnp.zeros_like(both)], axis=0)
    high = both.astype(BF16)
    rest = (both - high.astype(F32)).astype(BF16)
    ga[0, at : at + 16, :] = jnp.concatenate([high, rest], axis=0)
    for copy in copies[3:6]:
        copy.wait()
    gb[0, 0:per, :] = up_s[...].astype(BF16)
    gb[0, per : 2 * per, :] = down_s[...].astype(BF16)
    gb[0, 2 * per :, :] = out_s[...].astype(BF16)
    for copy in copies[6:]:
        copy.wait()


def stack_kernel(own, got, both):
    n = own.shape[0]
    both[:n] = own[...]
    both[n:] = got[...]


def leaver(sems):
    leaving = []

    def leave(src, dst):
        leaving.append(pltpu.make_async_copy(src, dst, sems.at[len(leaving)]))
        leaving[-1].start()

    return leaving, leave


def attend(x, w, groups, bias, qkv_o, qkv_h, pt_o, pt_h, mix_o, leave):
    win = x.shape[0]
    heads = by_head(win)
    for g in groups:
        at = g * 3 * LANES
        qkv = mm(x[...], w[:, at : at + 3 * LANES]).astype(BF16)
        q = qkv[:, :LANES] * jnp.asarray(HD**-0.5, BF16)
        k = qkv[:, LANES : 2 * LANES]
        v = qkv[:, 2 * LANES :]
        qkv_o[:, at : at + LANES] = q
        qkv_o[:, at + LANES : at + 3 * LANES] = qkv[:, LANES:]
        leave(qkv_o.at[:, at : at + 3 * LANES], qkv_h.at[:, at : at + 3 * LANES])
        for j in range(win // QUERIES):
            ext = (j + 1) * QUERIES
            cols = slice(j * QUERIES, ext)
            mixed = jnp.zeros((QUERIES, LANES), F32)
            for h, only in enumerate(heads):
                s = mm(only(k)[:ext], q[cols], NT) + bias[:ext, cols]
                e = jnp.exp(s - jnp.max(s, axis=0, keepdims=True))
                p = (e * (1.0 / jnp.sum(e, axis=0, keepdims=True))).astype(BF16)
                pt_o[len(heads) * g + h, :ext, cols] = p
                mixed += mm(p, only(v)[:ext], TN)
            mix_o[cols, g * LANES : (g + 1) * LANES] = mixed.astype(BF16)
            for h in range(len(heads)):
                leave(pt_o.at[len(heads) * g + h, :ext, cols], pt_h.at[len(heads) * g + h, :ext, cols])


def attention_kernel(places, n_pieces, scal, *refs):
    own, rx, c1, c3, segs = refs[:5]
    pieces = refs[5 : 5 + n_pieces]
    hid_o, qkv_h, pt_h, mix_o, w_h, nrm_o, x_s, wlast_o, bias_s, pos_s, nrm_s, w_o, qkv_o, pt_o, out_sems = refs[5 + n_pieces :]
    leaving, leave = leaver(out_sems)
    me_dp, me_t = scal[0], scal[1]
    win, width = x_s.shape
    groups = w_o.shape[1] // (3 * LANES)
    fill_window(me_t, 0, (own, rx, c1, c3), x_s)
    if places is None:
        w_o[...] = pieces[0][...]
        pos_s[...] = pieces[1][...]
        nrm_o[...] = pieces[2][...]
    else:
        n_dp = nrm_s.shape[0]
        per = width // n_dp
        pos_per = win // (n_dp * groups)
        for ref, (xr, yr, zs, c) in zip(pieces, places, strict=True):
            tr = xr * 2 + c
            for i, zr in enumerate(zs):
                src = me_dp ^ (zr * 2 + yr)
                for t in range(3):
                    at = (tr * 3 + t) * LANES
                    w_o[rows_at(src * per, per, per), at : at + LANES] = ref[i, t * per : (t + 1) * per]
                where = (me_t ^ tr) * (win // groups) + src * pos_per
                for k in range(width // LANES):
                    at = 3 * per + k * pos_per
                    pos_s[rows_at(where, pos_per, pos_per), k * LANES : (k + 1) * LANES] = ref[i, at : at + pos_per]
                if tr == 0:
                    at = 3 * per + width // LANES * pos_per
                    nrm_s[src] = ref[i, at : at + 16].astype(F32)
        low_lane = lax.broadcasted_iota(jnp.int32, (8, LANES), 1) < per
        for j in range(n_dp // 2):
            left = nrm_s[2 * j]
            right = nrm_s[2 * j + 1]
            both = jnp.where(low_lane, left[0:8] + left[8:16], right[0:8] + right[8:16])
            nrm_o[:, j * LANES : (j + 1) * LANES] = both

    leave(w_o, w_h)

    seg = segs[pl.ds(me_t, 1), :].astype(F32)
    seg_col = jnp.transpose(jnp.broadcast_to(seg, (LANES, win)))
    for i in range(win // LANES):
        key_seg = seg_col[i * LANES : (i + 1) * LANES, 0:1]
        key_at = lax.broadcasted_iota(jnp.int32, (LANES, win), 0) + i * LANES
        query_at = lax.broadcasted_iota(jnp.int32, (LANES, win), 1)
        counts = (key_seg == seg) & (query_at >= key_at)
        bias_s[i * LANES : (i + 1) * LANES, :] = jnp.where(counts, 0.0, NEG_FILL)

    hidden = x_s[...].astype(F32) + pos_s[...].astype(F32)
    hid_o[...] = hidden
    x_s[...] = hidden.astype(BF16)
    first = qkv_o.shape[1] // (3 * LANES)
    attend(x_s, w_o, range(first), bias_s, qkv_o, qkv_h, pt_o, pt_h, mix_o, leave)
    wlast_o[...] = w_o[:, first * 3 * LANES :]
    for copy in leaving:
        copy.wait()


def attention_rest_kernel(x, w, bias, qkv_h, pt_h, mix_o, qkv_o, pt_o, out_sems):
    leaving, leave = leaver(out_sems)
    attend(x, w, range(w.shape[1] // (3 * LANES)), bias, qkv_o, qkv_h, pt_o, pt_h, mix_o, leave)
    for copy in leaving:
        copy.wait()


def norm_forward(v):
    center = v - jnp.mean(v, axis=-1, keepdims=True)
    rs = lax.rsqrt(jnp.mean(center * center, axis=-1, keepdims=True) + NORM_EPS)
    return center * rs, rs


def norm_backward(g, xhat, rs, gain):
    e = g * gain
    return rs * (e - jnp.mean(e, axis=-1, keepdims=True) - xhat * jnp.mean(e * xhat, axis=-1, keepdims=True))


def put_blocks(me_t, value, keep, s1, sx):
    n = keep.shape[0]
    for r, ref in ((0, keep), (1, s1.at[0]), (2, sx.at[0]), (3, sx.at[1])):
        ref[...] = value[rows_at((me_t ^ r) * n, n, n), :].astype(ref.dtype)


CHUNK = 128


def chunk_of(refs, tr, r):
    c, xr, yr, zr = tr & 1, tr >> 1, r & 1, r >> 1
    half = refs[0].shape[0] // 2
    if zr < half:
        kind, slot = (0, yr * half + zr) if xr == 1 else (2, yr * half + zr)
    else:
        kind, slot = (1, xr * half + zr - half) if yr == 1 else (2, 2 * half + xr * half + zr - half)
    return refs[3 * c + kind], slot


def ffn_kernel(places, n_pieces, scal, *refs):
    own, rx, c1, c3, hid, mixed_a, mixed_b, nrm = refs[:8]
    pieces = refs[8 : 8 + n_pieces]
    rest = refs[8 + n_pieces :]
    res_k, res_1, res_x, gone_o, gm_o, gnorm_o = rest[:6]
    if places is None:
        gup_o, gdown_o, gout_o = rest[6:9]
        rest = rest[9:]
    else:
        chunks_o = rest[6:12]
        rest = rest[12:]
    cot_s, out_s, up_s, down_s, a_s, b_s, g_s, xh1_s, r1_s, n1_s, sent_s, act_s, dg_s, low_s, xt_s, mixed = rest
    split = mixed_a.shape[1]
    mixed[:, :split] = mixed_a[...]
    mixed[:, split:] = mixed_b[...]
    me_dp, me_t = scal[0], scal[1]
    win, width = hid.shape
    groups = up_s.shape[0]
    fill_window(me_t, 1, (own, rx, c1, c3), cot_s)
    if places is None:
        n_dp = 1
        for src, dst in zip(pieces, (out_s, up_s, down_s), strict=True):
            dst[...] = src[...]
    else:
        n_dp = chunks_o[2].shape[0]
        per = width // n_dp
        out_per = LANES // n_dp
        for ref, (xr, yr, zs, c) in zip(pieces, places, strict=True):
            tr = xr * 2 + c
            for i, zr in enumerate(zs):
                src = me_dp ^ (zr * 2 + yr)
                up_s[tr, rows_at(src * per, per, per), :] = ref[i, 0:per]
                down_s[tr, rows_at(src * per, per, per), :] = ref[i, per : 2 * per]
                out_s[rows_at(tr * LANES + src * out_per, out_per, out_per), :] = ref[i, 2 * per : 2 * per + out_per]

    def chunks(fn):
        for i in range(win // CHUNK):
            fn(slice(i * CHUNK, (i + 1) * CHUNK))

    a_s[0] = mm(mixed[...], out_s[...])

    def norm_one(at):
        xhat, rs = norm_forward(hid[at, :] + a_s[0, at, :])
        xh1_s[at, :] = xhat
        r1_s[at, :] = jnp.broadcast_to(rs, (CHUNK, LANES))
        normed = xhat * nrm[0:1, :] + nrm[1:2, :]
        n1_s[at, :] = normed
        sent_s[at, :] = normed.astype(BF16)

    chunks(norm_one)

    for g in range(groups):
        a_s[g % 2] = mm(sent_s[...], up_s[g])

        def gelu(at, g=g):
            v = a_s[g % 2, at, :]
            square = v * v
            half = 0.5 + 0.5 * jnp.tanh(v * (GELU_A + GELU_A * GELU_B * square))
            act_s[g, at, :] = (v * half).astype(BF16)
            dg_s[g, at, :] = half + (half - half * half) * (v * (2.0 * GELU_A + 6.0 * GELU_A * GELU_B * square))

        chunks(gelu)
        n1_s[...] += mm(act_s[g], down_s[g])

    def norm_two(i, sums):
        at = slice(i * CHUNK, (i + 1) * CHUNK)
        xhat, rs = norm_forward(n1_s[at, :])
        n1_s[at, :] = xhat * nrm[2:3, :] + nrm[3:4, :]
        g = cot_s[at, :].astype(F32)
        grad = norm_backward(g, xhat, rs, nrm[2:3, :])
        b_s[at, :] = grad
        low_s[at, :] = grad.astype(BF16)
        return (sums[0] + jnp.sum((g * xhat).reshape(-1, 8, width), axis=0), sums[1] + jnp.sum(g.reshape(-1, 8, width), axis=0))

    def every(step):
        sums = (jnp.zeros((8, width), F32),) * 2
        for i in range(win // CHUNK):
            sums = step(i, sums)
        return sums

    gain_two, shift_two = every(norm_two)
    put_blocks(me_t, n1_s, res_k, res_1, res_x)

    def put(g, first, height, source, base):
        for r in range(n_dp):
            ref, slot = chunk_of(chunks_o, g, r)
            ref[slot, first : first + height, :] = source[rows_at(base + (r ^ me_dp) * height, height, height), :]

    xt_s[...] = jnp.transpose(sent_s[...])
    for g in range(groups):
        gdown = mm(jnp.transpose(act_s[g]), low_s[...])
        if places is None:
            gdown_o[g] = gdown.astype(BF16)
        else:
            g_s[0] = gdown.astype(BF16)
            put(g, per, per, g_s.at[0], 0)
        act_s[g] = (mm(low_s[...], down_s[g], NT) * dg_s[g]).astype(BF16)
        gup = mm(xt_s[...], act_s[g])
        if places is None:
            gup_o[g] = gup.astype(BF16)
        else:
            g_s[1] = gup.astype(BF16)
            put(g, 0, per, g_s.at[1], 0)
        b_s[...] += mm(act_s[g], up_s[g], NT)

    def norm_one_back(i, sums):
        at = slice(i * CHUNK, (i + 1) * CHUNK)
        g = b_s[at, :]
        xhat = xh1_s[at, :]
        grad = norm_backward(g, xhat, r1_s[at, 0:1], nrm[0:1, :])
        gone_o[at, :] = grad
        low_s[at, :] = grad.astype(BF16)
        return (sums[0] + jnp.sum((g * xhat).reshape(-1, 8, width), axis=0), sums[1] + jnp.sum(g.reshape(-1, 8, width), axis=0))

    gain_one, shift_one = every(norm_one_back)
    for k, total in enumerate((gain_one, shift_one, gain_two, shift_two)):
        gnorm_o[k : k + 1, :] = jnp.sum(total, axis=0, keepdims=True)
    gnorm_o[4:8, :] = jnp.zeros((4, width), F32)

    gout = mm(jnp.transpose(mixed[...]), low_s[...])
    if places is None:
        gout_o[...] = gout.astype(BF16)
    else:
        g_s[0] = gout.astype(BF16)
        for g in range(groups):
            put(g, 2 * per, out_per, g_s.at[0], g * LANES)
    gm = mm(low_s[...], out_s[...], NT).astype(BF16)
    for g in range(groups):
        gm_o[g] = gm[:, g * LANES : (g + 1) * LANES]


def attention_back_kernel(fast, scal, hid, qkv_a, qkv_b, pt_a, pt_b, gm, w_h, gone, gnorm, *rest):
    gi_k, gi_1, gi_x = rest[:3]
    if fast:
        chunks_o = rest[3:9]
        rest = rest[9:]
    else:
        gattn_o, gpos_o = rest[3:5]
        rest = rest[5:]
    ht_s, ds_s, dqkv_s, acc_s, g_s, qkv, pt, w, sems = rest
    me_dp, me_t = scal[0], scal[1]
    win, width = hid.shape
    groups = w.shape[1] // (3 * LANES)
    heads = by_head(win)
    arriving = []
    for g in range(groups):
        first = qkv_a.shape[1] // (3 * LANES)
        qkv_h, pt_h, base = (qkv_a, pt_a, 0) if g < first else (qkv_b, pt_b, first)
        lanes = slice(g * 3 * LANES, (g + 1) * 3 * LANES)
        there = slice((g - base) * 3 * LANES, (g - base + 1) * 3 * LANES)
        arriving.append(pltpu.make_async_copy(qkv_h.at[:, there], qkv.at[:, lanes], sems.at[len(arriving)]))
        for n in range(g * len(heads), (g + 1) * len(heads)):
            for j in range(win // QUERIES):
                ext = (j + 1) * QUERIES
                cols = slice(j * QUERIES, ext)
                arriving.append(pltpu.make_async_copy(pt_h.at[n - base * len(heads), :ext, cols], pt.at[n, :ext, cols], sems.at[len(arriving)]))
    arriving.append(pltpu.make_async_copy(w_h, w, sems.at[len(arriving)]))
    for copy in arriving:
        copy.start()
    ht_s[...] = jnp.transpose(hid[...].astype(BF16))
    for g in range(groups):
        at = g * 3 * LANES
        per_group = 1 + len(heads) * (win // QUERIES)
        for copy in arriving[g * per_group : (g + 1) * per_group]:
            copy.wait()
        q = qkv[:, at : at + LANES]
        k = qkv[:, at + LANES : at + 2 * LANES]
        v = qkv[:, at + 2 * LANES : at + 3 * LANES]
        d_mixed = gm[g]
        for j in range(win // QUERIES):
            ext = (j + 1) * QUERIES
            cols = slice(j * QUERIES, ext)
            dq = jnp.zeros((QUERIES, LANES), F32)
            for h, only in enumerate(heads):
                p = pt[len(heads) * g + h, :ext, cols].astype(F32)
                dp = mm(v[:ext], only(d_mixed)[cols], NT)
                ds = (p * (dp - jnp.sum(p * dp, axis=0, keepdims=True))).astype(BF16)
                ds_s[len(heads) * g + h, :ext, cols] = ds
                dq += mm(ds, only(k)[:ext], TN)
            dqkv_s[cols, at : at + LANES] = (dq * HD**-0.5).astype(BF16)
        for i in range(win // QUERIES):
            rows = slice(i * QUERIES, (i + 1) * QUERIES)
            dk = jnp.zeros((QUERIES, LANES), F32)
            dv = jnp.zeros((QUERIES, LANES), F32)
            for h, only in enumerate(heads):
                dk += mm(ds_s[len(heads) * g + h, rows, i * QUERIES :], only(q)[i * QUERIES :])
                dv += mm(pt[len(heads) * g + h, rows, i * QUERIES :], only(d_mixed)[i * QUERIES :])
            dqkv_s[rows, at + LANES : at + 2 * LANES] = dk.astype(BF16)
            dqkv_s[rows, at + 2 * LANES : at + 3 * LANES] = dv.astype(BF16)
    arriving[-1].wait()
    acc_s[...] = gone[...] + mm(dqkv_s[...], w[...], NT)

    put_blocks(me_t, acc_s, gi_k, gi_1, gi_x)
    if not fast:
        for g in range(groups):
            gattn_o[g] = mm(ht_s[...], dqkv_s[:, g * 3 * LANES : (g + 1) * 3 * LANES]).astype(BF16)
        gpos_o[...] = acc_s[...].astype(BF16)
        return
    n_dp = chunks_o[2].shape[0]
    per = width // n_dp
    pos_per = win // (n_dp * groups)
    for g in range(groups):
        g_s[g % 2] = mm(ht_s[...], dqkv_s[:, g * 3 * LANES : (g + 1) * 3 * LANES]).astype(BF16)
        for r in range(n_dp):
            d = r ^ me_dp
            ref, slot = chunk_of(chunks_o, g, r)
            for t in range(3):
                ref[slot, t * per : (t + 1) * per, :] = g_s[g % 2, rows_at(d * per, per, per), t * LANES : (t + 1) * LANES]
            where = (me_t ^ g) * (win // groups) + d * pos_per
            for k in range(width // LANES):
                at = 3 * per + k * pos_per
                ref[slot, at : at + pos_per, :] = acc_s[rows_at(where, pos_per, pos_per), k * LANES : (k + 1) * LANES].astype(BF16)
            at = 3 * per + width // LANES * pos_per
            tile = gnorm[0:8, rows_at((d >> 1) * LANES, LANES, LANES)]
            ref[slot, at : at + 16, :] = jnp.concatenate([tile, tile], axis=0).astype(BF16)


def near_kernel(rest, got, x, y, x2, y2, own, far, odd):
    own[...] = total(rest[0], got[0], x[0], x2[0])
    far[...] = total(rest[4], got[4], y[0], y2[0])
    odd[0] = low(rest[1], got[1], x[1], x2[1])
    odd[1] = low(rest[5], got[5], y[1], y2[1])


def second_kernel(done, rest, got, x, y, a, b):
    del done
    for i in range(2):
        a[i] = low(rest[2 + i], got[2 + i], x[2 + i])
        b[i] = low(rest[6 + i], got[6 + i], y[2 + i])


def far_kernel(own, far, near, own_o, far_o):
    own_o[...] = total(own[...], near[0])
    far_o[0] = low(far[...], near[1])


def far_near_kernel(own, far, near, rest, got, x, y, x2, y2, own_o, far_o, *others):
    far_kernel(own, far, near, own_o, far_o)
    near_kernel(rest, got, x, y, x2, y2, *others)


def update(refs, gradient, rate, decay):
    weight, one, two, new_weight, new_one, new_two = refs
    new_weight[...], new_one[...], new_two[...] = adam_step(weight[...], gradient, one[...], two[...], rate, decay)


def rows_update_kernel(which, own, far, *refs):
    n = len(which)
    *refs, token = refs
    token[...] = jnp.zeros_like(token)
    grad = total(own[...], far[0])
    at = 0
    for i, index in enumerate(which):
        height = refs[i].shape[0]
        update(refs[i :: n], grad[at : at + height], RATES[index], DECAYS[index])
        at += height


def tiles_update_kernel(scal, done, own, far, *refs):
    *refs, token = refs
    token[...] = done[...]
    attn, pos, norm = refs[0::3], refs[1::3], refs[2::3]
    grad = total(own[...], far[0])
    per = attn[0].shape[1]
    pos_per, width = pos[0].shape
    update(attn, grad[: 3 * per].reshape(attn[0].shape), RATES[0], DECAYS[0])
    at = 3 * per
    rows = [grad[at + k * pos_per : at + (k + 1) * pos_per] for k in range(width // LANES)]
    update(pos, jnp.concatenate(rows, axis=1), RATES[4], DECAYS[4])
    at += width // LANES * pos_per
    tile = grad[at : at + 8]
    half = jnp.where((scal[0] & 1) == 1, tile[:4, LANES // 2 :], tile[:4, : LANES // 2])
    update(norm, half, RATES[5], DECAYS[5])


def finish_kernel(scal, done, res_k, gi_k, res_1, gi_1, r2, r3, res_o, gi_o, gi_s, sems):
    del done
    me_t = scal[1]
    moves = [(gi_k, gi_o.at[me_t])]
    moves += [(res, res_o.at[me_t ^ r]) for r, res in enumerate((res_k, res_1.at[0], r2.at[0], r3.at[0]))]
    copies = copies_in(moves, sems)
    for r, gi in ((1, gi_1.at[0]), (2, r2.at[1]), (3, r3.at[1])):
        gi_s[r - 1] = gi[...].astype(F32)
        copies.append(pltpu.make_async_copy(gi_s.at[r - 1], gi_o.at[me_t ^ r], sems.at[4 + r]))
        copies[-1].start()
    for copy in copies:
        copy.wait()


def after(value, *others):
    return lax.optimization_barrier((value, *others))[0]


def stacked(q, got):
    out = jax.ShapeDtypeStruct((2 * q.shape[0], *q.shape[1:]), q.dtype)
    return call(stack_kernel, [out], [], [q, got], "vv", 6, 1_000)[0]


def gather_z(value, *others):
    nz = lax.axis_size("dp") // 2
    q, order = value, [0]
    step = nz // 2
    while step:
        if step == 1:
            q = after(q, *others)
        q = stacked(q, swap(q, step * 2, 0))
        order = order + [z ^ step for z in order]
        step //= 2
    return q, tuple(order)


def gather_xy(q, order, qx=None, qy=None, *others):
    half = len(order) // 2
    if qx is None:
        qx, qy = swap(q, 0, 2), swap(q, 1, 0)
    a, b = after(qx[:half], *others), after(qy[half:], *others)
    return [(q, (0, 0, order)), (qx, (1, 0, order)), (qy, (0, 1, order)), (swap(a, 1, 0), (1, 1, order[:half])), (swap(b, 0, 2), (1, 1, order[half:]))]


def both_cores(found):
    out = []
    for array, place in found:
        out.append((array, (*place, 0)))
        out.append((swap(array, 0, 1), (*place, 1)))
    return [f[0] for f in out], tuple(f[1] for f in out)


class Reduction:
    def __init__(self, keep_a, keep_b, keep_rest, send_a, send_b, send_rest):
        self.half = keep_a.shape[0] // 2
        self.n = keep_a.shape[0]
        self.sums = [(keep_rest,)]
        self.send_rest = send_rest
        got_a, got_b = swap(send_a, 0, 1), swap(send_b, 0, 1)
        self.a, self.b = low(keep_a, got_a), low(keep_b, got_b)

    def terms(self, a, start, stop):
        at = 0 if a else self.n
        found = [k[at + start : at + stop] for k in self.rest]
        for pair in self.got:
            g = pair[0 if a else 1]
            if g.shape[0] >= stop:
                found.append(g[start:stop])
        return found

    def first(self):
        self.rest = [self.sums[0][0], swap(self.send_rest, 0, 1)]
        self.got = [(swap(self.a, 0, 2), swap(self.b, 1, 0))]
        return self.got[0]

    def second(self, *others):
        h = self.half
        a, b = [after(low(*self.terms(part, h, 2 * h)), *others) for part in (True, False)]
        self.got.append((swap(a, 1, 0), swap(b, 0, 2)))
        return self.got[1]

    def over_z(self, *others):
        h = self.half
        arrived = []
        for z in range(1, 2 * h):
            chunk = low(*self.terms(z < h, z % h, z % h + 1))
            arrived.append(swap(after(chunk, *others), 2 * z, 0))
        return arrived

    def result(self, arrived):
        return total(*self.terms(True, 0, 1), *arrived)[0]


def call(kernel, outs, scratch, args, spaces, mib, flops):
    vmem = pl.BlockSpec(memory_space=pltpu.VMEM)
    args = [pltpu.with_memory_space_constraint(v, pltpu.HBM) if k == "h" else v for v, k in zip(args, spaces, strict=True)]
    kinds = {"s": pl.BlockSpec(memory_space=pltpu.SMEM), "v": vmem, "a": pl.BlockSpec(memory_space=pl.ANY), "h": pl.BlockSpec(memory_space=pltpu.HBM)}
    return pl.pallas_call(
        kernel,
        out_shape=outs,
        in_specs=[kinds[k] for k in spaces],
        out_specs=[vmem if isinstance(v, jax.ShapeDtypeStruct) else kinds["h"] for v in outs],
        scratch_shapes=[pltpu.VMEM(*s) if isinstance(s, tuple) else pltpu.SemaphoreType.DMA(tuple(s)) for s in scratch],
        compiler_params=pltpu.CompilerParams(vmem_limit_bytes=mib * 1024 * 1024),
        cost_estimate=pl.CostEstimate(flops=flops, bytes_accessed=0, transcendentals=0),
    )(*args)


def body(
    inputs,
    segment_ids,
    cotangent,
    attn_proj,
    out_proj,
    up_proj,
    down_proj,
    pos_table,
    norm_params,
    first_attn,
    second_attn,
    first_out,
    second_out,
    first_up,
    second_up,
    first_down,
    second_down,
    first_pos,
    second_pos,
    first_norm,
    second_norm,
):
    n_dp, n_t = lax.axis_size("dp"), lax.axis_size("tensor")
    me_dp, me_t = lax.axis_index("dp"), lax.axis_index("tensor")
    scal = jnp.stack([me_dp, me_t]).astype(jnp.int32)
    windows, block, width = inputs.shape
    win = block * n_t
    inner = up_proj.shape[1]
    group = attn_proj.shape[2]
    per, out_per, pos_per = attn_proj.shape[1], out_proj.shape[0], pos_table.shape[0]
    fast = out_per % 16 == 0 and pos_per % 16 == 0 and 2 * per == LANES and n_dp == 8 and n_t == 4
    sds = jax.ShapeDtypeStruct

    if fast:
        ga, gb, xs, c1, own = call(
            prepare_kernel,
            [
                sds((1, 3 * per + width // LANES * pos_per + 16, LANES), BF16),
                sds((1, 2 * per + out_per, width), BF16),
                sds((4, block, width), BF16),
                sds((2, block, width), BF16),
                sds((2, block, width), BF16),
            ],
            [(v.shape, F32) for v in (attn_proj, pos_table, norm_params, out_proj, up_proj, down_proj)] + [[14]],
            [scal, inputs, cotangent, attn_proj, pos_table, norm_params, out_proj, up_proj, down_proj],
            "s" + "h" * 8,
            8,
            1_000,
        )
        a2 = stacked(ga, swap(ga, 4, 0))
        qa, za = stacked(a2, swap(a2, 2, 0)), (0, 2, 1, 3)
        gb = after(gb, a2)
        rx = swap(xs, 0, 2)
        qb, zb = gather_z(gb, qa)
        c1 = swap(c1, 0, 1)
        c3 = swap(rx[2:], 0, 1)
        qax, qay, qaxy = swap(qa, 0, 2), swap(qa, 1, 0), swap(qa, 1, 2)
        a_args, a_places = both_cores([(qa, (0, 0, za)), (qax, (1, 0, za)), (qay, (0, 1, za)), (qaxy, (1, 1, za))])
        qb = after(qb, rx, qax, qay)
        qbx, qby = swap(qb, 0, 2), swap(qb, 1, 0)
    else:

        def pair(rel):
            return jnp.concatenate([lax.dynamic_slice_in_dim(v, me_t ^ rel, 1, 0) for v in (inputs, cotangent)])

        rx = swap(jnp.concatenate([pair(2), pair(3)]), 0, 2)
        own, c1 = pair(0), swap(pair(1), 0, 1)
        c3 = swap(rx[2:], 0, 1)
        relative = me_t ^ jnp.arange(n_t)
        whole = [lax.all_gather(lax.all_gather(v.astype(BF16), "dp"), "tensor") for v in (attn_proj, out_proj, up_proj, down_proj)]
        attn_w, out_w, up_w, down_w = [jnp.take(v, relative, axis=0) for v in whole]
        attn_w = attn_w.transpose(1, 3, 0, 2, 4).reshape(width, n_t * 3 * group)
        pos_w = lax.all_gather(lax.all_gather(pos_table.astype(BF16), "dp", axis=0, tiled=True), "tensor", axis=0, tiled=True)
        norm_w = lax.all_gather(norm_params, "dp", axis=1, tiled=True)
        norm_w = jnp.concatenate([norm_w, jnp.zeros_like(norm_w)])
        a_args, a_places = [attn_w, pos_w, norm_w], None
        b_args, b_places = [out_w.reshape(n_t * group, width), up_w.reshape(n_t, width, inner), down_w.reshape(n_t, inner, width)], None

    first = n_t - 1
    heads_of = group // HD

    def kept(groups):
        return [pltpu.HBM((win, groups * 3 * group), BF16), pltpu.HBM((groups * heads_of, win, win), BF16), sds((win, groups * group), BF16)]

    def work(groups):
        return [((win, groups * 3 * group), BF16), ((groups * heads_of, win, win), BF16), [groups * (1 + 2 * heads_of) + 1]]

    hid, qkv_a, pt_a, mixed_a, attn_all, norm_all, x_all, w_last, bias = call(
        functools.partial(attention_kernel, a_places, len(a_args)),
        [
            sds((win, width), F32),
            *kept(first),
            pltpu.HBM((width, n_t * 3 * group), BF16),
            sds((8, width), F32),
            sds((win, width), BF16),
            sds((width, 3 * group), BF16),
            sds((win, win), F32),
        ],
        [((win, width), BF16), ((n_dp, 16, LANES), F32), ((width, n_t * 3 * group), BF16), *work(first)],
        [scal, own, rx, c1, c3, segment_ids, *a_args],
        "svvvvv" + "v" * len(a_args),
        14,
        1_000_000,
    )
    if fast:
        found = gather_xy(qb, zb, qbx, qby, x_all)
    qkv_b, pt_b, mixed_b = call(attention_rest_kernel, kept(1), work(1), [x_all, w_last, bias], "vvv", 6, 1_000_000)
    if fast:
        found[3:] = [(after(v, mixed_b), at) for v, at in found[3:]]
        b_args, b_places = both_cores(found)

    blocks = [sds((block, width), BF16), sds((1, block, width), BF16), sds((2, block, width), BF16)]
    if fast:
        rows_b = 2 * per + out_per
        grads_b = [sds((n, rows_b, width), BF16) for n in (n_dp // 2, n_dp // 2, n_dp)] * 2
    else:
        grads_b = [sds((n_t, width, inner), BF16), sds((n_t, inner, width), BF16), sds((n_t * group, width), BF16)]
    res_k, res_1, res_x, gone, gm, gnorm, *got_b = call(
        functools.partial(ffn_kernel, b_places, len(b_args)),
        [*blocks, sds((win, width), F32), sds((n_t, win, group), BF16), sds((8, width), F32), *grads_b],
        [
            ((win, width), BF16),
            ((n_t * group, width), BF16),
            ((n_t, width, inner), BF16),
            ((n_t, inner, width), BF16),
            ((2, win, width), F32),
            ((win, width), F32),
            ((2, win, width), BF16),
            ((win, width), F32),
            ((win, LANES), F32),
            ((win, width), F32),
            ((win, width), BF16),
            ((n_t, win, inner), BF16),
            ((n_t, win, inner), F32),
            ((win, width), BF16),
            ((width, win), BF16),
            ((win, n_t * group), BF16),
        ],
        [scal, own, rx, c1, c3, hid, mixed_a, mixed_b, norm_all, *b_args],
        "svvvvvvvv" + "v" * len(b_args),
        26,
        1_000_000,
    )
    if fast:
        red_b = Reduction(*got_b)
        gone = after(gone, red_b.a, red_b.b)
        first_b = red_b.first()

    blocks = [sds((block, width), F32), *blocks[1:]]
    if fast:
        rows_a = 3 * per + width // LANES * pos_per + 16
        grads_a = [sds((n, rows_a, LANES), BF16) for n in (n_dp // 2, n_dp // 2, n_dp)] * 2
    else:
        grads_a = [sds((n_t, width, 3 * group), BF16), sds((win, width), BF16)]
    gi_k, gi_1, gi_x, *got_a = call(
        functools.partial(attention_back_kernel, fast),
        [*blocks, *grads_a],
        [
            ((width, win), BF16),
            ((n_t * group // HD, win, win), BF16),
            ((win, n_t * 3 * group), BF16),
            ((win, width), F32),
            ((2, width, 3 * group), BF16),
            ((win, n_t * 3 * group), BF16),
            ((n_t * group // HD, win, win), BF16),
            ((width, n_t * 3 * group), BF16),
            [1 + n_t + 2 * n_t * group // HD],
        ],
        [scal, hid, qkv_a, qkv_b, pt_a, pt_b, gm, attn_all, gone, gnorm],
        "svhhhhvhvv",
        18,
        1_000_000,
    )
    leaving = [jnp.concatenate([res_x[i : i + 1], gi_x[i : i + 1]]) for i in range(2)]
    if fast:
        red_a = Reduction(*got_a)
        first_a, second_b = red_a.first(), red_b.second()
        chunk_b, chunk_a = got_b[0].shape[1:], got_a[0].shape[1:]
        before_z = [[sds(chunk, F32), sds(chunk, F32), sds((2, *chunk), BF16)] for chunk in (chunk_b, chunk_a)]
        last = [[sds(chunk, F32), sds((1, *chunk), BF16)] for chunk in (chunk_b, chunk_a)]
        own_b, far_b, odd_b = call(near_kernel, before_z[0], [], [*red_b.rest, *first_b, *second_b], "v" * 6, 8, 1_000)
        a_y, a_x = call(second_kernel, [sds((2, *chunk_a), BF16)] * 2, [], [own_b, *red_a.rest, *first_a], "avvvv", 8, 1_000)
        second_a = swap(a_y, 1, 0), swap(a_x, 0, 2)
        near_b = swap(odd_b, 2, 0)
        own_b, far_b, own_a, far_a, odd_a = call(
            far_near_kernel,
            last[0] + before_z[1],
            [],
            [own_b, far_b, near_b, *red_a.rest, *first_a, *second_a],
            "v" * 9,
            8,
            1_000,
        )
        far_b = swap(far_b, 4, 0)
        r2, r3 = [swap(after(v, own_a), 0, m) for v, m in zip(leaving, (2, 3), strict=True)]
        own_a, far_a = call(far_kernel, last[1], [], [own_a, far_a, swap(odd_a, 2, 0)], "vvv", 4, 1_000)
        far_a = swap(far_a, 4, 0)
    else:
        r2, r3 = [swap(v, 0, m) for v, m in zip(leaving, (2, 3), strict=True)]
    r1 = [swap(res_1, 0, 1), swap(gi_1, 0, 1)]
    masters = (attn_proj, out_proj, up_proj, down_proj, pos_table, norm_params)
    firsts = (first_attn, first_out, first_up, first_down, first_pos, first_norm)
    seconds = (second_attn, second_out, second_up, second_down, second_pos, second_norm)
    updated = [None] * 6
    token = sds((8, LANES), F32)
    done = jnp.zeros(token.shape, F32)
    if fast:
        which = (2, 3, 1)
        state = [group[i] for group in (masters, firsts, seconds) for i in which]
        new = call(
            functools.partial(rows_update_kernel, which),
            [sds(v.shape, F32) for v in state] + [token],
            [],
            [own_b, far_b, *state],
            "v" * 11,
            8,
            2_000_000_000,
        )
        for i, index in enumerate(which):
            updated[index] = new[i:9:3]
        done = new[9]
    if fast:
        which = (0, 4, 5)
        state = [group[i] for group in (masters, firsts, seconds) for i in which]
        new = call(
            tiles_update_kernel,
            [sds(v.shape, F32) for v in state] + [token],
            [],
            [scal, done, own_a, far_a, *state],
            "sv" + "v" * 11,
            8,
            1_000_000,
        )
        for i, index in enumerate(which):
            updated[index] = new[i:9:3]
        done = new[9]
    outputs, grad_input = call(
        finish_kernel,
        [pltpu.HBM(inputs.shape, BF16), pltpu.HBM(inputs.shape, F32)],
        [((3, block, width), F32), [8]],
        [scal, done, res_k, gi_k, *r1, r2, r3],
        "sv" + "v" * 6,
        8,
        1_000,
    )
    if not fast:

        def reduced(value, own_axis):
            arrived = lax.all_to_all(value, "dp", split_axis=0, concat_axis=0, tiled=True)
            part = arrived.astype(F32).sum(axis=0).astype(BF16)
            arrived = lax.all_to_all(part, "tensor", split_axis=0, concat_axis=0, tiled=True)
            return arrived.astype(F32).sum(axis=0)

        gup, gdown, gout = got_b
        gattn, gpos = got_a
        gup, gdown, gout, gattn = [jnp.take(v, relative, axis=0) for v in (gup, gdown, gout.reshape(n_t, group, width), gattn)]
        g_up = reduced(gup.reshape(n_t, n_dp, per, inner).swapaxes(0, 1), 0)
        g_down = reduced(gdown.reshape(n_t, n_dp, inner // n_dp, width).swapaxes(0, 1), 0)
        g_out = reduced(gout.reshape(n_t, n_dp, out_per, width).swapaxes(0, 1), 0)
        g_pos = reduced(gpos.reshape(n_t, n_dp, pos_per, width).swapaxes(0, 1), 0)
        g_attn = reduced(gattn.reshape(n_t, n_dp, per, 3, group).swapaxes(0, 1), 0).swapaxes(0, 1)
        cut = gnorm[:4].reshape(4, n_dp, width // n_dp).swapaxes(0, 1).astype(BF16)
        g_norm = reduced(jnp.broadcast_to(cut[:, None], (n_dp, n_t, *cut.shape[1:])), 0)

        gradients = (g_attn, g_out, g_up, g_down, g_pos, g_norm)
        for index in range(6):
            updated[index] = adam_step(masters[index], gradients[index], firsts[index], seconds[index], RATES[index], DECAYS[index])
    return (outputs, grad_input, *[v for new in updated for v in new])


def solution(mesh):
    acts = P("dp", "tensor", None)
    attn = P(None, "dp", "tensor")
    both = P(("tensor", "dp"), None)
    up = P("dp", "tensor")
    norm = P(None, "dp")
    return jax.shard_map(
        body,
        mesh=mesh,
        in_specs=(acts, P("dp", None), acts, attn, both, up, both, both, norm, *(attn,) * 2, *(both,) * 2, *(up,) * 2, *(both,) * 4, *(norm,) * 2),
        out_specs=(acts, acts, *(attn,) * 3, *(both,) * 3, *(up,) * 3, *(both,) * 6, *(norm,) * 3),
        check_vma=False,
    )
```

```python
import functools

import jax
import jax.numpy as jnp
from jax import lax
from jax.experimental import pallas as pl
from jax.experimental.pallas import tpu as pltpu
from jax.sharding import PartitionSpec as P

HD = 64
STEP = 10
LANES = 128

NORM_EPS = 1e-05
NEG_FILL = -1e30
BETA_ONE = 0.9
BETA_TWO = 0.95
ADAM_EPS = 1e-08
RATES = (0.03, 0.2, 0.03, 0.02, 0.3, 0.3)
DECAYS = (0.1, 0.1, 0.1, 0.1, 0.1, 0.0)
GELU_A = 0.7978845608028654
GELU_B = 0.044715

F32 = jnp.float32
BF16 = jnp.bfloat16
AXES = ("dp", "tensor")

NN = (((1,), (0,)), ((), ()))
NT = (((1,), (1,)), ((), ()))
TN = (((0,), (0,)), ((), ()))
QUERIES = 256


def total(*parts):
    return sum(p.astype(F32) for p in parts)


def low(*parts):
    return total(*parts).astype(BF16)


def adam_step(weight, gradient, moment_one, second, step_rate, decay_rate):
    first_new = BETA_ONE * moment_one + (1.0 - BETA_ONE) * gradient
    second_new = BETA_TWO * second + (1.0 - BETA_TWO) * gradient * gradient
    fixed_first = first_new / (1.0 - BETA_ONE**STEP)
    fixed_second = second_new / (1.0 - BETA_TWO**STEP)
    weight_new = weight - step_rate * (fixed_first / (jnp.sqrt(fixed_second) + ADAM_EPS) + decay_rate * weight)
    return (weight_new, first_new, second_new)


def mm(a, b, dims=NN):
    return lax.dot_general(a, b, dims, preferred_element_type=F32)


def swap(value, rd, rt):
    n_t = lax.axis_size("tensor")
    mask = rd * n_t + rt
    return lax.ppermute(value, AXES, [(i, i ^ mask) for i in range(lax.axis_size("dp") * n_t)])


def rows_at(start, size, step):
    return pl.ds(pl.multiple_of(start, step), size)


def by_head(rows):
    lane = lax.broadcasted_iota(jnp.int32, (rows, LANES), 1)

    def keep(h):
        here = (lane >= h * HD) & (lane < (h + 1) * HD)
        return lambda v: jnp.where(here, v, jnp.zeros_like(v))

    return [keep(h) for h in range(LANES // HD)]


def fill_window(me_t, which, parts, out_ref):
    own, rx, c1, c3 = parts
    n = own.shape[1]
    for r, ref in enumerate((own, c1, rx, c3)):
        out_ref[rows_at((me_t ^ r) * n, n, n), :] = ref[which]


def copies_in(moves, sems):
    copies = [pltpu.make_async_copy(src, dst, sems.at[i]) for i, (src, dst) in enumerate(moves)]
    for copy in copies:
        copy.start()
    return copies


def prepare_kernel(scal, inputs, cot, attn, pos, norm, out, up, down, ga, gb, xs, c1, own, attn_s, pos_s, norm_s, out_s, up_s, down_s, sems):
    me_t = scal[1]
    moves = [(attn, attn_s), (pos, pos_s), (norm, norm_s), (up, up_s), (down, down_s), (out, out_s)]
    for rel, ref, at in ((2, xs, 0), (3, xs, 2), (1, c1, 0), (0, own, 0)):
        moves += [(inputs.at[me_t ^ rel], ref.at[at]), (cot.at[me_t ^ rel], ref.at[at + 1])]
    copies = copies_in(moves, sems)
    for copy in copies[:3]:
        copy.wait()
    per = attn.shape[1]
    pos_per = pos.shape[0]
    tiles = pos.shape[1] // LANES
    for t in range(3):
        ga[0, t * per : (t + 1) * per, :] = attn_s[t].astype(BF16)
    for k in range(tiles):
        at = 3 * per + k * pos_per
        ga[0, at : at + pos_per, :] = pos_s[:, k * LANES : (k + 1) * LANES].astype(BF16)
    at = 3 * per + tiles * pos_per
    both = norm_s[...]
    both = jnp.concatenate([both, both], axis=1)
    both = jnp.concatenate([both, jnp.zeros_like(both)], axis=0)
    high = both.astype(BF16)
    rest = (both - high.astype(F32)).astype(BF16)
    ga[0, at : at + 16, :] = jnp.concatenate([high, rest], axis=0)
    for copy in copies[3:6]:
        copy.wait()
    gb[0, 0:per, :] = up_s[...].astype(BF16)
    gb[0, per : 2 * per, :] = down_s[...].astype(BF16)
    gb[0, 2 * per :, :] = out_s[...].astype(BF16)
    for copy in copies[6:]:
        copy.wait()


def stack_kernel(own, got, both):
    n = own.shape[0]
    both[:n] = own[...]
    both[n:] = got[...]


def leaver(sems):
    leaving = []

    def leave(src, dst):
        leaving.append(pltpu.make_async_copy(src, dst, sems.at[len(leaving)]))
        leaving[-1].start()

    return leaving, leave


def attend(x, w, groups, bias, qkv_o, qkv_h, pt_o, pt_h, mix_o, leave):
    win = x.shape[0]
    heads = by_head(win)
    for g in groups:
        at = g * 3 * LANES
        qkv = mm(x[...], w[:, at : at + 3 * LANES]).astype(BF16)
        q = qkv[:, :LANES] * jnp.asarray(HD**-0.5, BF16)
        k = qkv[:, LANES : 2 * LANES]
        v = qkv[:, 2 * LANES :]
        qkv_o[:, at : at + LANES] = q
        qkv_o[:, at + LANES : at + 3 * LANES] = qkv[:, LANES:]
        leave(qkv_o.at[:, at : at + 3 * LANES], qkv_h.at[:, at : at + 3 * LANES])
        for j in range(win // QUERIES):
            ext = (j + 1) * QUERIES
            cols = slice(j * QUERIES, ext)
            mixed = jnp.zeros((QUERIES, LANES), F32)
            for h, only in enumerate(heads):
                s = mm(only(k)[:ext], q[cols], NT) + bias[:ext, cols]
                e = jnp.exp(s - jnp.max(s, axis=0, keepdims=True))
                p = (e * (1.0 / jnp.sum(e, axis=0, keepdims=True))).astype(BF16)
                pt_o[len(heads) * g + h, :ext, cols] = p
                mixed += mm(p, only(v)[:ext], TN)
            mix_o[cols, g * LANES : (g + 1) * LANES] = mixed.astype(BF16)
            for h in range(len(heads)):
                leave(pt_o.at[len(heads) * g + h, :ext, cols], pt_h.at[len(heads) * g + h, :ext, cols])


def attention_kernel(places, n_pieces, scal, *refs):
    own, rx, c1, c3, segs = refs[:5]
    pieces = refs[5 : 5 + n_pieces]
    hid_o, qkv_h, pt_h, mix_o, w_h, nrm_o, x_s, wlast_o, bias_s, pos_s, nrm_s, w_o, qkv_o, pt_o, out_sems = refs[5 + n_pieces :]
    leaving, leave = leaver(out_sems)
    me_dp, me_t = scal[0], scal[1]
    win, width = x_s.shape
    groups = w_o.shape[1] // (3 * LANES)
    fill_window(me_t, 0, (own, rx, c1, c3), x_s)
    if places is None:
        w_o[...] = pieces[0][...]
        pos_s[...] = pieces[1][...]
        nrm_o[...] = pieces[2][...]
    else:
        n_dp = nrm_s.shape[0]
        per = width // n_dp
        pos_per = win // (n_dp * groups)
        for ref, (xr, yr, zs, c) in zip(pieces, places, strict=True):
            tr = xr * 2 + c
            for i, zr in enumerate(zs):
                src = me_dp ^ (zr * 2 + yr)
                for t in range(3):
                    at = (tr * 3 + t) * LANES
                    w_o[rows_at(src * per, per, per), at : at + LANES] = ref[i, t * per : (t + 1) * per]
                where = (me_t ^ tr) * (win // groups) + src * pos_per
                for k in range(width // LANES):
                    at = 3 * per + k * pos_per
                    pos_s[rows_at(where, pos_per, pos_per), k * LANES : (k + 1) * LANES] = ref[i, at : at + pos_per]
                if tr == 0:
                    at = 3 * per + width // LANES * pos_per
                    nrm_s[src] = ref[i, at : at + 16].astype(F32)
        low_lane = lax.broadcasted_iota(jnp.int32, (8, LANES), 1) < per
        for j in range(n_dp // 2):
            left = nrm_s[2 * j]
            right = nrm_s[2 * j + 1]
            both = jnp.where(low_lane, left[0:8] + left[8:16], right[0:8] + right[8:16])
            nrm_o[:, j * LANES : (j + 1) * LANES] = both

    leave(w_o, w_h)

    seg = segs[pl.ds(me_t, 1), :].astype(F32)
    seg_col = jnp.transpose(jnp.broadcast_to(seg, (LANES, win)))
    for i in range(win // LANES):
        key_seg = seg_col[i * LANES : (i + 1) * LANES, 0:1]
        key_at = lax.broadcasted_iota(jnp.int32, (LANES, win), 0) + i * LANES
        query_at = lax.broadcasted_iota(jnp.int32, (LANES, win), 1)
        counts = (key_seg == seg) & (query_at >= key_at)
        bias_s[i * LANES : (i + 1) * LANES, :] = jnp.where(counts, 0.0, NEG_FILL)

    hidden = x_s[...].astype(F32) + pos_s[...].astype(F32)
    hid_o[...] = hidden
    x_s[...] = hidden.astype(BF16)
    first = qkv_o.shape[1] // (3 * LANES)
    attend(x_s, w_o, range(first), bias_s, qkv_o, qkv_h, pt_o, pt_h, mix_o, leave)
    wlast_o[...] = w_o[:, first * 3 * LANES :]
    for copy in leaving:
        copy.wait()


def attention_rest_kernel(x, w, bias, qkv_h, pt_h, mix_o, qkv_o, pt_o, out_sems):
    leaving, leave = leaver(out_sems)
    attend(x, w, range(w.shape[1] // (3 * LANES)), bias, qkv_o, qkv_h, pt_o, pt_h, mix_o, leave)
    for copy in leaving:
        copy.wait()


def norm_forward(v):
    center = v - jnp.mean(v, axis=-1, keepdims=True)
    rs = lax.rsqrt(jnp.mean(center * center, axis=-1, keepdims=True) + NORM_EPS)
    return center * rs, rs


def norm_backward(g, xhat, rs, gain):
    e = g * gain
    return rs * (e - jnp.mean(e, axis=-1, keepdims=True) - xhat * jnp.mean(e * xhat, axis=-1, keepdims=True))


def put_blocks(me_t, value, keep, s1, sx):
    n = keep.shape[0]
    for r, ref in ((0, keep), (1, s1.at[0]), (2, sx.at[0]), (3, sx.at[1])):
        ref[...] = value[rows_at((me_t ^ r) * n, n, n), :].astype(ref.dtype)


CHUNK = 128


def chunk_of(refs, tr, r):
    c, xr, yr, zr = tr & 1, tr >> 1, r & 1, r >> 1
    half = refs[0].shape[0] // 2
    if zr < half:
        kind, slot = (0, yr * half + zr) if xr == 1 else (2, yr * half + zr)
    else:
        kind, slot = (1, xr * half + zr - half) if yr == 1 else (2, 2 * half + xr * half + zr - half)
    return refs[3 * c + kind], slot


def ffn_kernel(places, n_pieces, scal, *refs):
    own, rx, c1, c3, hid, mixed_a, mixed_b, nrm = refs[:8]
    pieces = refs[8 : 8 + n_pieces]
    rest = refs[8 + n_pieces :]
    res_k, res_1, res_x, gone_o, gm_o, gnorm_o = rest[:6]
    if places is None:
        gup_o, gdown_o, gout_o = rest[6:9]
        rest = rest[9:]
    else:
        chunks_o = rest[6:12]
        rest = rest[12:]
    cot_s, out_s, up_s, down_s, a_s, b_s, g_s, xh1_s, r1_s, n1_s, sent_s, act_s, dg_s, low_s, xt_s, mixed = rest
    split = mixed_a.shape[1]
    mixed[:, :split] = mixed_a[...]
    mixed[:, split:] = mixed_b[...]
    me_dp, me_t = scal[0], scal[1]
    win, width = hid.shape
    groups = up_s.shape[0]
    fill_window(me_t, 1, (own, rx, c1, c3), cot_s)
    if places is None:
        n_dp = 1
        for src, dst in zip(pieces, (out_s, up_s, down_s), strict=True):
            dst[...] = src[...]
    else:
        n_dp = chunks_o[2].shape[0]
        per = width // n_dp
        out_per = LANES // n_dp
        for ref, (xr, yr, zs, c) in zip(pieces, places, strict=True):
            tr = xr * 2 + c
            for i, zr in enumerate(zs):
                src = me_dp ^ (zr * 2 + yr)
                up_s[tr, rows_at(src * per, per, per), :] = ref[i, 0:per]
                down_s[tr, rows_at(src * per, per, per), :] = ref[i, per : 2 * per]
                out_s[rows_at(tr * LANES + src * out_per, out_per, out_per), :] = ref[i, 2 * per : 2 * per + out_per]

    def chunks(fn):
        for i in range(win // CHUNK):
            fn(slice(i * CHUNK, (i + 1) * CHUNK))

    a_s[0] = mm(mixed[...], out_s[...])

    def norm_one(at):
        xhat, rs = norm_forward(hid[at, :] + a_s[0, at, :])
        xh1_s[at, :] = xhat
        r1_s[at, :] = jnp.broadcast_to(rs, (CHUNK, LANES))
        normed = xhat * nrm[0:1, :] + nrm[1:2, :]
        n1_s[at, :] = normed
        sent_s[at, :] = normed.astype(BF16)

    chunks(norm_one)

    for g in range(groups):
        a_s[g % 2] = mm(sent_s[...], up_s[g])

        def gelu(at, g=g):
            v = a_s[g % 2, at, :]
            square = v * v
            half = 0.5 + 0.5 * jnp.tanh(v * (GELU_A + GELU_A * GELU_B * square))
            act_s[g, at, :] = (v * half).astype(BF16)
            dg_s[g, at, :] = half + (half - half * half) * (v * (2.0 * GELU_A + 6.0 * GELU_A * GELU_B * square))

        chunks(gelu)
        n1_s[...] += mm(act_s[g], down_s[g])

    def norm_two(i, sums):
        at = slice(i * CHUNK, (i + 1) * CHUNK)
        xhat, rs = norm_forward(n1_s[at, :])
        n1_s[at, :] = xhat * nrm[2:3, :] + nrm[3:4, :]
        g = cot_s[at, :].astype(F32)
        grad = norm_backward(g, xhat, rs, nrm[2:3, :])
        b_s[at, :] = grad
        low_s[at, :] = grad.astype(BF16)
        return (sums[0] + jnp.sum((g * xhat).reshape(-1, 8, width), axis=0), sums[1] + jnp.sum(g.reshape(-1, 8, width), axis=0))

    def every(step):
        sums = (jnp.zeros((8, width), F32),) * 2
        for i in range(win // CHUNK):
            sums = step(i, sums)
        return sums

    gain_two, shift_two = every(norm_two)
    put_blocks(me_t, n1_s, res_k, res_1, res_x)

    def put(g, first, height, source, base):
        for r in range(n_dp):
            ref, slot = chunk_of(chunks_o, g, r)
            ref[slot, first : first + height, :] = source[rows_at(base + (r ^ me_dp) * height, height, height), :]

    xt_s[...] = jnp.transpose(sent_s[...])
    for g in range(groups):
        gdown = mm(jnp.transpose(act_s[g]), low_s[...])
        if places is None:
            gdown_o[g] = gdown.astype(BF16)
        else:
            g_s[0] = gdown.astype(BF16)
            put(g, per, per, g_s.at[0], 0)
        act_s[g] = (mm(low_s[...], down_s[g], NT) * dg_s[g]).astype(BF16)
        gup = mm(xt_s[...], act_s[g])
        if places is None:
            gup_o[g] = gup.astype(BF16)
        else:
            g_s[1] = gup.astype(BF16)
            put(g, 0, per, g_s.at[1], 0)
        b_s[...] += mm(act_s[g], up_s[g], NT)

    def norm_one_back(i, sums):
        at = slice(i * CHUNK, (i + 1) * CHUNK)
        g = b_s[at, :]
        xhat = xh1_s[at, :]
        grad = norm_backward(g, xhat, r1_s[at, 0:1], nrm[0:1, :])
        gone_o[at, :] = grad
        low_s[at, :] = grad.astype(BF16)
        return (sums[0] + jnp.sum((g * xhat).reshape(-1, 8, width), axis=0), sums[1] + jnp.sum(g.reshape(-1, 8, width), axis=0))

    gain_one, shift_one = every(norm_one_back)
    for k, total in enumerate((gain_one, shift_one, gain_two, shift_two)):
        gnorm_o[k : k + 1, :] = jnp.sum(total, axis=0, keepdims=True)
    gnorm_o[4:8, :] = jnp.zeros((4, width), F32)

    gout = mm(jnp.transpose(mixed[...]), low_s[...])
    if places is None:
        gout_o[...] = gout.astype(BF16)
    else:
        g_s[0] = gout.astype(BF16)
        for g in range(groups):
            put(g, 2 * per, out_per, g_s.at[0], g * LANES)
    gm = mm(low_s[...], out_s[...], NT).astype(BF16)
    for g in range(groups):
        gm_o[g] = gm[:, g * LANES : (g + 1) * LANES]


def attention_back_kernel(fast, scal, hid, qkv_a, qkv_b, pt_a, pt_b, gm, w_h, gone, gnorm, *rest):
    gi_k, gi_1, gi_x = rest[:3]
    if fast:
        chunks_o = rest[3:9]
        rest = rest[9:]
    else:
        gattn_o, gpos_o = rest[3:5]
        rest = rest[5:]
    ht_s, ds_s, dqkv_s, acc_s, g_s, qkv, pt, w, sems = rest
    me_dp, me_t = scal[0], scal[1]
    win, width = hid.shape
    groups = w.shape[1] // (3 * LANES)
    heads = by_head(win)
    arriving = []
    for g in range(groups):
        first = qkv_a.shape[1] // (3 * LANES)
        qkv_h, pt_h, base = (qkv_a, pt_a, 0) if g < first else (qkv_b, pt_b, first)
        lanes = slice(g * 3 * LANES, (g + 1) * 3 * LANES)
        there = slice((g - base) * 3 * LANES, (g - base + 1) * 3 * LANES)
        arriving.append(pltpu.make_async_copy(qkv_h.at[:, there], qkv.at[:, lanes], sems.at[len(arriving)]))
        for n in range(g * len(heads), (g + 1) * len(heads)):
            for j in range(win // QUERIES):
                ext = (j + 1) * QUERIES
                cols = slice(j * QUERIES, ext)
                arriving.append(pltpu.make_async_copy(pt_h.at[n - base * len(heads), :ext, cols], pt.at[n, :ext, cols], sems.at[len(arriving)]))
    arriving.append(pltpu.make_async_copy(w_h, w, sems.at[len(arriving)]))
    for copy in arriving:
        copy.start()
    ht_s[...] = jnp.transpose(hid[...].astype(BF16))
    for g in range(groups):
        at = g * 3 * LANES
        per_group = 1 + len(heads) * (win // QUERIES)
        for copy in arriving[g * per_group : (g + 1) * per_group]:
            copy.wait()
        q = qkv[:, at : at + LANES]
        k = qkv[:, at + LANES : at + 2 * LANES]
        v = qkv[:, at + 2 * LANES : at + 3 * LANES]
        d_mixed = gm[g]
        for j in range(win // QUERIES):
            ext = (j + 1) * QUERIES
            cols = slice(j * QUERIES, ext)
            dq = jnp.zeros((QUERIES, LANES), F32)
            for h, only in enumerate(heads):
                p = pt[len(heads) * g + h, :ext, cols].astype(F32)
                dp = mm(v[:ext], only(d_mixed)[cols], NT)
                ds = (p * (dp - jnp.sum(p * dp, axis=0, keepdims=True))).astype(BF16)
                ds_s[len(heads) * g + h, :ext, cols] = ds
                dq += mm(ds, only(k)[:ext], TN)
            dqkv_s[cols, at : at + LANES] = (dq * HD**-0.5).astype(BF16)
        for i in range(win // QUERIES):
            rows = slice(i * QUERIES, (i + 1) * QUERIES)
            dk = jnp.zeros((QUERIES, LANES), F32)
            dv = jnp.zeros((QUERIES, LANES), F32)
            for h, only in enumerate(heads):
                dk += mm(ds_s[len(heads) * g + h, rows, i * QUERIES :], only(q)[i * QUERIES :])
                dv += mm(pt[len(heads) * g + h, rows, i * QUERIES :], only(d_mixed)[i * QUERIES :])
            dqkv_s[rows, at + LANES : at + 2 * LANES] = dk.astype(BF16)
            dqkv_s[rows, at + 2 * LANES : at + 3 * LANES] = dv.astype(BF16)
    arriving[-1].wait()
    acc_s[...] = gone[...] + mm(dqkv_s[...], w[...], NT)

    put_blocks(me_t, acc_s, gi_k, gi_1, gi_x)
    if not fast:
        for g in range(groups):
            gattn_o[g] = mm(ht_s[...], dqkv_s[:, g * 3 * LANES : (g + 1) * 3 * LANES]).astype(BF16)
        gpos_o[...] = acc_s[...].astype(BF16)
        return
    n_dp = chunks_o[2].shape[0]
    per = width // n_dp
    pos_per = win // (n_dp * groups)
    for g in range(groups):
        g_s[g % 2] = mm(ht_s[...], dqkv_s[:, g * 3 * LANES : (g + 1) * 3 * LANES]).astype(BF16)
        for r in range(n_dp):
            d = r ^ me_dp
            ref, slot = chunk_of(chunks_o, g, r)
            for t in range(3):
                ref[slot, t * per : (t + 1) * per, :] = g_s[g % 2, rows_at(d * per, per, per), t * LANES : (t + 1) * LANES]
            where = (me_t ^ g) * (win // groups) + d * pos_per
            for k in range(width // LANES):
                at = 3 * per + k * pos_per
                ref[slot, at : at + pos_per, :] = acc_s[rows_at(where, pos_per, pos_per), k * LANES : (k + 1) * LANES].astype(BF16)
            at = 3 * per + width // LANES * pos_per
            tile = gnorm[0:8, rows_at((d >> 1) * LANES, LANES, LANES)]
            ref[slot, at : at + 16, :] = jnp.concatenate([tile, tile], axis=0).astype(BF16)


def near_kernel(rest, got, x, y, x2, y2, own, far, odd):
    own[...] = total(rest[0], got[0], x[0], x2[0])
    far[...] = total(rest[4], got[4], y[0], y2[0])
    odd[0] = low(rest[1], got[1], x[1], x2[1])
    odd[1] = low(rest[5], got[5], y[1], y2[1])


def second_kernel(done, rest, got, x, y, a, b):
    del done
    for i in range(2):
        a[i] = low(rest[2 + i], got[2 + i], x[2 + i])
        b[i] = low(rest[6 + i], got[6 + i], y[2 + i])


def far_kernel(own, far, near, own_o, far_o):
    own_o[...] = total(own[...], near[0])
    far_o[0] = low(far[...], near[1])


def far_near_kernel(own, far, near, rest, got, x, y, x2, y2, own_o, far_o, *others):
    far_kernel(own, far, near, own_o, far_o)
    near_kernel(rest, got, x, y, x2, y2, *others)


def update(refs, gradient, rate, decay):
    weight, one, two, new_weight, new_one, new_two = refs
    new_weight[...], new_one[...], new_two[...] = adam_step(weight[...], gradient, one[...], two[...], rate, decay)


def rows_update_kernel(which, own, far, *refs):
    n = len(which)
    *refs, token = refs
    token[...] = jnp.zeros_like(token)
    grad = total(own[...], far[0])
    at = 0
    for i, index in enumerate(which):
        height = refs[i].shape[0]
        update(refs[i :: n], grad[at : at + height], RATES[index], DECAYS[index])
        at += height


def tiles_update_kernel(scal, done, own, far, *refs):
    *refs, token = refs
    token[...] = done[...]
    attn, pos, norm = refs[0::3], refs[1::3], refs[2::3]
    grad = total(own[...], far[0])
    per = attn[0].shape[1]
    pos_per, width = pos[0].shape
    update(attn, grad[: 3 * per].reshape(attn[0].shape), RATES[0], DECAYS[0])
    at = 3 * per
    rows = [grad[at + k * pos_per : at + (k + 1) * pos_per] for k in range(width // LANES)]
    update(pos, jnp.concatenate(rows, axis=1), RATES[4], DECAYS[4])
    at += width // LANES * pos_per
    tile = grad[at : at + 8]
    half = jnp.where((scal[0] & 1) == 1, tile[:4, LANES // 2 :], tile[:4, : LANES // 2])
    update(norm, half, RATES[5], DECAYS[5])


def finish_kernel(scal, done, res_k, gi_k, res_1, gi_1, r2, r3, res_o, gi_o, gi_s, sems):
    del done
    me_t = scal[1]
    moves = [(gi_k, gi_o.at[me_t])]
    moves += [(res, res_o.at[me_t ^ r]) for r, res in enumerate((res_k, res_1.at[0], r2.at[0], r3.at[0]))]
    copies = copies_in(moves, sems)
    for r, gi in ((1, gi_1.at[0]), (2, r2.at[1]), (3, r3.at[1])):
        gi_s[r - 1] = gi[...].astype(F32)
        copies.append(pltpu.make_async_copy(gi_s.at[r - 1], gi_o.at[me_t ^ r], sems.at[4 + r]))
        copies[-1].start()
    for copy in copies:
        copy.wait()


def after(value, *others):
    return lax.optimization_barrier((value, *others))[0]


def stacked(q, got):
    out = jax.ShapeDtypeStruct((2 * q.shape[0], *q.shape[1:]), q.dtype)
    return call(stack_kernel, [out], [], [q, got], "vv", 6, 1_000)[0]


def gather_z(value, *others):
    nz = lax.axis_size("dp") // 2
    q, order = value, [0]
    step = nz // 2
    while step:
        if step == 1:
            q = after(q, *others)
        q = stacked(q, swap(q, step * 2, 0))
        order = order + [z ^ step for z in order]
        step //= 2
    return q, tuple(order)


def gather_xy(q, order, qx=None, qy=None, *others):
    half = len(order) // 2
    if qx is None:
        qx, qy = swap(q, 0, 2), swap(q, 1, 0)
    a, b = after(qx[:half], *others), after(qy[half:], *others)
    return [(q, (0, 0, order)), (qx, (1, 0, order)), (qy, (0, 1, order)), (swap(a, 1, 0), (1, 1, order[:half])), (swap(b, 0, 2), (1, 1, order[half:]))]


def both_cores(found):
    out = []
    for array, place in found:
        out.append((array, (*place, 0)))
        out.append((swap(array, 0, 1), (*place, 1)))
    return [f[0] for f in out], tuple(f[1] for f in out)


class Reduction:
    def __init__(self, keep_a, keep_b, keep_rest, send_a, send_b, send_rest):
        self.half = keep_a.shape[0] // 2
        self.n = keep_a.shape[0]
        self.sums = [(keep_rest,)]
        self.send_rest = send_rest
        got_a, got_b = swap(send_a, 0, 1), swap(send_b, 0, 1)
        self.a, self.b = low(keep_a, got_a), low(keep_b, got_b)

    def terms(self, a, start, stop):
        at = 0 if a else self.n
        found = [k[at + start : at + stop] for k in self.rest]
        for pair in self.got:
            g = pair[0 if a else 1]
            if g.shape[0] >= stop:
                found.append(g[start:stop])
        return found

    def first(self):
        self.rest = [self.sums[0][0], swap(self.send_rest, 0, 1)]
        self.got = [(swap(self.a, 0, 2), swap(self.b, 1, 0))]
        return self.got[0]

    def second(self, *others):
        h = self.half
        a, b = [after(low(*self.terms(part, h, 2 * h)), *others) for part in (True, False)]
        self.got.append((swap(a, 1, 0), swap(b, 0, 2)))
        return self.got[1]

    def over_z(self, *others):
        h = self.half
        arrived = []
        for z in range(1, 2 * h):
            chunk = low(*self.terms(z < h, z % h, z % h + 1))
            arrived.append(swap(after(chunk, *others), 2 * z, 0))
        return arrived

    def result(self, arrived):
        return total(*self.terms(True, 0, 1), *arrived)[0]


def call(kernel, outs, scratch, args, spaces, mib, flops):
    vmem = pl.BlockSpec(memory_space=pltpu.VMEM)
    args = [pltpu.with_memory_space_constraint(v, pltpu.HBM) if k == "h" else v for v, k in zip(args, spaces, strict=True)]
    kinds = {"s": pl.BlockSpec(memory_space=pltpu.SMEM), "v": vmem, "a": pl.BlockSpec(memory_space=pl.ANY), "h": pl.BlockSpec(memory_space=pltpu.HBM)}
    return pl.pallas_call(
        kernel,
        out_shape=outs,
        in_specs=[kinds[k] for k in spaces],
        out_specs=[vmem if isinstance(v, jax.ShapeDtypeStruct) else kinds["h"] for v in outs],
        scratch_shapes=[pltpu.VMEM(*s) if isinstance(s, tuple) else pltpu.SemaphoreType.DMA(tuple(s)) for s in scratch],
        compiler_params=pltpu.CompilerParams(vmem_limit_bytes=mib * 1024 * 1024),
        cost_estimate=pl.CostEstimate(flops=flops, bytes_accessed=0, transcendentals=0),
    )(*args)


def body(
    inputs,
    segment_ids,
    cotangent,
    attn_proj,
    out_proj,
    up_proj,
    down_proj,
    pos_table,
    norm_params,
    first_attn,
    second_attn,
    first_out,
    second_out,
    first_up,
    second_up,
    first_down,
    second_down,
    first_pos,
    second_pos,
    first_norm,
    second_norm,
):
    n_dp, n_t = lax.axis_size("dp"), lax.axis_size("tensor")
    me_dp, me_t = lax.axis_index("dp"), lax.axis_index("tensor")
    scal = jnp.stack([me_dp, me_t]).astype(jnp.int32)
    windows, block, width = inputs.shape
    win = block * n_t
    inner = up_proj.shape[1]
    group = attn_proj.shape[2]
    per, out_per, pos_per = attn_proj.shape[1], out_proj.shape[0], pos_table.shape[0]
    fast = out_per % 16 == 0 and pos_per % 16 == 0 and 2 * per == LANES and n_dp == 8 and n_t == 4
    sds = jax.ShapeDtypeStruct

    if fast:
        ga, gb, xs, c1, own = call(
            prepare_kernel,
            [
                sds((1, 3 * per + width // LANES * pos_per + 16, LANES), BF16),
                sds((1, 2 * per + out_per, width), BF16),
                sds((4, block, width), BF16),
                sds((2, block, width), BF16),
                sds((2, block, width), BF16),
            ],
            [(v.shape, F32) for v in (attn_proj, pos_table, norm_params, out_proj, up_proj, down_proj)] + [[14]],
            [scal, inputs, cotangent, attn_proj, pos_table, norm_params, out_proj, up_proj, down_proj],
            "s" + "h" * 8,
            8,
            1_000,
        )
        a2 = stacked(ga, swap(ga, 4, 0))
        qa, za = stacked(a2, swap(a2, 2, 0)), (0, 2, 1, 3)
        gb = after(gb, a2)
        rx = swap(xs, 0, 2)
        qb, zb = gather_z(gb, qa)
        c1 = swap(c1, 0, 1)
        c3 = swap(rx[2:], 0, 1)
        qax, qay, qaxy = swap(qa, 0, 2), swap(qa, 1, 0), swap(qa, 1, 2)
        a_args, a_places = both_cores([(qa, (0, 0, za)), (qax, (1, 0, za)), (qay, (0, 1, za)), (qaxy, (1, 1, za))])
        qb = after(qb, rx, qax, qay)
        qbx, qby = swap(qb, 0, 2), swap(qb, 1, 0)
    else:

        def pair(rel):
            return jnp.concatenate([lax.dynamic_slice_in_dim(v, me_t ^ rel, 1, 0) for v in (inputs, cotangent)])

        rx = swap(jnp.concatenate([pair(2), pair(3)]), 0, 2)
        own, c1 = pair(0), swap(pair(1), 0, 1)
        c3 = swap(rx[2:], 0, 1)
        relative = me_t ^ jnp.arange(n_t)
        whole = [lax.all_gather(lax.all_gather(v.astype(BF16), "dp"), "tensor") for v in (attn_proj, out_proj, up_proj, down_proj)]
        attn_w, out_w, up_w, down_w = [jnp.take(v, relative, axis=0) for v in whole]
        attn_w = attn_w.transpose(1, 3, 0, 2, 4).reshape(width, n_t * 3 * group)
        pos_w = lax.all_gather(lax.all_gather(pos_table.astype(BF16), "dp", axis=0, tiled=True), "tensor", axis=0, tiled=True)
        norm_w = lax.all_gather(norm_params, "dp", axis=1, tiled=True)
        norm_w = jnp.concatenate([norm_w, jnp.zeros_like(norm_w)])
        a_args, a_places = [attn_w, pos_w, norm_w], None
        b_args, b_places = [out_w.reshape(n_t * group, width), up_w.reshape(n_t, width, inner), down_w.reshape(n_t, inner, width)], None

    first = n_t // 2
    heads_of = group // HD

    def kept(groups):
        return [pltpu.HBM((win, groups * 3 * group), BF16), pltpu.HBM((groups * heads_of, win, win), BF16), sds((win, groups * group), BF16)]

    def work(groups):
        return [((win, groups * 3 * group), BF16), ((groups * heads_of, win, win), BF16), [groups * (1 + 2 * heads_of) + 1]]

    hid, qkv_a, pt_a, mixed_a, attn_all, norm_all, x_all, w_last, bias = call(
        functools.partial(attention_kernel, a_places, len(a_args)),
        [
            sds((win, width), F32),
            *kept(first),
            pltpu.HBM((width, n_t * 3 * group), BF16),
            sds((8, width), F32),
            sds((win, width), BF16),
            sds((width, (n_t - first) * 3 * group), BF16),
            sds((win, win), F32),
        ],
        [((win, width), BF16), ((n_dp, 16, LANES), F32), ((width, n_t * 3 * group), BF16), *work(first)],
        [scal, own, rx, c1, c3, segment_ids, *a_args],
        "svvvvv" + "v" * len(a_args),
        14,
        1_000_000,
    )
    if fast:
        found = gather_xy(qb, zb, qbx, qby, x_all)
    qkv_b, pt_b, mixed_b = call(attention_rest_kernel, kept(n_t - first), work(n_t - first), [x_all, w_last, bias], "vvv", 6, 1_000_000)
    if fast:
        found[3:] = [(after(v, mixed_b), at) for v, at in found[3:]]
        b_args, b_places = both_cores(found)

    blocks = [sds((block, width), BF16), sds((1, block, width), BF16), sds((2, block, width), BF16)]
    if fast:
        rows_b = 2 * per + out_per
        grads_b = [sds((n, rows_b, width), BF16) for n in (n_dp // 2, n_dp // 2, n_dp)] * 2
    else:
        grads_b = [sds((n_t, width, inner), BF16), sds((n_t, inner, width), BF16), sds((n_t * group, width), BF16)]
    res_k, res_1, res_x, gone, gm, gnorm, *got_b = call(
        functools.partial(ffn_kernel, b_places, len(b_args)),
        [*blocks, sds((win, width), F32), sds((n_t, win, group), BF16), sds((8, width), F32), *grads_b],
        [
            ((win, width), BF16),
            ((n_t * group, width), BF16),
            ((n_t, width, inner), BF16),
            ((n_t, inner, width), BF16),
            ((2, win, width), F32),
            ((win, width), F32),
            ((2, win, width), BF16),
            ((win, width), F32),
            ((win, LANES), F32),
            ((win, width), F32),
            ((win, width), BF16),
            ((n_t, win, inner), BF16),
            ((n_t, win, inner), F32),
            ((win, width), BF16),
            ((width, win), BF16),
            ((win, n_t * group), BF16),
        ],
        [scal, own, rx, c1, c3, hid, mixed_a, mixed_b, norm_all, *b_args],
        "svvvvvvvv" + "v" * len(b_args),
        26,
        1_000_000,
    )
    if fast:
        red_b = Reduction(*got_b)
        gone = after(gone, red_b.a, red_b.b)
        first_b = red_b.first()

    blocks = [sds((block, width), F32), *blocks[1:]]
    if fast:
        rows_a = 3 * per + width // LANES * pos_per + 16
        grads_a = [sds((n, rows_a, LANES), BF16) for n in (n_dp // 2, n_dp // 2, n_dp)] * 2
    else:
        grads_a = [sds((n_t, width, 3 * group), BF16), sds((win, width), BF16)]
    gi_k, gi_1, gi_x, *got_a = call(
        functools.partial(attention_back_kernel, fast),
        [*blocks, *grads_a],
        [
            ((width, win), BF16),
            ((n_t * group // HD, win, win), BF16),
            ((win, n_t * 3 * group), BF16),
            ((win, width), F32),
            ((2, width, 3 * group), BF16),
            ((win, n_t * 3 * group), BF16),
            ((n_t * group // HD, win, win), BF16),
            ((width, n_t * 3 * group), BF16),
            [1 + n_t + 2 * n_t * group // HD],
        ],
        [scal, hid, qkv_a, qkv_b, pt_a, pt_b, gm, attn_all, gone, gnorm],
        "svhhhhvhvv",
        18,
        1_000_000,
    )
    leaving = [jnp.concatenate([res_x[i : i + 1], gi_x[i : i + 1]]) for i in range(2)]
    if fast:
        red_a = Reduction(*got_a)
        first_a, second_b = red_a.first(), red_b.second()
        chunk_b, chunk_a = got_b[0].shape[1:], got_a[0].shape[1:]
        before_z = [[sds(chunk, F32), sds(chunk, F32), sds((2, *chunk), BF16)] for chunk in (chunk_b, chunk_a)]
        last = [[sds(chunk, F32), sds((1, *chunk), BF16)] for chunk in (chunk_b, chunk_a)]
        own_b, far_b, odd_b = call(near_kernel, before_z[0], [], [*red_b.rest, *first_b, *second_b], "v" * 6, 8, 1_000)
        a_y, a_x = call(second_kernel, [sds((2, *chunk_a), BF16)] * 2, [], [own_b, *red_a.rest, *first_a], "avvvv", 8, 1_000)
        second_a = swap(a_y, 1, 0), swap(a_x, 0, 2)
        near_b = swap(odd_b, 2, 0)
        own_b, far_b, own_a, far_a, odd_a = call(
            far_near_kernel,
            last[0] + before_z[1],
            [],
            [own_b, far_b, near_b, *red_a.rest, *first_a, *second_a],
            "v" * 9,
            8,
            1_000,
        )
        far_b = swap(far_b, 4, 0)
        r2, r3 = [swap(after(v, own_a), 0, m) for v, m in zip(leaving, (2, 3), strict=True)]
        own_a, far_a = call(far_kernel, last[1], [], [own_a, far_a, swap(odd_a, 2, 0)], "vvv", 4, 1_000)
        far_a = swap(far_a, 4, 0)
    else:
        r2, r3 = [swap(v, 0, m) for v, m in zip(leaving, (2, 3), strict=True)]
    r1 = [swap(res_1, 0, 1), swap(gi_1, 0, 1)]
    masters = (attn_proj, out_proj, up_proj, down_proj, pos_table, norm_params)
    firsts = (first_attn, first_out, first_up, first_down, first_pos, first_norm)
    seconds = (second_attn, second_out, second_up, second_down, second_pos, second_norm)
    updated = [None] * 6
    token = sds((8, LANES), F32)
    done = jnp.zeros(token.shape, F32)
    if fast:
        which = (2, 3, 1)
        state = [group[i] for group in (masters, firsts, seconds) for i in which]
        new = call(
            functools.partial(rows_update_kernel, which),
            [sds(v.shape, F32) for v in state] + [token],
            [],
            [own_b, far_b, *state],
            "v" * 11,
            8,
            2_000_000_000,
        )
        for i, index in enumerate(which):
            updated[index] = new[i:9:3]
        done = new[9]
    if fast:
        which = (0, 4, 5)
        state = [group[i] for group in (masters, firsts, seconds) for i in which]
        new = call(
            tiles_update_kernel,
            [sds(v.shape, F32) for v in state] + [token],
            [],
            [scal, done, own_a, far_a, *state],
            "sv" + "v" * 11,
            8,
            1_000_000,
        )
        for i, index in enumerate(which):
            updated[index] = new[i:9:3]
        done = new[9]
    outputs, grad_input = call(
        finish_kernel,
        [pltpu.HBM(inputs.shape, BF16), pltpu.HBM(inputs.shape, F32)],
        [((3, block, width), F32), [8]],
        [scal, done, res_k, gi_k, *r1, r2, r3],
        "sv" + "v" * 6,
        8,
        1_000,
    )
    if not fast:

        def reduced(value, own_axis):
            arrived = lax.all_to_all(value, "dp", split_axis=0, concat_axis=0, tiled=True)
            part = arrived.astype(F32).sum(axis=0).astype(BF16)
            arrived = lax.all_to_all(part, "tensor", split_axis=0, concat_axis=0, tiled=True)
            return arrived.astype(F32).sum(axis=0)

        gup, gdown, gout = got_b
        gattn, gpos = got_a
        gup, gdown, gout, gattn = [jnp.take(v, relative, axis=0) for v in (gup, gdown, gout.reshape(n_t, group, width), gattn)]
        g_up = reduced(gup.reshape(n_t, n_dp, per, inner).swapaxes(0, 1), 0)
        g_down = reduced(gdown.reshape(n_t, n_dp, inner // n_dp, width).swapaxes(0, 1), 0)
        g_out = reduced(gout.reshape(n_t, n_dp, out_per, width).swapaxes(0, 1), 0)
        g_pos = reduced(gpos.reshape(n_t, n_dp, pos_per, width).swapaxes(0, 1), 0)
        g_attn = reduced(gattn.reshape(n_t, n_dp, per, 3, group).swapaxes(0, 1), 0).swapaxes(0, 1)
        cut = gnorm[:4].reshape(4, n_dp, width // n_dp).swapaxes(0, 1).astype(BF16)
        g_norm = reduced(jnp.broadcast_to(cut[:, None], (n_dp, n_t, *cut.shape[1:])), 0)

        gradients = (g_attn, g_out, g_up, g_down, g_pos, g_norm)
        for index in range(6):
            updated[index] = adam_step(masters[index], gradients[index], firsts[index], seconds[index], RATES[index], DECAYS[index])
    return (outputs, grad_input, *[v for new in updated for v in new])


def solution(mesh):
    acts = P("dp", "tensor", None)
    attn = P(None, "dp", "tensor")
    both = P(("tensor", "dp"), None)
    up = P("dp", "tensor")
    norm = P(None, "dp")
    return jax.shard_map(
        body,
        mesh=mesh,
        in_specs=(acts, P("dp", None), acts, attn, both, up, both, both, norm, *(attn,) * 2, *(both,) * 2, *(up,) * 2, *(both,) * 4, *(norm,) * 2),
        out_specs=(acts, acts, *(attn,) * 3, *(both,) * 3, *(up,) * 3, *(both,) * 6, *(norm,) * 3),
        check_vma=False,
    )
```

```python
import functools

import jax
import jax.numpy as jnp
from jax import lax
from jax.experimental import pallas as pl
from jax.experimental.pallas import tpu as pltpu
from jax.sharding import PartitionSpec as P

HD = 64
STEP = 10
LANES = 128

NORM_EPS = 1e-05
NEG_FILL = -1e30
BETA_ONE = 0.9
BETA_TWO = 0.95
ADAM_EPS = 1e-08
RATES = (0.03, 0.2, 0.03, 0.02, 0.3, 0.3)
DECAYS = (0.1, 0.1, 0.1, 0.1, 0.1, 0.0)
GELU_A = 0.7978845608028654
GELU_B = 0.044715

F32 = jnp.float32
BF16 = jnp.bfloat16
AXES = ("dp", "tensor")

NN = (((1,), (0,)), ((), ()))
NT = (((1,), (1,)), ((), ()))
TN = (((0,), (0,)), ((), ()))
QUERIES = 256


def total(*parts):
    return sum(p.astype(F32) for p in parts)


def low(*parts):
    return total(*parts).astype(BF16)


def adam_step(weight, gradient, moment_one, second, step_rate, decay_rate):
    first_new = BETA_ONE * moment_one + (1.0 - BETA_ONE) * gradient
    second_new = BETA_TWO * second + (1.0 - BETA_TWO) * gradient * gradient
    fixed_first = first_new / (1.0 - BETA_ONE**STEP)
    fixed_second = second_new / (1.0 - BETA_TWO**STEP)
    weight_new = weight - step_rate * (fixed_first / (jnp.sqrt(fixed_second) + ADAM_EPS) + decay_rate * weight)
    return (weight_new, first_new, second_new)


def mm(a, b, dims=NN):
    return lax.dot_general(a, b, dims, preferred_element_type=F32)


def swap(value, rd, rt):
    n_t = lax.axis_size("tensor")
    mask = rd * n_t + rt
    return lax.ppermute(value, AXES, [(i, i ^ mask) for i in range(lax.axis_size("dp") * n_t)])


def rows_at(start, size, step):
    return pl.ds(pl.multiple_of(start, step), size)


def by_head(rows):
    lane = lax.broadcasted_iota(jnp.int32, (rows, LANES), 1)

    def keep(h):
        here = (lane >= h * HD) & (lane < (h + 1) * HD)
        return lambda v: jnp.where(here, v, jnp.zeros_like(v))

    return [keep(h) for h in range(LANES // HD)]


def fill_window(me_t, which, parts, out_ref):
    own, rx, c1, c3 = parts
    n = own.shape[1]
    for r, ref in enumerate((own, c1, rx, c3)):
        out_ref[rows_at((me_t ^ r) * n, n, n), :] = ref[which]


def copies_in(moves, sems):
    copies = [pltpu.make_async_copy(src, dst, sems.at[i]) for i, (src, dst) in enumerate(moves)]
    for copy in copies:
        copy.start()
    return copies


def prepare_kernel(scal, inputs, cot, attn, pos, norm, out, up, down, ga, gb, xs, c1, own, attn_s, pos_s, norm_s, out_s, up_s, down_s, sems):
    me_t = scal[1]
    moves = [(attn, attn_s), (pos, pos_s), (norm, norm_s), (up, up_s), (down, down_s), (out, out_s)]
    for rel, ref, at in ((2, xs, 0), (3, xs, 2), (1, c1, 0), (0, own, 0)):
        moves += [(inputs.at[me_t ^ rel], ref.at[at]), (cot.at[me_t ^ rel], ref.at[at + 1])]
    copies = copies_in(moves, sems)
    for copy in copies[:3]:
        copy.wait()
    per = attn.shape[1]
    pos_per = pos.shape[0]
    tiles = pos.shape[1] // LANES
    for t in range(3):
        ga[0, t * per : (t + 1) * per, :] = attn_s[t].astype(BF16)
    for k in range(tiles):
        at = 3 * per + k * pos_per
        ga[0, at : at + pos_per, :] = pos_s[:, k * LANES : (k + 1) * LANES].astype(BF16)
    at = 3 * per + tiles * pos_per
    both = norm_s[...]
    both = jnp.concatenate([both, both], axis=1)
    both = jnp.concatenate([both, jnp.zeros_like(both)], axis=0)
    high = both.astype(BF16)
    rest = (both - high.astype(F32)).astype(BF16)
    ga[0, at : at + 16, :] = jnp.concatenate([high, rest], axis=0)
    for copy in copies[3:6]:
        copy.wait()
    gb[0, 0:per, :] = up_s[...].astype(BF16)
    gb[0, per : 2 * per, :] = down_s[...].astype(BF16)
    gb[0, 2 * per :, :] = out_s[...].astype(BF16)
    for copy in copies[6:]:
        copy.wait()


def mask_kernel(scal, segs, bias):
    me_t = scal[1]
    win = bias.shape[0]
    seg = segs[pl.ds(me_t, 1), :].astype(F32)
    seg_col = jnp.transpose(jnp.broadcast_to(seg, (LANES, win)))
    for i in range(win // LANES):
        key_seg = seg_col[i * LANES : (i + 1) * LANES, 0:1]
        key_at = lax.broadcasted_iota(jnp.int32, (LANES, win), 0) + i * LANES
        query_at = lax.broadcasted_iota(jnp.int32, (LANES, win), 1)
        counts = (key_seg == seg) & (query_at >= key_at)
        bias[i * LANES : (i + 1) * LANES, :] = jnp.where(counts, 0.0, NEG_FILL)


def stack_mask_kernel(scal, segs, own, got, both, bias):
    stack_kernel(own, got, both)
    mask_kernel(scal, segs, bias)


def stack_kernel(own, got, both):
    n = own.shape[0]
    both[:n] = own[...]
    both[n:] = got[...]


def leaver(sems):
    leaving = []

    def leave(src, dst):
        leaving.append(pltpu.make_async_copy(src, dst, sems.at[len(leaving)]))
        leaving[-1].start()

    return leaving, leave


def attend(x, w, groups, bias, qkv_o, qkv_h, pt_o, pt_h, mix_o, leave):
    win = x.shape[0]
    heads = by_head(win)
    for g in groups:
        at = g * 3 * LANES
        qkv = mm(x[...], w[:, at : at + 3 * LANES]).astype(BF16)
        q = qkv[:, :LANES] * jnp.asarray(HD**-0.5, BF16)
        k = qkv[:, LANES : 2 * LANES]
        v = qkv[:, 2 * LANES :]
        qkv_o[:, at : at + LANES] = q
        qkv_o[:, at + LANES : at + 3 * LANES] = qkv[:, LANES:]
        leave(qkv_o.at[:, at : at + 3 * LANES], qkv_h.at[:, at : at + 3 * LANES])
        for j in range(win // QUERIES):
            ext = (j + 1) * QUERIES
            cols = slice(j * QUERIES, ext)
            mixed = jnp.zeros((QUERIES, LANES), F32)
            for h, only in enumerate(heads):
                s = mm(only(k)[:ext], q[cols], NT) + bias[:ext, cols]
                e = jnp.exp(s - jnp.max(s, axis=0, keepdims=True))
                p = (e * (1.0 / jnp.sum(e, axis=0, keepdims=True))).astype(BF16)
                pt_o[len(heads) * g + h, :ext, cols] = p
                mixed += mm(p, only(v)[:ext], TN)
            mix_o[cols, g * LANES : (g + 1) * LANES] = mixed.astype(BF16)
            for h in range(len(heads)):
                leave(pt_o.at[len(heads) * g + h, :ext, cols], pt_h.at[len(heads) * g + h, :ext, cols])


def attention_kernel(places, n_pieces, scal, *refs):
    own, rx, c1, c3, bias = refs[:5]
    pieces = refs[5 : 5 + n_pieces]
    hid_o, qkv_h, pt_h, mix_o, w_h, nrm_o, x_s, wlast_o, pos_s, nrm_s, w_o, qkv_o, pt_o, out_sems = refs[5 + n_pieces :]
    leaving, leave = leaver(out_sems)
    me_dp, me_t = scal[0], scal[1]
    win, width = x_s.shape
    groups = w_o.shape[1] // (3 * LANES)
    fill_window(me_t, 0, (own, rx, c1, c3), x_s)
    if places is None:
        w_o[...] = pieces[0][...]
        pos_s[...] = pieces[1][...]
        nrm_o[...] = pieces[2][...]
    else:
        n_dp = nrm_s.shape[0]
        per = width // n_dp
        pos_per = win // (n_dp * groups)
        for ref, (xr, yr, zs, c) in zip(pieces, places, strict=True):
            tr = xr * 2 + c
            for i, zr in enumerate(zs):
                src = me_dp ^ (zr * 2 + yr)
                for t in range(3):
                    at = (tr * 3 + t) * LANES
                    w_o[rows_at(src * per, per, per), at : at + LANES] = ref[i, t * per : (t + 1) * per]
                where = (me_t ^ tr) * (win // groups) + src * pos_per
                for k in range(width // LANES):
                    at = 3 * per + k * pos_per
                    pos_s[rows_at(where, pos_per, pos_per), k * LANES : (k + 1) * LANES] = ref[i, at : at + pos_per]
                if tr == 0:
                    at = 3 * per + width // LANES * pos_per
                    nrm_s[src] = ref[i, at : at + 16].astype(F32)
        low_lane = lax.broadcasted_iota(jnp.int32, (8, LANES), 1) < per
        for j in range(n_dp // 2):
            left = nrm_s[2 * j]
            right = nrm_s[2 * j + 1]
            both = jnp.where(low_lane, left[0:8] + left[8:16], right[0:8] + right[8:16])
            nrm_o[:, j * LANES : (j + 1) * LANES] = both

    leave(w_o, w_h)

    hidden = x_s[...].astype(F32) + pos_s[...].astype(F32)
    hid_o[...] = hidden
    x_s[...] = hidden.astype(BF16)
    first = qkv_o.shape[1] // (3 * LANES)
    attend(x_s, w_o, range(first), bias, qkv_o, qkv_h, pt_o, pt_h, mix_o, leave)
    wlast_o[...] = w_o[:, first * 3 * LANES :]
    for copy in leaving:
        copy.wait()


def attention_rest_kernel(x, w, bias, qkv_h, pt_h, mix_o, qkv_o, pt_o, out_sems):
    leaving, leave = leaver(out_sems)
    attend(x, w, range(w.shape[1] // (3 * LANES)), bias, qkv_o, qkv_h, pt_o, pt_h, mix_o, leave)
    for copy in leaving:
        copy.wait()


def norm_forward(v):
    center = v - jnp.mean(v, axis=-1, keepdims=True)
    rs = lax.rsqrt(jnp.mean(center * center, axis=-1, keepdims=True) + NORM_EPS)
    return center * rs, rs


def norm_backward(g, xhat, rs, gain):
    e = g * gain
    return rs * (e - jnp.mean(e, axis=-1, keepdims=True) - xhat * jnp.mean(e * xhat, axis=-1, keepdims=True))


def put_blocks(me_t, value, keep, s1, sx):
    n = keep.shape[0]
    for r, ref in ((0, keep), (1, s1.at[0]), (2, sx.at[0]), (3, sx.at[1])):
        ref[...] = value[rows_at((me_t ^ r) * n, n, n), :].astype(ref.dtype)


CHUNK = 128


def chunk_of(refs, tr, r):
    c, xr, yr, zr = tr & 1, tr >> 1, r & 1, r >> 1
    half = refs[0].shape[0] // 2
    if zr < half:
        kind, slot = (0, yr * half + zr) if xr == 1 else (2, yr * half + zr)
    else:
        kind, slot = (1, xr * half + zr - half) if yr == 1 else (2, 2 * half + xr * half + zr - half)
    return refs[3 * c + kind], slot


def ffn_kernel(places, n_pieces, scal, *refs):
    own, rx, c1, c3, hid, mixed_a, mixed_b, nrm = refs[:8]
    pieces = refs[8 : 8 + n_pieces]
    rest = refs[8 + n_pieces :]
    res_k, res_1, res_x, gone_o, gm_o, gnorm_o = rest[:6]
    if places is None:
        gup_o, gdown_o, gout_o = rest[6:9]
        rest = rest[9:]
    else:
        chunks_o = rest[6:12]
        rest = rest[12:]
    cot_s, out_s, up_s, down_s, a_s, b_s, g_s, xh1_s, r1_s, n1_s, sent_s, act_s, dg_s, low_s, xt_s, mixed = rest
    split = mixed_a.shape[1]
    mixed[:, :split] = mixed_a[...]
    mixed[:, split:] = mixed_b[...]
    me_dp, me_t = scal[0], scal[1]
    win, width = hid.shape
    groups = up_s.shape[0]
    fill_window(me_t, 1, (own, rx, c1, c3), cot_s)
    if places is None:
        n_dp = 1
        for src, dst in zip(pieces, (out_s, up_s, down_s), strict=True):
            dst[...] = src[...]
    else:
        n_dp = chunks_o[2].shape[0]
        per = width // n_dp
        out_per = LANES // n_dp
        for ref, (xr, yr, zs, c) in zip(pieces, places, strict=True):
            tr = xr * 2 + c
            for i, zr in enumerate(zs):
                src = me_dp ^ (zr * 2 + yr)
                up_s[tr, rows_at(src * per, per, per), :] = ref[i, 0:per]
                down_s[tr, rows_at(src * per, per, per), :] = ref[i, per : 2 * per]
                out_s[rows_at(tr * LANES + src * out_per, out_per, out_per), :] = ref[i, 2 * per : 2 * per + out_per]

    def chunks(fn):
        for i in range(win // CHUNK):
            fn(slice(i * CHUNK, (i + 1) * CHUNK))

    a_s[0] = mm(mixed[...], out_s[...])

    def norm_one(at):
        xhat, rs = norm_forward(hid[at, :] + a_s[0, at, :])
        xh1_s[at, :] = xhat
        r1_s[at, :] = jnp.broadcast_to(rs, (CHUNK, LANES))
        normed = xhat * nrm[0:1, :] + nrm[1:2, :]
        n1_s[at, :] = normed
        sent_s[at, :] = normed.astype(BF16)

    chunks(norm_one)

    for g in range(groups):
        a_s[g % 2] = mm(sent_s[...], up_s[g])

        def gelu(at, g=g):
            v = a_s[g % 2, at, :]
            square = v * v
            half = 0.5 + 0.5 * jnp.tanh(v * (GELU_A + GELU_A * GELU_B * square))
            act_s[g, at, :] = (v * half).astype(BF16)
            dg_s[g, at, :] = half + (half - half * half) * (v * (2.0 * GELU_A + 6.0 * GELU_A * GELU_B * square))

        chunks(gelu)
        n1_s[...] += mm(act_s[g], down_s[g])

    def norm_two(i, sums):
        at = slice(i * CHUNK, (i + 1) * CHUNK)
        xhat, rs = norm_forward(n1_s[at, :])
        n1_s[at, :] = xhat * nrm[2:3, :] + nrm[3:4, :]
        g = cot_s[at, :].astype(F32)
        grad = norm_backward(g, xhat, rs, nrm[2:3, :])
        b_s[at, :] = grad
        low_s[at, :] = grad.astype(BF16)
        return (sums[0] + jnp.sum((g * xhat).reshape(-1, 8, width), axis=0), sums[1] + jnp.sum(g.reshape(-1, 8, width), axis=0))

    def every(step):
        sums = (jnp.zeros((8, width), F32),) * 2
        for i in range(win // CHUNK):
            sums = step(i, sums)
        return sums

    gain_two, shift_two = every(norm_two)
    put_blocks(me_t, n1_s, res_k, res_1, res_x)

    def put(g, first, height, source, base):
        for r in range(n_dp):
            ref, slot = chunk_of(chunks_o, g, r)
            ref[slot, first : first + height, :] = source[rows_at(base + (r ^ me_dp) * height, height, height), :]

    xt_s[...] = jnp.transpose(sent_s[...])
    for g in range(groups):
        gdown = mm(jnp.transpose(act_s[g]), low_s[...])
        if places is None:
            gdown_o[g] = gdown.astype(BF16)
        else:
            g_s[0] = gdown.astype(BF16)
            put(g, per, per, g_s.at[0], 0)
        act_s[g] = (mm(low_s[...], down_s[g], NT) * dg_s[g]).astype(BF16)
        gup = mm(xt_s[...], act_s[g])
        if places is None:
            gup_o[g] = gup.astype(BF16)
        else:
            g_s[1] = gup.astype(BF16)
            put(g, 0, per, g_s.at[1], 0)
        b_s[...] += mm(act_s[g], up_s[g], NT)

    def norm_one_back(i, sums):
        at = slice(i * CHUNK, (i + 1) * CHUNK)
        g = b_s[at, :]
        xhat = xh1_s[at, :]
        grad = norm_backward(g, xhat, r1_s[at, 0:1], nrm[0:1, :])
        gone_o[at, :] = grad
        low_s[at, :] = grad.astype(BF16)
        return (sums[0] + jnp.sum((g * xhat).reshape(-1, 8, width), axis=0), sums[1] + jnp.sum(g.reshape(-1, 8, width), axis=0))

    gain_one, shift_one = every(norm_one_back)
    for k, total in enumerate((gain_one, shift_one, gain_two, shift_two)):
        gnorm_o[k : k + 1, :] = jnp.sum(total, axis=0, keepdims=True)
    gnorm_o[4:8, :] = jnp.zeros((4, width), F32)

    gout = mm(jnp.transpose(mixed[...]), low_s[...])
    if places is None:
        gout_o[...] = gout.astype(BF16)
    else:
        g_s[0] = gout.astype(BF16)
        for g in range(groups):
            put(g, 2 * per, out_per, g_s.at[0], g * LANES)
    gm = mm(low_s[...], out_s[...], NT).astype(BF16)
    for g in range(groups):
        gm_o[g] = gm[:, g * LANES : (g + 1) * LANES]


def attention_back_kernel(fast, scal, hid, qkv_a, qkv_b, pt_a, pt_b, gm, w_h, gone, gnorm, *rest):
    gi_k, gi_1, gi_x = rest[:3]
    if fast:
        chunks_o = rest[3:9]
        rest = rest[9:]
    else:
        gattn_o, gpos_o = rest[3:5]
        rest = rest[5:]
    ht_s, ds_s, dqkv_s, acc_s, g_s, qkv, pt, w, sems = rest
    me_dp, me_t = scal[0], scal[1]
    win, width = hid.shape
    groups = w.shape[1] // (3 * LANES)
    heads = by_head(win)
    arriving = []
    for g in range(groups):
        first = qkv_a.shape[1] // (3 * LANES)
        qkv_h, pt_h, base = (qkv_a, pt_a, 0) if g < first else (qkv_b, pt_b, first)
        lanes = slice(g * 3 * LANES, (g + 1) * 3 * LANES)
        there = slice((g - base) * 3 * LANES, (g - base + 1) * 3 * LANES)
        arriving.append(pltpu.make_async_copy(qkv_h.at[:, there], qkv.at[:, lanes], sems.at[len(arriving)]))
        for n in range(g * len(heads), (g + 1) * len(heads)):
            for j in range(win // QUERIES):
                ext = (j + 1) * QUERIES
                cols = slice(j * QUERIES, ext)
                arriving.append(pltpu.make_async_copy(pt_h.at[n - base * len(heads), :ext, cols], pt.at[n, :ext, cols], sems.at[len(arriving)]))
    arriving.append(pltpu.make_async_copy(w_h, w, sems.at[len(arriving)]))
    for copy in arriving:
        copy.start()
    ht_s[...] = jnp.transpose(hid[...].astype(BF16))
    for g in range(groups):
        at = g * 3 * LANES
        per_group = 1 + len(heads) * (win // QUERIES)
        for copy in arriving[g * per_group : (g + 1) * per_group]:
            copy.wait()
        q = qkv[:, at : at + LANES]
        k = qkv[:, at + LANES : at + 2 * LANES]
        v = qkv[:, at + 2 * LANES : at + 3 * LANES]
        d_mixed = gm[g]
        for j in range(win // QUERIES):
            ext = (j + 1) * QUERIES
            cols = slice(j * QUERIES, ext)
            dq = jnp.zeros((QUERIES, LANES), F32)
            for h, only in enumerate(heads):
                p = pt[len(heads) * g + h, :ext, cols].astype(F32)
                dp = mm(v[:ext], only(d_mixed)[cols], NT)
                ds = (p * (dp - jnp.sum(p * dp, axis=0, keepdims=True))).astype(BF16)
                ds_s[len(heads) * g + h, :ext, cols] = ds
                dq += mm(ds, only(k)[:ext], TN)
            dqkv_s[cols, at : at + LANES] = (dq * HD**-0.5).astype(BF16)
        for i in range(win // QUERIES):
            rows = slice(i * QUERIES, (i + 1) * QUERIES)
            dk = jnp.zeros((QUERIES, LANES), F32)
            dv = jnp.zeros((QUERIES, LANES), F32)
            for h, only in enumerate(heads):
                dk += mm(ds_s[len(heads) * g + h, rows, i * QUERIES :], only(q)[i * QUERIES :])
                dv += mm(pt[len(heads) * g + h, rows, i * QUERIES :], only(d_mixed)[i * QUERIES :])
            dqkv_s[rows, at + LANES : at + 2 * LANES] = dk.astype(BF16)
            dqkv_s[rows, at + 2 * LANES : at + 3 * LANES] = dv.astype(BF16)
    arriving[-1].wait()
    acc_s[...] = gone[...] + mm(dqkv_s[...], w[...], NT)

    put_blocks(me_t, acc_s, gi_k, gi_1, gi_x)
    if not fast:
        for g in range(groups):
            gattn_o[g] = mm(ht_s[...], dqkv_s[:, g * 3 * LANES : (g + 1) * 3 * LANES]).astype(BF16)
        gpos_o[...] = acc_s[...].astype(BF16)
        return
    n_dp = chunks_o[2].shape[0]
    per = width // n_dp
    pos_per = win // (n_dp * groups)
    for g in range(groups):
        g_s[g % 2] = mm(ht_s[...], dqkv_s[:, g * 3 * LANES : (g + 1) * 3 * LANES]).astype(BF16)
        for r in range(n_dp):
            d = r ^ me_dp
            ref, slot = chunk_of(chunks_o, g, r)
            for t in range(3):
                ref[slot, t * per : (t + 1) * per, :] = g_s[g % 2, rows_at(d * per, per, per), t * LANES : (t + 1) * LANES]
            where = (me_t ^ g) * (win // groups) + d * pos_per
            for k in range(width // LANES):
                at = 3 * per + k * pos_per
                ref[slot, at : at + pos_per, :] = acc_s[rows_at(where, pos_per, pos_per), k * LANES : (k + 1) * LANES].astype(BF16)
            at = 3 * per + width // LANES * pos_per
            tile = gnorm[0:8, rows_at((d >> 1) * LANES, LANES, LANES)]
            ref[slot, at : at + 16, :] = jnp.concatenate([tile, tile], axis=0).astype(BF16)


def near_kernel(rest, got, x, y, x2, y2, own, far, odd):
    own[...] = total(rest[0], got[0], x[0], x2[0])
    far[...] = total(rest[4], got[4], y[0], y2[0])
    odd[0] = low(rest[1], got[1], x[1], x2[1])
    odd[1] = low(rest[5], got[5], y[1], y2[1])


def second_kernel(done, rest, got, x, y, a, b):
    del done
    for i in range(2):
        a[i] = low(rest[2 + i], got[2 + i], x[2 + i])
        b[i] = low(rest[6 + i], got[6 + i], y[2 + i])


def far_kernel(own, far, near, own_o, far_o):
    own_o[...] = total(own[...], near[0])
    far_o[0] = low(far[...], near[1])


def far_near_kernel(own, far, near, rest, got, x, y, x2, y2, own_o, far_o, *others):
    far_kernel(own, far, near, own_o, far_o)
    near_kernel(rest, got, x, y, x2, y2, *others)


def update(refs, gradient, rate, decay):
    weight, one, two, new_weight, new_one, new_two = refs
    new_weight[...], new_one[...], new_two[...] = adam_step(weight[...], gradient, one[...], two[...], rate, decay)


def rows_update_kernel(which, own, far, *refs):
    n = len(which)
    *refs, token = refs
    token[...] = jnp.zeros_like(token)
    grad = total(own[...], far[0])
    at = 0
    for i, index in enumerate(which):
        height = refs[i].shape[0]
        update(refs[i :: n], grad[at : at + height], RATES[index], DECAYS[index])
        at += height


def tiles_update_kernel(scal, done, own, far, *refs):
    *refs, token = refs
    token[...] = done[...]
    attn, pos, norm = refs[0::3], refs[1::3], refs[2::3]
    grad = total(own[...], far[0])
    per = attn[0].shape[1]
    pos_per, width = pos[0].shape
    update(attn, grad[: 3 * per].reshape(attn[0].shape), RATES[0], DECAYS[0])
    at = 3 * per
    rows = [grad[at + k * pos_per : at + (k + 1) * pos_per] for k in range(width // LANES)]
    update(pos, jnp.concatenate(rows, axis=1), RATES[4], DECAYS[4])
    at += width // LANES * pos_per
    tile = grad[at : at + 8]
    half = jnp.where((scal[0] & 1) == 1, tile[:4, LANES // 2 :], tile[:4, : LANES // 2])
    update(norm, half, RATES[5], DECAYS[5])


def finish_kernel(scal, done, res_k, gi_k, res_1, gi_1, r2, r3, res_o, gi_o, gi_s, sems):
    del done
    me_t = scal[1]
    moves = [(gi_k, gi_o.at[me_t])]
    moves += [(res, res_o.at[me_t ^ r]) for r, res in enumerate((res_k, res_1.at[0], r2.at[0], r3.at[0]))]
    copies = copies_in(moves, sems)
    for r, gi in ((1, gi_1.at[0]), (2, r2.at[1]), (3, r3.at[1])):
        gi_s[r - 1] = gi[...].astype(F32)
        copies.append(pltpu.make_async_copy(gi_s.at[r - 1], gi_o.at[me_t ^ r], sems.at[4 + r]))
        copies[-1].start()
    for copy in copies:
        copy.wait()


def after(value, *others):
    return lax.optimization_barrier((value, *others))[0]


def stacked(q, got):
    out = jax.ShapeDtypeStruct((2 * q.shape[0], *q.shape[1:]), q.dtype)
    return call(stack_kernel, [out], [], [q, got], "vv", 6, 1_000)[0]


def gather_z(value, *others):
    nz = lax.axis_size("dp") // 2
    q, order = value, [0]
    step = nz // 2
    while step:
        if step == 1:
            q = after(q, *others)
        q = stacked(q, swap(q, step * 2, 0))
        order = order + [z ^ step for z in order]
        step //= 2
    return q, tuple(order)


def gather_xy(q, order, qx=None, qy=None, *others):
    half = len(order) // 2
    if qx is None:
        qx, qy = swap(q, 0, 2), swap(q, 1, 0)
    a, b = after(qx[:half], *others), after(qy[half:], *others)
    return [(q, (0, 0, order)), (qx, (1, 0, order)), (qy, (0, 1, order)), (swap(a, 1, 0), (1, 1, order[:half])), (swap(b, 0, 2), (1, 1, order[half:]))]


def both_cores(found):
    out = []
    for array, place in found:
        out.append((array, (*place, 0)))
        out.append((swap(array, 0, 1), (*place, 1)))
    return [f[0] for f in out], tuple(f[1] for f in out)


class Reduction:
    def __init__(self, keep_a, keep_b, keep_rest, send_a, send_b, send_rest):
        self.half = keep_a.shape[0] // 2
        self.n = keep_a.shape[0]
        self.sums = [(keep_rest,)]
        self.send_rest = send_rest
        got_a, got_b = swap(send_a, 0, 1), swap(send_b, 0, 1)
        self.a, self.b = low(keep_a, got_a), low(keep_b, got_b)

    def terms(self, a, start, stop):
        at = 0 if a else self.n
        found = [k[at + start : at + stop] for k in self.rest]
        for pair in self.got:
            g = pair[0 if a else 1]
            if g.shape[0] >= stop:
                found.append(g[start:stop])
        return found

    def first(self):
        self.rest = [self.sums[0][0], swap(self.send_rest, 0, 1)]
        self.got = [(swap(self.a, 0, 2), swap(self.b, 1, 0))]
        return self.got[0]

    def second(self, *others):
        h = self.half
        a, b = [after(low(*self.terms(part, h, 2 * h)), *others) for part in (True, False)]
        self.got.append((swap(a, 1, 0), swap(b, 0, 2)))
        return self.got[1]

    def over_z(self, *others):
        h = self.half
        arrived = []
        for z in range(1, 2 * h):
            chunk = low(*self.terms(z < h, z % h, z % h + 1))
            arrived.append(swap(after(chunk, *others), 2 * z, 0))
        return arrived

    def result(self, arrived):
        return total(*self.terms(True, 0, 1), *arrived)[0]


def call(kernel, outs, scratch, args, spaces, mib, flops):
    vmem = pl.BlockSpec(memory_space=pltpu.VMEM)
    args = [pltpu.with_memory_space_constraint(v, pltpu.HBM) if k == "h" else v for v, k in zip(args, spaces, strict=True)]
    kinds = {"s": pl.BlockSpec(memory_space=pltpu.SMEM), "v": vmem, "a": pl.BlockSpec(memory_space=pl.ANY), "h": pl.BlockSpec(memory_space=pltpu.HBM)}
    return pl.pallas_call(
        kernel,
        out_shape=outs,
        in_specs=[kinds[k] for k in spaces],
        out_specs=[vmem if isinstance(v, jax.ShapeDtypeStruct) else kinds["h"] for v in outs],
        scratch_shapes=[pltpu.VMEM(*s) if isinstance(s, tuple) else pltpu.SemaphoreType.DMA(tuple(s)) for s in scratch],
        compiler_params=pltpu.CompilerParams(vmem_limit_bytes=mib * 1024 * 1024),
        cost_estimate=pl.CostEstimate(flops=flops, bytes_accessed=0, transcendentals=0),
    )(*args)


def body(
    inputs,
    segment_ids,
    cotangent,
    attn_proj,
    out_proj,
    up_proj,
    down_proj,
    pos_table,
    norm_params,
    first_attn,
    second_attn,
    first_out,
    second_out,
    first_up,
    second_up,
    first_down,
    second_down,
    first_pos,
    second_pos,
    first_norm,
    second_norm,
):
    n_dp, n_t = lax.axis_size("dp"), lax.axis_size("tensor")
    me_dp, me_t = lax.axis_index("dp"), lax.axis_index("tensor")
    scal = jnp.stack([me_dp, me_t]).astype(jnp.int32)
    windows, block, width = inputs.shape
    win = block * n_t
    inner = up_proj.shape[1]
    group = attn_proj.shape[2]
    per, out_per, pos_per = attn_proj.shape[1], out_proj.shape[0], pos_table.shape[0]
    fast = out_per % 16 == 0 and pos_per % 16 == 0 and 2 * per == LANES and n_dp == 8 and n_t == 4
    sds = jax.ShapeDtypeStruct

    if fast:
        ga, gb, xs, c1, own = call(
            prepare_kernel,
            [
                sds((1, 3 * per + width // LANES * pos_per + 16, LANES), BF16),
                sds((1, 2 * per + out_per, width), BF16),
                sds((4, block, width), BF16),
                sds((2, block, width), BF16),
                sds((2, block, width), BF16),
            ],
            [(v.shape, F32) for v in (attn_proj, pos_table, norm_params, out_proj, up_proj, down_proj)] + [[14]],
            [scal, inputs, cotangent, attn_proj, pos_table, norm_params, out_proj, up_proj, down_proj],
            "s" + "h" * 8,
            8,
            1_000,
        )
        a2 = stacked(ga, swap(ga, 4, 0))
        qa, za = stacked(a2, swap(a2, 2, 0)), (0, 2, 1, 3)
        gb = after(gb, a2)
        rx = swap(xs, 0, 2)
        b2 = after(stacked(gb, swap(gb, 4, 0)), qa)
        qb, bias = call(
            stack_mask_kernel,
            [sds((2 * b2.shape[0], *b2.shape[1:]), BF16), sds((win, win), F32)],
            [],
            [scal, segment_ids, b2, swap(b2, 2, 0)],
            "svvv",
            10,
            1_000,
        )
        zb = za
        c1 = swap(c1, 0, 1)
        c3 = swap(rx[2:], 0, 1)
        qax, qay, qaxy = swap(qa, 0, 2), swap(qa, 1, 0), swap(qa, 1, 2)
        a_args, a_places = both_cores([(qa, (0, 0, za)), (qax, (1, 0, za)), (qay, (0, 1, za)), (qaxy, (1, 1, za))])
        qb = after(qb, rx, qax, qay)
        qbx, qby = swap(qb, 0, 2), swap(qb, 1, 0)
    else:

        bias = call(mask_kernel, [sds((win, win), F32)], [], [scal, segment_ids], "sv", 6, 1_000)[0]

        def pair(rel):
            return jnp.concatenate([lax.dynamic_slice_in_dim(v, me_t ^ rel, 1, 0) for v in (inputs, cotangent)])

        rx = swap(jnp.concatenate([pair(2), pair(3)]), 0, 2)
        own, c1 = pair(0), swap(pair(1), 0, 1)
        c3 = swap(rx[2:], 0, 1)
        relative = me_t ^ jnp.arange(n_t)
        whole = [lax.all_gather(lax.all_gather(v.astype(BF16), "dp"), "tensor") for v in (attn_proj, out_proj, up_proj, down_proj)]
        attn_w, out_w, up_w, down_w = [jnp.take(v, relative, axis=0) for v in whole]
        attn_w = attn_w.transpose(1, 3, 0, 2, 4).reshape(width, n_t * 3 * group)
        pos_w = lax.all_gather(lax.all_gather(pos_table.astype(BF16), "dp", axis=0, tiled=True), "tensor", axis=0, tiled=True)
        norm_w = lax.all_gather(norm_params, "dp", axis=1, tiled=True)
        norm_w = jnp.concatenate([norm_w, jnp.zeros_like(norm_w)])
        a_args, a_places = [attn_w, pos_w, norm_w], None
        b_args, b_places = [out_w.reshape(n_t * group, width), up_w.reshape(n_t, width, inner), down_w.reshape(n_t, inner, width)], None

    first = n_t // 2
    heads_of = group // HD

    def kept(groups):
        return [pltpu.HBM((win, groups * 3 * group), BF16), pltpu.HBM((groups * heads_of, win, win), BF16), sds((win, groups * group), BF16)]

    def work(groups):
        return [((win, groups * 3 * group), BF16), ((groups * heads_of, win, win), BF16), [groups * (1 + 2 * heads_of) + 1]]

    hid, qkv_a, pt_a, mixed_a, attn_all, norm_all, x_all, w_last = call(
        functools.partial(attention_kernel, a_places, len(a_args)),
        [
            sds((win, width), F32),
            *kept(first),
            pltpu.HBM((width, n_t * 3 * group), BF16),
            sds((8, width), F32),
            sds((win, width), BF16),
            sds((width, (n_t - first) * 3 * group), BF16),
        ],
        [((win, width), BF16), ((n_dp, 16, LANES), F32), ((width, n_t * 3 * group), BF16), *work(first)],
        [scal, own, rx, c1, c3, bias, *a_args],
        "svvvvv" + "v" * len(a_args),
        14,
        1_000_000,
    )
    if fast:
        found = gather_xy(qb, zb, qbx, qby, x_all)
    qkv_b, pt_b, mixed_b = call(attention_rest_kernel, kept(n_t - first), work(n_t - first), [x_all, w_last, bias], "vvv", 6, 1_000_000)
    if fast:
        found[3:] = [(after(v, mixed_b), at) for v, at in found[3:]]
        b_args, b_places = both_cores(found)

    blocks = [sds((block, width), BF16), sds((1, block, width), BF16), sds((2, block, width), BF16)]
    if fast:
        rows_b = 2 * per + out_per
        grads_b = [sds((n, rows_b, width), BF16) for n in (n_dp // 2, n_dp // 2, n_dp)] * 2
    else:
        grads_b = [sds((n_t, width, inner), BF16), sds((n_t, inner, width), BF16), sds((n_t * group, width), BF16)]
    res_k, res_1, res_x, gone, gm, gnorm, *got_b = call(
        functools.partial(ffn_kernel, b_places, len(b_args)),
        [*blocks, sds((win, width), F32), sds((n_t, win, group), BF16), sds((8, width), F32), *grads_b],
        [
            ((win, width), BF16),
            ((n_t * group, width), BF16),
            ((n_t, width, inner), BF16),
            ((n_t, inner, width), BF16),
            ((2, win, width), F32),
            ((win, width), F32),
            ((2, win, width), BF16),
            ((win, width), F32),
            ((win, LANES), F32),
            ((win, width), F32),
            ((win, width), BF16),
            ((n_t, win, inner), BF16),
            ((n_t, win, inner), F32),
            ((win, width), BF16),
            ((width, win), BF16),
            ((win, n_t * group), BF16),
        ],
        [scal, own, rx, c1, c3, hid, mixed_a, mixed_b, norm_all, *b_args],
        "svvvvvvvv" + "v" * len(b_args),
        26,
        1_000_000,
    )
    if fast:
        red_b = Reduction(*got_b)
        gone = after(gone, red_b.a, red_b.b)
        first_b = red_b.first()

    blocks = [sds((block, width), F32), *blocks[1:]]
    if fast:
        rows_a = 3 * per + width // LANES * pos_per + 16
        grads_a = [sds((n, rows_a, LANES), BF16) for n in (n_dp // 2, n_dp // 2, n_dp)] * 2
    else:
        grads_a = [sds((n_t, width, 3 * group), BF16), sds((win, width), BF16)]
    gi_k, gi_1, gi_x, *got_a = call(
        functools.partial(attention_back_kernel, fast),
        [*blocks, *grads_a],
        [
            ((width, win), BF16),
            ((n_t * group // HD, win, win), BF16),
            ((win, n_t * 3 * group), BF16),
            ((win, width), F32),
            ((2, width, 3 * group), BF16),
            ((win, n_t * 3 * group), BF16),
            ((n_t * group // HD, win, win), BF16),
            ((width, n_t * 3 * group), BF16),
            [1 + n_t + 2 * n_t * group // HD],
        ],
        [scal, hid, qkv_a, qkv_b, pt_a, pt_b, gm, attn_all, gone, gnorm],
        "svhhhhvhvv",
        18,
        1_000_000,
    )
    leaving = [jnp.concatenate([res_x[i : i + 1], gi_x[i : i + 1]]) for i in range(2)]
    if fast:
        red_a = Reduction(*got_a)
        first_a, second_b = red_a.first(), red_b.second()
        chunk_b, chunk_a = got_b[0].shape[1:], got_a[0].shape[1:]
        before_z = [[sds(chunk, F32), sds(chunk, F32), sds((2, *chunk), BF16)] for chunk in (chunk_b, chunk_a)]
        last = [[sds(chunk, F32), sds((1, *chunk), BF16)] for chunk in (chunk_b, chunk_a)]
        own_b, far_b, odd_b = call(near_kernel, before_z[0], [], [*red_b.rest, *first_b, *second_b], "v" * 6, 8, 1_000)
        a_y, a_x = call(second_kernel, [sds((2, *chunk_a), BF16)] * 2, [], [own_b, *red_a.rest, *first_a], "avvvv", 8, 1_000)
        second_a = swap(a_y, 1, 0), swap(a_x, 0, 2)
        near_b = swap(odd_b, 2, 0)
        own_b, far_b, own_a, far_a, odd_a = call(
            far_near_kernel,
            last[0] + before_z[1],
            [],
            [own_b, far_b, near_b, *red_a.rest, *first_a, *second_a],
            "v" * 9,
            8,
            1_000,
        )
        far_b = swap(far_b, 4, 0)
        r2, r3 = [swap(after(v, own_a), 0, m) for v, m in zip(leaving, (2, 3), strict=True)]
        own_a, far_a = call(far_kernel, last[1], [], [own_a, far_a, swap(odd_a, 2, 0)], "vvv", 4, 1_000)
        far_a = swap(far_a, 4, 0)
    else:
        r2, r3 = [swap(v, 0, m) for v, m in zip(leaving, (2, 3), strict=True)]
    r1 = [swap(res_1, 0, 1), swap(gi_1, 0, 1)]
    masters = (attn_proj, out_proj, up_proj, down_proj, pos_table, norm_params)
    firsts = (first_attn, first_out, first_up, first_down, first_pos, first_norm)
    seconds = (second_attn, second_out, second_up, second_down, second_pos, second_norm)
    updated = [None] * 6
    token = sds((8, LANES), F32)
    done = jnp.zeros(token.shape, F32)
    if fast:
        which = (2, 3, 1)
        state = [group[i] for group in (masters, firsts, seconds) for i in which]
        new = call(
            functools.partial(rows_update_kernel, which),
            [sds(v.shape, F32) for v in state] + [token],
            [],
            [own_b, far_b, *state],
            "v" * 11,
            8,
            2_000_000_000,
        )
        for i, index in enumerate(which):
            updated[index] = new[i:9:3]
        done = new[9]
    if fast:
        which = (0, 4, 5)
        state = [group[i] for group in (masters, firsts, seconds) for i in which]
        new = call(
            tiles_update_kernel,
            [sds(v.shape, F32) for v in state] + [token],
            [],
            [scal, done, own_a, far_a, *state],
            "sv" + "v" * 11,
            8,
            1_000_000,
        )
        for i, index in enumerate(which):
            updated[index] = new[i:9:3]
        done = new[9]
    outputs, grad_input = call(
        finish_kernel,
        [pltpu.HBM(inputs.shape, BF16), pltpu.HBM(inputs.shape, F32)],
        [((3, block, width), F32), [8]],
        [scal, done, res_k, gi_k, *r1, r2, r3],
        "sv" + "v" * 6,
        8,
        1_000,
    )
    if not fast:

        def reduced(value, own_axis):
            arrived = lax.all_to_all(value, "dp", split_axis=0, concat_axis=0, tiled=True)
            part = arrived.astype(F32).sum(axis=0).astype(BF16)
            arrived = lax.all_to_all(part, "tensor", split_axis=0, concat_axis=0, tiled=True)
            return arrived.astype(F32).sum(axis=0)

        gup, gdown, gout = got_b
        gattn, gpos = got_a
        gup, gdown, gout, gattn = [jnp.take(v, relative, axis=0) for v in (gup, gdown, gout.reshape(n_t, group, width), gattn)]
        g_up = reduced(gup.reshape(n_t, n_dp, per, inner).swapaxes(0, 1), 0)
        g_down = reduced(gdown.reshape(n_t, n_dp, inner // n_dp, width).swapaxes(0, 1), 0)
        g_out = reduced(gout.reshape(n_t, n_dp, out_per, width).swapaxes(0, 1), 0)
        g_pos = reduced(gpos.reshape(n_t, n_dp, pos_per, width).swapaxes(0, 1), 0)
        g_attn = reduced(gattn.reshape(n_t, n_dp, per, 3, group).swapaxes(0, 1), 0).swapaxes(0, 1)
        cut = gnorm[:4].reshape(4, n_dp, width // n_dp).swapaxes(0, 1).astype(BF16)
        g_norm = reduced(jnp.broadcast_to(cut[:, None], (n_dp, n_t, *cut.shape[1:])), 0)

        gradients = (g_attn, g_out, g_up, g_down, g_pos, g_norm)
        for index in range(6):
            updated[index] = adam_step(masters[index], gradients[index], firsts[index], seconds[index], RATES[index], DECAYS[index])
    return (outputs, grad_input, *[v for new in updated for v in new])


def solution(mesh):
    acts = P("dp", "tensor", None)
    attn = P(None, "dp", "tensor")
    both = P(("tensor", "dp"), None)
    up = P("dp", "tensor")
    norm = P(None, "dp")
    return jax.shard_map(
        body,
        mesh=mesh,
        in_specs=(acts, P("dp", None), acts, attn, both, up, both, both, norm, *(attn,) * 2, *(both,) * 2, *(up,) * 2, *(both,) * 4, *(norm,) * 2),
        out_specs=(acts, acts, *(attn,) * 3, *(both,) * 3, *(up,) * 3, *(both,) * 6, *(norm,) * 3),
        check_vma=False,
    )
```
